32 devices in a mesh: groups: 2 (over y), ep: 4 (over z), kv: 2 (over x), tp: 2 (over core).
Axes of the slice: x: 2, y: 2, z: 4, core: 2. Of those that a mesh axis runs over, the one named last changes fastest.
Arguments:
- queries: bfloat16 [512, 4096], P(('groups', 'ep'), ('kv', 'tp')), parts along dimension 0, may hold values from -16 to 16
- new_kv: bfloat16 [512, 4, 256], P(('groups', 'ep'), 'kv'), parts along dimension 0, may hold values from -16 to 16
- cache_pool: bfloat16 [512, 16, 4, 256], P(('groups', 'ep'), None, 'kv'), parts along dimension 0, may hold values from -5 to 5
- hit_pages: int32 [128], P('groups'), parts along dimension 0, may hold values from 0 to 255, as said below
- span_lengths: int32 [8], P('groups'), parts along dimension 0, may hold values from 1 to 64, as said below
- out_weight: bfloat16 [4096, 4096], P(('kv', 'tp')), may hold values from -0.09375 to 0.09375
- hidden_in: bfloat16 [512, 4096], P(('groups', 'ep')), parts along dimension 0, may hold values from -1.2 to 1.2
- norm_gain: float32 [4096], replicated, may hold values from 0.1 to 1.9
- expert_ids: int32 [512, 4], P(('groups', 'ep')), parts along dimension 0, may hold values from 0 to 3, all different within a row; in each aligned block of 64 rows (0 to 63, 64 to 127, ...) at most 64 rows name the same one
- gate_weights: float32 [512, 4], P(('groups', 'ep')), parts along dimension 0, may hold values from 0.02 to 0.4
- gate_up: bfloat16 [4, 2, 1536, 4096], P('ep', None, ('kv', 'tp')), may hold values from -0.09375 to 0.09375
- down_weight: bfloat16 [4, 1536, 4096], P('ep', ('kv', 'tp')), may hold values from -0.15625 to 0.15625
- new_owner: int32 [32], P('groups'), parts along dimension 0, may hold values from 0 to 3, as said below
Outputs:
- layer_out: bfloat16 [512, 4096], P(('groups', 'ep', 'kv', 'tp')), parts along dimension 0
- decode_pages: bfloat16 [64, 16, 4, 256], P(('groups', 'ep'), None, 'kv'), parts along dimension 0
The draws below stay inside these ranges and needn't reach their ends.
There are 2 independent parts, one for each index of `groups`. The reference program is written for one: setup_inputs(seed, part) draws one part's arguments, and reference() takes and returns one part's arrays. A program takes and returns all parts, laid end to end along the dimension named above; an argument that names none is the same for every part. Nothing has to cross between parts.
Inputs may be any that keep to these rules, and one draw needn't show every extreme that they name: `hit_pages`: distinct pool pages; rows p * 64 to (p+1) * 64 - 1 of the pool stand on index p of ep; at most 16 of the pages fall on one index, and some index holds exactly 16. `span_lengths`: the lengths sum to 192; some span holds exactly 64 tokens. `new_owner`: at most 8 pages go to one owner, and some owner receives exactly 8. `expert_ids`: each row names 4 different experts; in the rows of one index of ep no expert is named more than 64 times.
All inputs are finite; a program needn't handle non-finite values.
Results may differ from the reference program's by a relative error of at most 0.03.
Values may be sent and summed in bfloat16 or wider, within the bound.
No kernel may reach another device: no remote copies, remote signals or barrier semaphores. Data moves between devices by JAX's collectives and lax.ppermute only.
A program may use at most 128 MiB of HBM per device.

```python
import math
import jax
import jax.numpy as jnp
import numpy as np
from jax import lax

D = 4096
HD = 128
HQ = 32
KVH = 4
FF = 1536
TOK_DEV = 64
PAGE = 16
POOL = 64
HIT = 64
HOLD_MOST = 16
FFB = 384
EXPERTS = 4
TOP = 4
CAP = 64
SLOTS = 256
SUFFIX = 192
OWN_MOST = 8
N_EP = 4


def column_factor(first_square):
    column_ids = jnp.arange(D)
    squares = jnp.where(column_ids < D // 2, first_square, 2.0 - first_square)
    return jnp.sqrt(squares.astype(jnp.float32))


def draw_queries(key, part):
    key = jax.random.fold_in(key, 11)
    drawn = 2.0 * jnp.clip(jax.random.normal(key, (SLOTS, HQ, HD), jnp.float32), -4.0, 4.0)
    return drawn.reshape(SLOTS, HQ * HD).astype(jnp.bfloat16)


def draw_new_kv(key, part):
    key = jax.random.fold_in(key, 13)
    drawn = jnp.clip(jax.random.normal(key, (SLOTS, KVH, 2 * HD), jnp.float32), -4.0, 4.0)
    return drawn.astype(jnp.bfloat16)


def draw_hidden_in(key, part):
    key = jax.random.fold_in(key, 41)
    spread = jnp.clip(jax.random.normal(key, (SLOTS, D), jnp.float32), -4.0, 4.0)
    values = 0.2 * spread * column_factor(1.8)[None, :]
    return values.astype(jnp.bfloat16)


def draw_out_weight(key, part):
    key = jax.random.fold_in(key, 43)
    fan_scale = 1.0 / math.sqrt(HQ * HD)
    spread = jnp.clip(jax.random.normal(key, (HQ * HD, D), jnp.float32), -4.0, 4.0)
    values = fan_scale * spread * column_factor(1.8)[None, :]
    return values.astype(jnp.bfloat16)


def draw_hit_pages(key, part):
    key = jax.random.fold_in(key, 23)
    split_keys = jax.random.split(key, 3)
    first_holder = jax.random.randint(split_keys[0], (), 0, N_EP)
    slot_total = N_EP * HOLD_MOST
    slot_ids = jnp.arange(slot_total, dtype=jnp.int32)
    ranking = jax.random.permutation(split_keys[1], slot_total).astype(jnp.int32)
    ranking = ranking + jnp.where(slot_ids // HOLD_MOST == first_holder, slot_total, 0)
    picked = jnp.argsort(-ranking, stable=True)[:HIT].astype(jnp.int32)
    holder = picked // HOLD_MOST
    within = picked % HOLD_MOST
    orders = jax.vmap(lambda sub: jax.random.permutation(sub, POOL))(jax.random.split(split_keys[2], N_EP))
    page_here = orders[holder, within]
    return (holder * POOL + page_here).astype(jnp.int32)


def draw_span_lengths(key, part):
    key = jax.random.fold_in(key, 29)
    split_keys = jax.random.split(key, 3)
    others = N_EP - 1
    remaining = SUFFIX - TOK_DEV
    base_len = remaining // others
    extra = remaining % others
    other_ids = jnp.arange(others, dtype=jnp.int32)
    lengths = base_len + (other_ids < extra).astype(jnp.int32)
    spread_most = max(0, min(TOK_DEV - base_len - 1, base_len - 1))
    offsets = jax.random.randint(split_keys[0], (others,), 0, spread_most + 1)
    signs = jnp.where(other_ids % 2 == 0, 1, -1)
    paired = offsets[other_ids // 2] * signs
    paired = jnp.where(other_ids // 2 * 2 + 1 < others, paired, 0)
    lengths = lengths + paired
    lengths = lengths[jax.random.permutation(split_keys[1], others)]
    longest_at = jax.random.randint(split_keys[2], (), 0, N_EP)
    spot_ids = jnp.arange(N_EP, dtype=jnp.int32)
    take_from = jnp.clip(spot_ids - (spot_ids > longest_at).astype(jnp.int32), 0, others - 1)
    full = jnp.where(spot_ids == longest_at, TOK_DEV, lengths[take_from])
    return full.astype(jnp.int32)


def draw_new_owner(key, part):
    key = jax.random.fold_in(key, 37)
    split_keys = jax.random.split(key, 3)
    per_span = TOK_DEV // PAGE
    owner_order = jax.random.permutation(split_keys[0], N_EP)
    spot_ids = jnp.arange(N_EP, dtype=jnp.int32)
    flips = jax.random.randint(split_keys[1], (N_EP,), 0, 2)
    signs = jnp.where(spot_ids % 2 == 0, 1, -1)
    shifts = flips[spot_ids // 2] * signs
    shifts = jnp.where(spot_ids // 2 * 2 + 1 < N_EP, shifts, 0)
    shifts = jnp.where(spot_ids == 0, per_span, jnp.where(spot_ids == 1, -per_span, shifts))
    counts = jnp.zeros((N_EP,), jnp.int32).at[owner_order].set((per_span + shifts).astype(jnp.int32))
    bounds = jnp.cumsum(counts)
    total_pages = N_EP * per_span
    labels = jnp.sum((bounds[None, :] <= jnp.arange(total_pages)[:, None]).astype(jnp.int32), axis=1)
    mixed = jax.random.permutation(split_keys[2], total_pages)
    return labels[mixed].astype(jnp.int32)


def block_scale(stream_key, shape, shards, least, largest):
    def one(dim, shards_of):
        steps = jax.random.uniform(jax.random.fold_in(jax.random.fold_in(stream_key, 6), dim), (shards_of,), jnp.float32, least / len(shards), largest / len(shards))
        return jnp.repeat(jnp.exp(steps), shape[dim] // shards_of).reshape((-1,) + (1,) * (len(shape) - dim - 1))

    loudness = one(*shards[0])
    for cut in shards[1:]:
        loudness = loudness * one(*cut)
    return loudness


def shared_out(stream_key, own, number, rows, count, top, bound, lean):
    order = jax.random.permutation(stream_key, count)
    packed, common = shares(count, rows * top, bound, lean, True), shares(count, rows * top, bound, lean, False)
    places = jnp.arange(count)

    def named(sizes, rotation):
        used = int((sizes > 0).sum())
        fixed = max(1, used // 4)
        passed = fixed + (places - fixed + rotation * (used - fixed)) % max(1, count - fixed)
        return jnp.zeros((count,), jnp.int32).at[order[jnp.where(places < fixed, places, passed)]].set(jnp.asarray(sizes, jnp.int32))

    sizes = jnp.where(number % 4 == 0, named(packed, number // 4), named(common, number - number // 4 - 1))
    mixed = jax.random.permutation(jax.random.fold_in(own, 3), count)
    giver, sink = mixed[0:count // 2 * 2:2], mixed[1:count // 2 * 2:2]
    slack = jnp.minimum(sizes[giver] - 1, bound - sizes[sink]) // 2
    slack = jnp.where((giver == order[0]) | (sink == order[0]) | (sizes[sink] == 0), 0, jnp.maximum(slack, 0))
    passed = jax.random.randint(jax.random.fold_in(own, 4), (count // 2,), 0, 1 << 20) % (slack + 1)
    sizes = sizes.at[giver].add(-passed).at[sink].add(passed)
    members = jnp.searchsorted(jnp.cumsum(sizes), jnp.arange(rows * top), side="right").astype(jnp.int32)
    grid = members.reshape(top, rows).T
    grid = grid[jax.random.permutation(jax.random.fold_in(own, 1), rows)]
    rotation = jax.random.randint(jax.random.fold_in(own, 2), (rows, 1), 0, top)
    return jnp.take_along_axis(grid, (jnp.arange(top)[None, :] + rotation) % top, axis=1)


def shares(amount, total, reach, lean, full):
    loads = [(1 << 20) // math.isqrt(grade ** lean) + 1 for grade in range(1, amount + 1)]
    largest = reach if full else min(reach, max(-(-total // amount), total * loads[0] // sum(loads)))
    least = 1 if total - largest >= amount - 1 else 0
    given, spare = [largest] + [least] * (amount - 1), total - largest - least * (amount - 1)
    while spare > 0:
        movable = [i for i in range(1, amount) if given[i] < largest] or [i for i in range(1, amount) if given[i] < reach]
        whole, left = sum([loads[i] for i in movable]), spare
        for i in movable:
            more = min(reach - given[i], max(1, left * loads[i] // whole), spare)
            given[i] = given[i] + more
            spare = spare - more
    return np.array(given)


def bell_draw(stream_key, dims, deviation, reach, cuts=(), held_as=jnp.bfloat16):
    entries = jax.random.normal(stream_key, dims, jnp.float32) * deviation
    if len(cuts) > 0:
        entries = block_scale(stream_key, dims, cuts, -0.22, 0.18) * entries
    return jnp.clip(entries, min=-reach, max=reach).astype(held_as)


def setup_inputs(seed: int = 0, part: int = 0) -> dict:
    key_of = jax.random.split(jax.random.key(seed), 14)
    part_splits = jax.random.split(jax.random.fold_in(key_of[13], part), 14)
    queries = draw_queries(jax.random.fold_in(jax.random.fold_in(key_of[13], part), 71), part)
    new_kv = draw_new_kv(jax.random.fold_in(jax.random.fold_in(key_of[13], part), 71), part)
    cache_pool = bell_draw(part_splits[2], (N_EP * POOL, PAGE, KVH, 2 * HD), 1.0, 5.0, ((0, 4), (2, 2)))
    hit_pages = draw_hit_pages(jax.random.fold_in(jax.random.fold_in(key_of[13], part), 71), part)
    span_lengths = draw_span_lengths(jax.random.fold_in(jax.random.fold_in(key_of[13], part), 71), part)
    out_weight = draw_out_weight(jax.random.fold_in(key_of[13], 71), part)
    hidden_in = draw_hidden_in(jax.random.fold_in(jax.random.fold_in(key_of[13], part), 71), part)
    norm_gain = jnp.clip(1.0 + 0.18 * jax.random.normal(key_of[7], (D,), jnp.float32), 0.1, 1.9)
    expert_ids_keys = jax.random.split(jax.random.fold_in(part_splits[8], 1), SLOTS // TOK_DEV)
    expert_ids_turns = jax.random.permutation(jax.random.fold_in(part_splits[8], 3), SLOTS // TOK_DEV)
    expert_ids = jax.vmap(lambda own, number: shared_out(jax.random.fold_in(part_splits[8], 2), own, number, TOK_DEV, EXPERTS, TOP, CAP, 2))(expert_ids_keys, expert_ids_turns).reshape((SLOTS, TOP))
    gate_weights = jnp.clip(jnp.exp(math.log(0.4) - 2.9957323 * jax.random.uniform(part_splits[9], (SLOTS, TOP), jnp.float32) ** block_scale(part_splits[9], (SLOTS, TOP), ((0, 4),), -0.2, 0.2)), 0.02, 0.4)
    gate_up = bell_draw(key_of[10], (EXPERTS, 2, FF, D), D ** -0.5, 0.09375, ((0, 4), (2, 4)))
    down_weight = bell_draw(key_of[11], (EXPERTS, FF, D), FF ** -0.5, 0.15625, ((0, 4), (1, 4)))
    new_owner = draw_new_owner(jax.random.fold_in(jax.random.fold_in(key_of[13], part), 71), part)
    return dict(queries=queries, new_kv=new_kv, cache_pool=cache_pool, hit_pages=hit_pages, span_lengths=span_lengths, out_weight=out_weight, hidden_in=hidden_in, norm_gain=norm_gain, expert_ids=expert_ids, gate_weights=gate_weights, gate_up=gate_up, down_weight=down_weight, new_owner=new_owner)


MASKED = -1e+30
EPSILON = 1e-06

def slot_table(span_lengths):
    starts = jnp.cumsum(span_lengths) - span_lengths
    slot_here = jnp.arange(TOK_DEV, dtype=jnp.int32)
    positions = (starts[:, None] + slot_here[None, :]).reshape(-1).astype(jnp.int32)
    filled = (slot_here[None, :] < span_lengths[:, None]).reshape(-1)
    return (positions, filled)

def attend(queries, new_kv, cache_pool, hit_pages, positions, filled):
    group_size = HQ // KVH
    prefix = jnp.take(cache_pool, hit_pages, axis=0).reshape(HIT * PAGE, KVH, 2 * HD)
    all_keys = jnp.concatenate([prefix, new_kv], axis=0)
    heads_keys = jnp.transpose(all_keys, (1, 0, 2))
    heads_query = jnp.transpose(queries.reshape(SLOTS, KVH, group_size, HD), (1, 0, 2, 3))
    causal = filled[None, :] & (positions[None, :] <= positions[:, None])
    allowed = jnp.concatenate([jnp.ones((SLOTS, HIT * PAGE), dtype=bool), causal], axis=1)
    score_scale = 1.0 / math.sqrt(HD)

    def one_head(head_pair):
        query_head, keyval = head_pair
        scores = jnp.einsum('sgd,kd->gsk', query_head.astype(jnp.float32), keyval[:, :HD].astype(jnp.float32)) * score_scale
        scores = jnp.where(allowed[None], scores, MASKED)
        attention_weights = jax.nn.softmax(scores, axis=-1).astype(jnp.bfloat16)
        head_out = jnp.einsum('gsk,kd->sgd', attention_weights.astype(jnp.float32), keyval[:, HD:].astype(jnp.float32))
        return head_out.astype(jnp.bfloat16)
    head_outs = lax.map(one_head, (heads_query, heads_keys))
    return jnp.transpose(head_outs, (1, 0, 2, 3)).reshape(SLOTS, HQ * HD)

def mixture_of(normed, expert_ids, gate_weights, gate_up, down_weight):
    row_limit = N_EP * CAP
    block_count = FF // FFB

    def one_expert(running_sum, item):
        expert_index, gate_pair, down_block = item
        named_mask = expert_ids == expert_index
        named_rows = jnp.any(named_mask, axis=1)
        share_weight = lax.optimization_barrier(jnp.sum(jnp.where(named_mask, gate_weights, 0.0), axis=1))
        row_order = jnp.argsort(jnp.logical_not(named_rows).astype(jnp.int32), stable=True)[:row_limit].astype(jnp.int32)
        picked_rows = jnp.take(normed, row_order, axis=0)
        gate_part = jnp.dot(picked_rows, gate_pair[0].T, preferred_element_type=jnp.float32)
        up_part = jnp.dot(picked_rows, gate_pair[1].T, preferred_element_type=jnp.float32)
        hidden = (jax.nn.silu(gate_part) * up_part).astype(jnp.bfloat16)
        block_parts = jnp.einsum('rbf,bfd->rbd', hidden.reshape(row_limit, block_count, FFB).astype(jnp.float32), down_block.reshape(block_count, FFB, D).astype(jnp.float32))
        rounded = lax.optimization_barrier(block_parts.astype(jnp.bfloat16))
        merged = lax.optimization_barrier(jnp.sum(rounded.astype(jnp.float32), axis=1))
        factor = jnp.take(share_weight, row_order) * jnp.take(named_rows, row_order).astype(share_weight.dtype)
        return (running_sum.at[row_order].add(factor[:, None] * merged), None)
    start_sum = jnp.zeros((SLOTS, D), jnp.float32)
    running_sum, _ = lax.scan(one_expert, start_sum, (jnp.arange(EXPERTS, dtype=jnp.int32), gate_up, down_weight))
    return running_sum

def reference(queries, new_kv, cache_pool, hit_pages, span_lengths, out_weight, hidden_in, norm_gain, expert_ids, gate_weights, gate_up, down_weight, new_owner):
    positions, filled = slot_table(span_lengths)
    attended = attend(queries, new_kv, cache_pool, hit_pages, positions, filled)
    residual = (hidden_in.astype(jnp.float32) + jnp.dot(attended, out_weight, preferred_element_type=jnp.float32)).astype(jnp.bfloat16)
    resid_wide = residual.astype(jnp.float32)
    normed = (resid_wide * lax.rsqrt(lax.optimization_barrier(jnp.mean(resid_wide * resid_wide, axis=1, keepdims=True)) + EPSILON) * norm_gain).astype(jnp.bfloat16)
    mixture = mixture_of(normed, expert_ids, gate_weights, gate_up, down_weight)
    layer_out = jnp.where(filled[:, None], resid_wide + mixture, 0.0).astype(jnp.bfloat16)
    page_count = SLOTS // PAGE
    new_pages = jnp.where(filled[:, None, None], new_kv, jnp.zeros_like(new_kv)).reshape(page_count, PAGE, KVH, 2 * HD)
    page_ids = jnp.arange(page_count, dtype=jnp.int32)
    earlier = (new_owner[None, :] == new_owner[:, None]) & (page_ids[None, :] < page_ids[:, None])
    owner_rank = lax.optimization_barrier(jnp.sum(earlier.astype(jnp.int32), axis=1)).astype(jnp.int32)
    destination = (new_owner * OWN_MOST + owner_rank).astype(jnp.int32)
    decode_pages = jnp.zeros((N_EP * OWN_MOST, PAGE, KVH, 2 * HD), jnp.bfloat16).at[destination].set(new_pages)
    return (layer_out, decode_pages)
```

```python
import math

import jax
import jax.numpy as jnp
from jax import lax
from jax.sharding import PartitionSpec as P

HD = 128
HQ = 32
KVH = 4
HOLD_MOST = 16
WEIGHT_ROWS = 16

MASKED = -1e30
EPSILON = 1e-06


def three_parts(wide):
    high = lax.reduce_precision(wide, 8, 7)
    rest = wide - high
    middle = lax.reduce_precision(rest, 8, 7)
    low = rest - middle
    return [part.astype(jnp.bfloat16) for part in (high, middle, low)]


def local(
    queries,
    new_kv,
    cache_pool,
    hit_pages,
    span_lengths,
    out_weight,
    hidden_in,
    norm_gain,
    expert_ids,
    gate_weights,
    gate_up,
    down_weight,
    new_owner,
):
    tokens = queries.shape[0]
    model_width = hidden_in.shape[1]
    ep_count = lax.axis_size("ep")
    tp_count = lax.axis_size("tp")
    blocks = lax.axis_size("kv") * tp_count
    ep_index = lax.axis_index("ep")
    kv_index = lax.axis_index("kv")
    tp_index = lax.axis_index("tp")
    block_index = kv_index * tp_count + tp_index
    keyval_local = new_kv.shape[1]
    heads_local = queries.shape[1] // HD
    keyval_pick = block_index * heads_local // (HQ // KVH) - kv_index * keyval_local
    row_count = tokens // blocks
    pool_pages = cache_pool.shape[0]
    page_size = cache_pool.shape[1]
    held = HOLD_MOST * page_size

    hits = hit_pages.shape[0]
    owned_hits = hit_pages // pool_pages == ep_index
    earlier = jnp.arange(hits)[None, :] < jnp.arange(hits)[:, None]
    hit_rank = jnp.sum((earlier & owned_hits[None, :]).astype(jnp.int32), axis=1)
    hit_pick = owned_hits[None, :] & (
        hit_rank[None, :] == jnp.arange(HOLD_MOST, dtype=jnp.int32)[:, None]
    )
    local_page = jnp.sum(jnp.where(hit_pick, hit_pages[None, :] - ep_index * pool_pages, 0), axis=1)
    chosen = cache_pool.at[local_page].get(mode="promise_in_bounds")
    own_pages = lax.dynamic_index_in_dim(chosen, keyval_pick, 2, keepdims=False).reshape(held, 2 * HD)
    own_suffix = lax.dynamic_index_in_dim(new_kv, keyval_pick, 1, keepdims=False)

    by_expert = jnp.sum(
        jnp.where(
            expert_ids[:, :, None] == jnp.arange(ep_count, dtype=jnp.int32)[None, None, :],
            gate_weights[:, :, None],
            0.0,
        ),
        axis=1,
    )
    weight_part = jnp.stack(three_parts(by_expert.T)).reshape(-1, 2 * HD)
    weight_rows = weight_part.shape[0]
    weight_part = jnp.pad(weight_part, ((0, -weight_rows % WEIGHT_ROWS), (0, 0)))
    payload = jnp.concatenate([own_pages, own_suffix, weight_part], axis=0)
    arrived = [payload]
    for step in range(1, ep_count):
        arrived.append(
            lax.ppermute(payload, "ep", [(i, (i + step) % ep_count) for i in range(ep_count)])
        )
    sources = [(ep_index - step) % ep_count for step in range(ep_count)]

    starts = jnp.cumsum(span_lengths) - span_lengths
    slots_here = jnp.arange(tokens, dtype=jnp.int32)
    own_positions = starts[ep_index] + slots_here
    own_filled = slots_here < span_lengths[ep_index]
    holder = hit_pages // pool_pages
    keys = []
    allowed = []
    for source, block in zip(sources, arrived):
        keys.append(block[: held + tokens])
        count = jnp.sum((holder == source).astype(jnp.int32))
        open_rows = jnp.arange(held, dtype=jnp.int32) < count * page_size
        causal = (slots_here < span_lengths[source])[None, :] & (
            (starts[source] + slots_here)[None, :] <= own_positions[:, None]
        )
        allowed += [jnp.broadcast_to(open_rows[None, :], (tokens, held)), causal]
    keys = jnp.concatenate(keys, axis=0)
    allowed = jnp.concatenate(allowed, axis=1)
    grouped = queries.reshape(tokens, heads_local, HD)
    scores = jnp.einsum(
        "thd,kd->htk", grouped, keys[:, :HD], preferred_element_type=jnp.float32
    ) * (1.0 / math.sqrt(HD))
    scores = jnp.where(allowed[None], scores, MASKED)
    attention_weights = jax.nn.softmax(scores, axis=-1).astype(jnp.bfloat16)
    attended = jnp.einsum(
        "htk,kd->thd", attention_weights, keys[:, HD:], preferred_element_type=jnp.float32
    )
    attended = attended.astype(jnp.bfloat16).reshape(tokens, heads_local * HD)
    projected = jnp.dot(attended, out_weight, preferred_element_type=jnp.float32)

    projected_rows = projected.astype(jnp.bfloat16)
    heads_out = lax.dynamic_slice_in_dim(projected, block_index * row_count, row_count, 0)
    for step in range(1, blocks):
        sent = lax.dynamic_slice_in_dim(
            projected_rows, (block_index ^ step) * row_count, row_count, 0
        )
        heads_out = heads_out + lax.ppermute(
            sent, ("kv", "tp"), [(i, i ^ step) for i in range(blocks)]
        ).astype(jnp.float32)
    own_hidden = lax.dynamic_slice_in_dim(hidden_in, block_index * row_count, row_count, 0)
    residual = (own_hidden.astype(jnp.float32) + heads_out).astype(jnp.bfloat16)
    resid_wide = residual.astype(jnp.float32)
    normed = (
        resid_wide
        * lax.rsqrt(jnp.mean(resid_wide * resid_wide, axis=1, keepdims=True) + EPSILON)
        * norm_gain
    ).astype(jnp.bfloat16)

    all_normed = lax.all_gather(normed, ("ep", "kv", "tp"), axis=0, tiled=True)
    contract = (((1,), (1,)), ((), ()))
    gate_part = lax.dot_general(
        all_normed, gate_up[0, 0], contract, preferred_element_type=jnp.float32
    )
    up_part = lax.dot_general(
        all_normed, gate_up[0, 1], contract, preferred_element_type=jnp.float32
    )
    hidden = (jax.nn.silu(gate_part) * up_part).astype(jnp.bfloat16)
    down_part = jnp.dot(hidden, down_weight[0], preferred_element_type=jnp.float32)
    row_weights = []
    for block in arrived:
        parts = block[held + tokens : held + tokens + weight_rows].astype(jnp.float32)
        parts = parts.reshape(3, ep_count, tokens)
        row_weights.append(lax.dynamic_index_in_dim(jnp.sum(parts, axis=0), ep_index, 0, False))
    row_weights = jnp.stack(row_weights)
    row_weights = row_weights[(ep_index - jnp.arange(ep_count)) % ep_count].reshape(-1)
    mixture = lax.psum_scatter(
        (row_weights[:, None] * down_part).astype(jnp.bfloat16),
        ("ep", "kv", "tp"),
        scatter_dimension=0,
        tiled=True,
    ).astype(jnp.float32)
    rows_filled = lax.dynamic_slice_in_dim(own_filled, block_index * row_count, row_count, 0)
    layer_out = jnp.where(rows_filled[:, None], resid_wide + mixture, 0.0).astype(jnp.bfloat16)

    own_most = 2 * (tokens // page_size)
    page_count = new_owner.shape[0]
    pages_here = tokens // page_size
    owned_pages = new_owner == ep_index
    page_ids = jnp.arange(page_count, dtype=jnp.int32)
    owner_rank = jnp.sum(
        ((page_ids[None, :] < page_ids[:, None]) & owned_pages[None, :]).astype(jnp.int32), axis=1
    )
    choose = owned_pages[None, :] & (
        owner_rank[None, :] == jnp.arange(own_most, dtype=jnp.int32)[:, None]
    )
    page_index = jnp.sum(jnp.where(choose, page_ids[None, :], 0), axis=1)
    has_page = jnp.any(choose, axis=1)
    suffix = jnp.concatenate([block[held : held + tokens] for block in arrived], axis=0)
    spot = (ep_index - page_index // pages_here) % ep_count * pages_here + page_index % pages_here
    taken = suffix.reshape(page_count, page_size, 2 * HD).at[spot].get(mode="promise_in_bounds")
    slot_in_span = (page_index % pages_here)[:, None] * page_size + jnp.arange(page_size)[None, :]
    kept = has_page[:, None] & (slot_in_span < span_lengths[page_index // pages_here][:, None])
    head_pages = jnp.where(kept[:, :, None], taken, jnp.zeros((), jnp.bfloat16))
    if keyval_local == 1:
        decode_pages = head_pages[:, :, None, :]
    else:
        other = lax.ppermute(head_pages, "tp", [(i, i ^ 1) for i in range(tp_count)])
        first = tp_index == 0
        decode_pages = jnp.stack(
            [jnp.where(first, head_pages, other), jnp.where(first, other, head_pages)], axis=2
        )
    return (layer_out, decode_pages)


def solution(mesh):
    placed = (
        P(("groups", "ep"), ("kv", "tp")),
        P(("groups", "ep"), "kv", None),
        P(("groups", "ep"), None, "kv", None),
        P("groups"),
        P("groups"),
        P(("kv", "tp"), None),
        P(("groups", "ep"), None),
        P(),
        P(("groups", "ep"), None),
        P(("groups", "ep"), None),
        P("ep", None, ("kv", "tp"), None),
        P("ep", ("kv", "tp"), None),
        P("groups"),
    )
    return jax.shard_map(
        local,
        mesh=mesh,
        in_specs=placed,
        out_specs=(P(("groups", "ep", "kv", "tp"), None), P(("groups", "ep"), None, "kv", None)),
        check_vma=False,
    )
```

```python
import math

import jax
import jax.numpy as jnp
from jax import lax
from jax.experimental import pallas as pl
from jax.experimental.pallas import tpu as pltpu
from jax.sharding import PartitionSpec as P

HD = 128
HQ = 32
KVH = 4
HOLD_MOST = 16
WEIGHT_ROWS = 16

MASKED = -1e30
EPSILON = 1e-06


def three_parts(wide):
    high = lax.reduce_precision(wide, 8, 7)
    rest = wide - high
    middle = lax.reduce_precision(rest, 8, 7)
    low = rest - middle
    return [part.astype(jnp.bfloat16) for part in (high, middle, low)]


def piece_order(blocks):
    order = [0]
    bit = 2
    while bit < blocks:
        order += [piece ^ bit for piece in order]
        bit *= 2
    return order + [piece ^ 1 for piece in order]


TRANSPOSED = (((1,), (1,)), ((), ()))
CHUNKS = 4


def expert_kernel(count, *refs):
    row_refs = refs[:count]
    weight_ref, gate_up, down_weight, kept_ref, sent_ref = refs[count : count + 5]
    gate_up_held, down_held, gate_up_sem, down_sem = refs[count + 5 :]
    width = gate_up_held.shape[-1]
    first = [
        pltpu.make_async_copy(
            gate_up.at[0, :, :, pl.ds(i * width, width)], gate_up_held.at[i], gate_up_sem.at[i]
        )
        for i in range(CHUNKS)
    ]
    second = [
        pltpu.make_async_copy(
            down_weight.at[0, :, pl.ds(i * width, width)], down_held.at[i], down_sem.at[i]
        )
        for i in range(CHUNKS)
    ]
    for copy in first + second:
        copy.start()
    gate_part = up_part = 0.0
    for i in range(CHUNKS):
        rows = jnp.concatenate([ref[:, i * width : (i + 1) * width] for ref in row_refs], axis=0)
        first[i].wait()
        gate_part += lax.dot_general(
            rows, gate_up_held[i, 0], TRANSPOSED, preferred_element_type=jnp.float32
        )
        up_part += lax.dot_general(
            rows, gate_up_held[i, 1], TRANSPOSED, preferred_element_type=jnp.float32
        )
    hidden = gate_part / (1.0 + jnp.exp(-gate_part)) * up_part
    hidden = (hidden * weight_ref[...]).astype(jnp.bfloat16)
    half = kept_ref.shape[0]
    for i in range(CHUNKS):
        second[i].wait()
        out = jnp.dot(hidden, down_held[i], preferred_element_type=jnp.float32)
        out = out.astype(jnp.bfloat16)
        kept_ref[:, i * width : (i + 1) * width] = out[:half]
        sent_ref[:, i * width : (i + 1) * width] = out[half:]


def expert_call(have, row_weight, gate_up, down_weight):
    if have[0].shape[0] % 16:
        have = [jnp.concatenate(have, axis=0)]
    tokens = sum(piece.shape[0] for piece in have)
    model_width = have[0].shape[1]
    hidden_units = down_weight.shape[1]
    width = model_width // CHUNKS
    whole = pl.BlockSpec(memory_space=pltpu.VMEM)
    half = jax.ShapeDtypeStruct((tokens // 2, model_width), jnp.bfloat16)
    return pl.pallas_call(
        lambda *refs: expert_kernel(len(have), *refs),
        out_shape=(half, half),
        in_specs=[whole] * (len(have) + 1) + [pl.BlockSpec(memory_space=pl.ANY)] * 2,
        out_specs=(whole, whole),
        scratch_shapes=[
            pltpu.VMEM((CHUNKS, 2, hidden_units, width), jnp.bfloat16),
            pltpu.VMEM((CHUNKS, hidden_units, width), jnp.bfloat16),
            pltpu.SemaphoreType.DMA((CHUNKS,)),
            pltpu.SemaphoreType.DMA((CHUNKS,)),
        ],
        compiler_params=pltpu.CompilerParams(vmem_limit_bytes=24 * 2**20),
        cost_estimate=pl.CostEstimate(
            flops=6 * tokens * hidden_units * model_width,
            bytes_accessed=6 * hidden_units * model_width,
            transcendentals=tokens * hidden_units,
        ),
        name="experts",
    )(*have, row_weight, gate_up, down_weight)


def local(
    queries,
    new_kv,
    cache_pool,
    hit_pages,
    span_lengths,
    out_weight,
    hidden_in,
    norm_gain,
    expert_ids,
    gate_weights,
    gate_up,
    down_weight,
    new_owner,
):
    tokens = queries.shape[0]
    model_width = hidden_in.shape[1]
    ep_count = lax.axis_size("ep")
    tp_count = lax.axis_size("tp")
    blocks = lax.axis_size("kv") * tp_count
    ep_index = lax.axis_index("ep")
    kv_index = lax.axis_index("kv")
    tp_index = lax.axis_index("tp")
    block_index = kv_index * tp_count + tp_index
    keyval_local = new_kv.shape[1]
    heads_local = queries.shape[1] // HD
    keyval_pick = block_index * heads_local // (HQ // KVH) - kv_index * keyval_local
    row_count = tokens // blocks
    pool_pages = cache_pool.shape[0]
    page_size = cache_pool.shape[1]
    held = HOLD_MOST * page_size

    hits = hit_pages.shape[0]
    owned_hits = hit_pages // pool_pages == ep_index
    earlier = jnp.arange(hits)[None, :] < jnp.arange(hits)[:, None]
    hit_rank = jnp.sum((earlier & owned_hits[None, :]).astype(jnp.int32), axis=1)
    hit_pick = owned_hits[None, :] & (
        hit_rank[None, :] == jnp.arange(HOLD_MOST, dtype=jnp.int32)[:, None]
    )
    local_page = jnp.sum(jnp.where(hit_pick, hit_pages[None, :] - ep_index * pool_pages, 0), axis=1)
    chosen = cache_pool.at[local_page].get(mode="promise_in_bounds")
    own_pages = lax.dynamic_index_in_dim(chosen, keyval_pick, 2, keepdims=False).reshape(held, 2 * HD)
    own_suffix = lax.dynamic_index_in_dim(new_kv, keyval_pick, 1, keepdims=False)

    by_expert = jnp.sum(
        jnp.where(
            expert_ids[:, :, None] == jnp.arange(ep_count, dtype=jnp.int32)[None, None, :],
            gate_weights[:, :, None],
            0.0,
        ),
        axis=1,
    )
    weight_part = jnp.stack(three_parts(by_expert.T)).reshape(-1, 2 * HD)
    weight_rows = weight_part.shape[0]
    weight_part = jnp.pad(weight_part, ((0, -weight_rows % WEIGHT_ROWS), (0, 0)))
    payload = jnp.concatenate([own_pages, own_suffix, weight_part], axis=0)
    arrived = [payload]
    for step in range(1, ep_count):
        arrived.append(
            lax.ppermute(payload, "ep", [(i, i ^ step) for i in range(ep_count)])
        )
    sources = [ep_index ^ step for step in range(ep_count)]

    starts = jnp.cumsum(span_lengths) - span_lengths
    slots_here = jnp.arange(tokens, dtype=jnp.int32)
    own_positions = starts[ep_index] + slots_here
    own_filled = slots_here < span_lengths[ep_index]
    holder = hit_pages // pool_pages
    keys = []
    allowed = []
    for source, block in zip(sources, arrived):
        keys.append(block[: held + tokens])
        count = jnp.sum((holder == source).astype(jnp.int32))
        open_rows = jnp.arange(held, dtype=jnp.int32) < count * page_size
        causal = (slots_here < span_lengths[source])[None, :] & (
            (starts[source] + slots_here)[None, :] <= own_positions[:, None]
        )
        allowed += [jnp.broadcast_to(open_rows[None, :], (tokens, held)), causal]
    keys = jnp.concatenate(keys, axis=0)
    allowed = jnp.concatenate(allowed, axis=1)
    grouped = queries.reshape(tokens, heads_local, HD)
    scores = jnp.einsum(
        "thd,kd->htk", grouped, keys[:, :HD], preferred_element_type=jnp.float32
    ) * (1.0 / math.sqrt(HD))
    scores = jnp.where(allowed[None], scores, MASKED)
    attention_weights = jax.nn.softmax(scores, axis=-1).astype(jnp.bfloat16)
    attended = jnp.einsum(
        "htk,kd->thd", attention_weights, keys[:, HD:], preferred_element_type=jnp.float32
    )
    attended = attended.astype(jnp.bfloat16).reshape(tokens, heads_local * HD)
    projected = jnp.dot(attended, out_weight, preferred_element_type=jnp.float32)

    projected_rows = projected.astype(jnp.bfloat16)
    heads_out = lax.dynamic_slice_in_dim(projected, block_index * row_count, row_count, 0)
    for step in range(1, blocks):
        sent = lax.dynamic_slice_in_dim(
            projected_rows, (block_index ^ step) * row_count, row_count, 0
        )
        heads_out = heads_out + lax.ppermute(
            sent, ("kv", "tp"), [(i, i ^ step) for i in range(blocks)]
        ).astype(jnp.float32)
    own_hidden = lax.dynamic_slice_in_dim(hidden_in, block_index * row_count, row_count, 0)
    residual = (own_hidden.astype(jnp.float32) + heads_out).astype(jnp.bfloat16)
    resid_wide = residual.astype(jnp.float32)
    normed = (
        resid_wide
        * lax.rsqrt(jnp.mean(resid_wide * resid_wide, axis=1, keepdims=True) + EPSILON)
        * norm_gain
    ).astype(jnp.bfloat16)

    pieces = [block_index ^ piece for piece in piece_order(blocks)]
    pieces = jnp.stack(pieces)
    row_weights = []
    for block in arrived:
        parts = block[held + tokens : held + tokens + weight_rows].astype(jnp.float32)
        parts = jnp.sum(parts.reshape(3, ep_count, tokens), axis=0)
        parts = lax.dynamic_index_in_dim(parts, ep_index, 0, False)
        row_weights.append(parts.reshape(blocks, row_count)[pieces].reshape(tokens, 1))
    exchange = lambda value, bit: lax.ppermute(
        value, ("kv", "tp"), [(i, i ^ bit) for i in range(blocks)]
    )
    across = lambda value, step: lax.ppermute(
        value, "ep", [(i, i ^ step) for i in range(ep_count)]
    )
    bits = [1 << place for place in range(1, blocks.bit_length() - 1)]
    mixture = resid_wide
    for step in range(ep_count):
        have = [normed if step == 0 else across(normed, step)]
        for bit in bits + [1]:
            have += [exchange(piece, bit) for piece in have]
        kept, sent = expert_call(have, row_weights[step], gate_up, down_weight)
        got = exchange(sent, 1)
        for bit in reversed(bits):
            half = kept.shape[0] // 2
            give = (kept[half:].astype(jnp.float32) + got[half:].astype(jnp.float32)).astype(
                jnp.bfloat16
            )
            kept = kept[:half].astype(jnp.float32) + got[:half].astype(jnp.float32)
            got = exchange(give, bit)
        own = kept.astype(jnp.float32) + got.astype(jnp.float32)
        if step > 0:
            own = across(own.astype(jnp.bfloat16), step).astype(jnp.float32)
        mixture = mixture + own
    rows_filled = lax.dynamic_slice_in_dim(own_filled, block_index * row_count, row_count, 0)
    layer_out = jnp.where(rows_filled[:, None], mixture, 0.0).astype(jnp.bfloat16)

    own_most = 2 * (tokens // page_size)
    page_count = new_owner.shape[0]
    pages_here = tokens // page_size
    owned_pages = new_owner == ep_index
    page_ids = jnp.arange(page_count, dtype=jnp.int32)
    owner_rank = jnp.sum(
        ((page_ids[None, :] < page_ids[:, None]) & owned_pages[None, :]).astype(jnp.int32), axis=1
    )
    choose = owned_pages[None, :] & (
        owner_rank[None, :] == jnp.arange(own_most, dtype=jnp.int32)[:, None]
    )
    page_index = jnp.sum(jnp.where(choose, page_ids[None, :], 0), axis=1)
    has_page = jnp.any(choose, axis=1)
    suffix = jnp.concatenate([block[held : held + tokens] for block in arrived], axis=0)
    spot = (ep_index ^ (page_index // pages_here)) * pages_here + page_index % pages_here
    taken = suffix.reshape(page_count, page_size, 2 * HD).at[spot].get(mode="promise_in_bounds")
    slot_in_span = (page_index % pages_here)[:, None] * page_size + jnp.arange(page_size)[None, :]
    kept = has_page[:, None] & (slot_in_span < span_lengths[page_index // pages_here][:, None])
    head_pages = jnp.where(kept[:, :, None], taken, jnp.zeros((), jnp.bfloat16))
    if keyval_local == 1:
        decode_pages = head_pages[:, :, None, :]
    else:
        other = lax.ppermute(head_pages, "tp", [(i, i ^ 1) for i in range(tp_count)])
        first = tp_index == 0
        decode_pages = jnp.stack(
            [jnp.where(first, head_pages, other), jnp.where(first, other, head_pages)], axis=2
        )
    return (layer_out, decode_pages)


def solution(mesh):
    placed = (
        P(("groups", "ep"), ("kv", "tp")),
        P(("groups", "ep"), "kv", None),
        P(("groups", "ep"), None, "kv", None),
        P("groups"),
        P("groups"),
        P(("kv", "tp"), None),
        P(("groups", "ep"), None),
        P(),
        P(("groups", "ep"), None),
        P(("groups", "ep"), None),
        P("ep", None, ("kv", "tp"), None),
        P("ep", ("kv", "tp"), None),
        P("groups"),
    )
    return jax.shard_map(
        local,
        mesh=mesh,
        in_specs=placed,
        out_specs=(P(("groups", "ep", "kv", "tp"), None), P(("groups", "ep"), None, "kv", None)),
        check_vma=False,
    )
```

```python
import math

import jax
import jax.numpy as jnp
from jax import lax
from jax.experimental import pallas as pl
from jax.experimental.pallas import tpu as pltpu
from jax.sharding import PartitionSpec as P

HD = 128
HQ = 32
KVH = 4
HOLD_MOST = 16
WEIGHT_ROWS = 16

MASKED = -1e30
EPSILON = 1e-06


def three_parts(wide):
    high = lax.reduce_precision(wide, 8, 7)
    rest = wide - high
    middle = lax.reduce_precision(rest, 8, 7)
    low = rest - middle
    return [part.astype(jnp.bfloat16) for part in (high, middle, low)]


def piece_order(blocks):
    order = [0]
    bit = 2
    while bit < blocks:
        order += [piece ^ bit for piece in order]
        bit *= 2
    return order + [piece ^ 1 for piece in order]


TRANSPOSED = (((1,), (1,)), ((), ()))
WHOLE = pl.BlockSpec(memory_space=pltpu.VMEM)
ANYWHERE = pl.BlockSpec(memory_space=pl.ANY)
SCALARS = pl.BlockSpec(memory_space=pltpu.SMEM)
COLUMNS = 1024
ROWS = 256
VMEM_LIMIT = 16 * 2**20


def hold_kernel(*refs):
    count = (len(refs) - 2) // 2
    sources, held, sem = refs[:count], refs[count + 1 : -1], refs[-1]
    copies = [
        pltpu.make_async_copy(source, target, sem.at[i])
        for i, (source, target) in enumerate(zip(sources, held))
    ]
    for copy in copies:
        copy.start()
    for copy in copies:
        copy.wait()


def hold_call(arrays, after):
    size = sum(math.prod(array.shape) * 2 for array in arrays)
    return pl.pallas_call(
        hold_kernel,
        out_shape=[jax.ShapeDtypeStruct(array.shape, array.dtype) for array in arrays],
        in_specs=[ANYWHERE] * (len(arrays) + 1),
        out_specs=[WHOLE] * len(arrays),
        scratch_shapes=[pltpu.SemaphoreType.DMA((len(arrays),))],
        compiler_params=pltpu.CompilerParams(vmem_limit_bytes=VMEM_LIMIT),
        cost_estimate=pl.CostEstimate(flops=0, bytes_accessed=2 * size, transcendentals=0),
        name="hold",
    )(*arrays, after)


def attend_kernel(ep_count, held, tokens, all_open, lens, place, counts, queries, *refs):
    blocks = refs[:ep_count]
    out_weight = refs[ep_count]
    own_ref, *sent_refs = refs[ep_count + 1 : -2]
    scores, projected = refs[-2:]
    heads = queries.shape[1] // HD
    ep_index = place[0]
    block_index = place[1]
    suffix = ep_count * tokens

    own_start = jnp.int32(0)
    for j in range(ep_count):
        own_start = own_start + jnp.where(j < ep_index, lens[j], 0)
    column = lax.broadcasted_iota(jnp.int32, (tokens, suffix), 1)
    slot = column % tokens
    query_position = own_start + lax.broadcasted_iota(jnp.int32, (tokens, suffix), 0)
    seen = jnp.zeros((tokens, suffix), jnp.int32)
    for step in range(ep_count):
        source = ep_index ^ step
        start = jnp.int32(0)
        for j in range(ep_count):
            start = start + jnp.where(j < source, lens[j], 0)
        last = jnp.minimum(query_position - start, lens[source] - 1)
        here = (column // tokens == step) & (slot <= last)
        seen = seen + here.astype(jnp.int32)
    bias = jnp.where(seen > 0, 0.0, MASKED)

    suffix_keys = jnp.concatenate([block[held : held + tokens, :HD] for block in blocks], axis=0)
    suffix_values = jnp.concatenate([block[held : held + tokens, HD:] for block in blocks], axis=0)
    scale = math.log2(math.e) / math.sqrt(HD)
    rows = min(ROWS, heads * tokens)
    together = rows // tokens
    attended = []
    for first in range(0, heads, together):
        grouped = jnp.concatenate(
            [queries[:, h * HD : (h + 1) * HD] for h in range(first, first + together)], axis=0
        )
        highest = None
        for step in range(ep_count):
            part = scale * lax.dot_general(
                grouped, blocks[step][:held, :HD], TRANSPOSED, preferred_element_type=jnp.float32
            )
            if not all_open:
                entry = lax.broadcasted_iota(jnp.int32, part.shape, 1)
                part = jnp.where(entry < counts[step], part, MASKED)
            scores[:, step * held : (step + 1) * held] = part
            top = jnp.max(part, axis=1, keepdims=True)
            highest = top if highest is None else jnp.maximum(highest, top)
        part = scale * lax.dot_general(
            grouped, suffix_keys, TRANSPOSED, preferred_element_type=jnp.float32
        )
        part = part + jnp.concatenate([bias] * together, axis=0)
        highest = jnp.maximum(highest, jnp.max(part, axis=1, keepdims=True))
        part = jnp.exp2(part - highest)
        total = jnp.sum(part, axis=1, keepdims=True)
        mixed = jnp.dot(
            part.astype(jnp.bfloat16), suffix_values, preferred_element_type=jnp.float32
        )
        for step in range(ep_count):
            part = jnp.exp2(scores[:, step * held : (step + 1) * held] - highest)
            total += jnp.sum(part, axis=1, keepdims=True)
            mixed += jnp.dot(
                part.astype(jnp.bfloat16),
                blocks[step][:held, HD:],
                preferred_element_type=jnp.float32,
            )
        mixed = (mixed / total).astype(jnp.bfloat16)
        attended += [mixed[h * tokens : (h + 1) * tokens] for h in range(together)]
    attended = jnp.concatenate(attended, axis=1)
    for at in range(0, out_weight.shape[1], COLUMNS):
        projected[:, at : at + COLUMNS] = jnp.dot(
            attended, out_weight[:, at : at + COLUMNS], preferred_element_type=jnp.float32
        )
    count = own_ref.shape[0]
    own_ref[...] = projected[pl.ds(pl.multiple_of(block_index * count, count), count), :]
    for step, ref in enumerate(sent_refs, 1):
        at = pl.multiple_of((block_index ^ step) * count, count)
        ref[...] = projected[pl.ds(at, count), :].astype(jnp.bfloat16)


def attend_call(lens, place, counts, queries, arrived, out_weight, held, blocks, all_open):
    tokens = queries.shape[0]
    ep_count = len(arrived)
    model_width = out_weight.shape[1]
    heads = queries.shape[1] // HD
    row_count = tokens // blocks
    keys = ep_count * (held + tokens)
    return pl.pallas_call(
        lambda *refs: attend_kernel(ep_count, held, tokens, all_open, *refs),
        out_shape=[jax.ShapeDtypeStruct((row_count, model_width), jnp.float32)]
        + [jax.ShapeDtypeStruct((row_count, model_width), jnp.bfloat16)] * (blocks - 1),
        in_specs=[SCALARS] * 3 + [WHOLE] * (ep_count + 2),
        out_specs=[WHOLE] * blocks,
        scratch_shapes=[
            pltpu.VMEM((min(ROWS, heads * tokens), ep_count * held), jnp.float32),
            pltpu.VMEM((tokens, model_width), jnp.float32),
        ],
        compiler_params=pltpu.CompilerParams(vmem_limit_bytes=VMEM_LIMIT),
        cost_estimate=pl.CostEstimate(
            flops=4 * heads * tokens * keys * HD + 2 * tokens * heads * HD * model_width,
            bytes_accessed=2 * heads * HD * model_width,
            transcendentals=heads * tokens * keys,
        ),
        name="attend",
    )(lens, place, counts, queries, *arrived, out_weight)


def expert_kernel(count, *refs):
    row_refs = refs[:count]
    weight_ref, gate_up, down_weight = refs[count : count + 3]
    kept_ref, sent_ref = refs[-2:]
    model_width = kept_ref.shape[1]
    gate_part = up_part = 0.0
    for at in range(0, model_width, COLUMNS):
        rows = jnp.concatenate([ref[:, at : at + COLUMNS] for ref in row_refs], axis=0)
        gate_part += lax.dot_general(
            rows, gate_up[0, 0, :, at : at + COLUMNS], TRANSPOSED, preferred_element_type=jnp.float32
        )
        up_part += lax.dot_general(
            rows, gate_up[0, 1, :, at : at + COLUMNS], TRANSPOSED, preferred_element_type=jnp.float32
        )
    hidden = gate_part / (1.0 + jnp.exp(-gate_part)) * up_part
    hidden = (hidden * weight_ref[...]).astype(jnp.bfloat16)
    half = kept_ref.shape[0]
    for at in range(0, model_width, COLUMNS):
        out = jnp.dot(
            hidden, down_weight[0, :, at : at + COLUMNS], preferred_element_type=jnp.float32
        ).astype(jnp.bfloat16)
        kept_ref[:, at : at + COLUMNS] = out[:half]
        sent_ref[:, at : at + COLUMNS] = out[half:]


def expert_call(have, row_weight, gate_up, down_weight, after):
    if have[0].shape[0] % 16:
        have = [jnp.concatenate(have, axis=0)]
    tokens = sum(piece.shape[0] for piece in have)
    model_width = have[0].shape[1]
    hidden_units = down_weight.shape[1]
    half = jax.ShapeDtypeStruct((tokens // 2, model_width), jnp.bfloat16)
    return pl.pallas_call(
        lambda *refs: expert_kernel(len(have), *refs),
        out_shape=(half, half),
        in_specs=[WHOLE] * (len(have) + 3) + [ANYWHERE] * len(after),
        out_specs=(WHOLE, WHOLE),
        compiler_params=pltpu.CompilerParams(vmem_limit_bytes=VMEM_LIMIT),
        cost_estimate=pl.CostEstimate(
            flops=6 * tokens * hidden_units * model_width,
            bytes_accessed=6 * hidden_units * model_width,
            transcendentals=tokens * hidden_units,
        ),
        name="experts",
    )(*have, row_weight, gate_up, down_weight, *after)


def local(
    queries,
    new_kv,
    cache_pool,
    hit_pages,
    span_lengths,
    out_weight,
    hidden_in,
    norm_gain,
    expert_ids,
    gate_weights,
    gate_up,
    down_weight,
    new_owner,
):
    tokens = queries.shape[0]
    model_width = hidden_in.shape[1]
    ep_count = lax.axis_size("ep")
    tp_count = lax.axis_size("tp")
    blocks = lax.axis_size("kv") * tp_count
    ep_index = lax.axis_index("ep")
    kv_index = lax.axis_index("kv")
    tp_index = lax.axis_index("tp")
    block_index = kv_index * tp_count + tp_index
    keyval_local = new_kv.shape[1]
    heads_local = queries.shape[1] // HD
    keyval_pick = block_index * heads_local // (HQ // KVH) - kv_index * keyval_local
    row_count = tokens // blocks
    pool_pages = cache_pool.shape[0]
    page_size = cache_pool.shape[1]
    held = HOLD_MOST * page_size

    hits = hit_pages.shape[0]
    owned_hits = hit_pages // pool_pages == ep_index
    earlier = jnp.arange(hits)[None, :] < jnp.arange(hits)[:, None]
    hit_rank = jnp.sum((earlier & owned_hits[None, :]).astype(jnp.int32), axis=1)
    hit_pick = owned_hits[None, :] & (
        hit_rank[None, :] == jnp.arange(HOLD_MOST, dtype=jnp.int32)[:, None]
    )
    local_page = jnp.sum(jnp.where(hit_pick, hit_pages[None, :] - ep_index * pool_pages, 0), axis=1)
    chosen = cache_pool.at[local_page].get(mode="promise_in_bounds")
    own_pages = lax.dynamic_index_in_dim(chosen, keyval_pick, 2, keepdims=False).reshape(held, 2 * HD)
    own_suffix = lax.dynamic_index_in_dim(new_kv, keyval_pick, 1, keepdims=False)

    by_expert = jnp.sum(
        jnp.where(
            expert_ids[:, :, None] == jnp.arange(ep_count, dtype=jnp.int32)[None, None, :],
            gate_weights[:, :, None],
            0.0,
        ),
        axis=1,
    )
    weight_part = jnp.stack(three_parts(by_expert.T)).reshape(-1, 2 * HD)
    weight_rows = weight_part.shape[0]
    weight_part = jnp.pad(weight_part, ((0, -weight_rows % WEIGHT_ROWS), (0, 0)))
    payload = jnp.concatenate([own_pages, own_suffix, weight_part], axis=0)
    arrived = [payload]
    for step in range(1, ep_count):
        arrived.append(
            lax.ppermute(payload, "ep", [(i, i ^ step) for i in range(ep_count)])
        )
    sources = [ep_index ^ step for step in range(ep_count)]

    held_out, held_gate_up, held_down = hold_call([out_weight, gate_up, down_weight], payload)
    all_open = hits == HOLD_MOST * ep_count
    holder = hit_pages // pool_pages
    counts = jnp.sum(
        (holder[None, :] == jnp.stack(sources)[:, None]).astype(jnp.int32) * page_size, axis=1
    )
    if all_open:
        counts = jnp.zeros((1,), jnp.int32)
    place = jnp.stack([ep_index, block_index]).astype(jnp.int32)
    heads_out, *sent_rows = attend_call(
        span_lengths, place, counts, queries, arrived, held_out, held, blocks, all_open
    )
    for step, sent in enumerate(sent_rows, 1):
        heads_out = heads_out + lax.ppermute(
            sent, ("kv", "tp"), [(i, i ^ step) for i in range(blocks)]
        ).astype(jnp.float32)
    own_hidden = lax.dynamic_slice_in_dim(hidden_in, block_index * row_count, row_count, 0)
    residual = (own_hidden.astype(jnp.float32) + heads_out).astype(jnp.bfloat16)
    resid_wide = residual.astype(jnp.float32)
    normed = (
        resid_wide
        * lax.rsqrt(jnp.mean(resid_wide * resid_wide, axis=1, keepdims=True) + EPSILON)
        * norm_gain
    ).astype(jnp.bfloat16)

    pieces = [block_index ^ piece for piece in piece_order(blocks)]
    pieces = jnp.stack(pieces)
    row_weights = []
    for block in arrived:
        parts = block[held + tokens : held + tokens + weight_rows].astype(jnp.float32)
        parts = jnp.sum(parts.reshape(3, ep_count, tokens), axis=0)
        parts = lax.dynamic_index_in_dim(parts, ep_index, 0, False)
        row_weights.append(parts.reshape(blocks, row_count)[pieces].reshape(tokens, 1))
    exchange = lambda value, bit: lax.ppermute(
        value, ("kv", "tp"), [(i, i ^ bit) for i in range(blocks)]
    )
    across = lambda value, step: lax.ppermute(
        value, "ep", [(i, i ^ step) for i in range(ep_count)]
    )
    bits = [1 << place for place in range(1, blocks.bit_length() - 1)]
    haves = []
    for step in range(ep_count):
        have = [normed if step == 0 else across(normed, step)]
        for bit in bits + [1]:
            have += [exchange(piece, bit) for piece in have]
        haves.append(have)
    mixture = resid_wide
    given = []
    finished = []
    for step in range(ep_count):
        after = given[step - 2 : step - 1] if step >= 2 else []
        after = after + (finished[step - 3 : step - 2] if step >= 3 else [])
        kept, sent = expert_call(haves[step], row_weights[step], held_gate_up, held_down, after)
        got = exchange(sent, 1)
        for bit in reversed(bits):
            half = kept.shape[0] // 2
            give = (kept[half:].astype(jnp.float32) + got[half:].astype(jnp.float32)).astype(
                jnp.bfloat16
            )
            if bit == bits[-1]:
                given.append(give)
            kept = kept[:half].astype(jnp.float32) + got[:half].astype(jnp.float32)
            got = exchange(give, bit)
        own = (kept.astype(jnp.float32) + got.astype(jnp.float32)).astype(jnp.bfloat16)
        finished.append(own)
        if step > 0:
            own = across(own, step)
        mixture = mixture + own.astype(jnp.float32)
    own_slots = block_index * row_count + jnp.arange(row_count, dtype=jnp.int32)
    rows_filled = own_slots < span_lengths[ep_index]
    layer_out = jnp.where(rows_filled[:, None], mixture, 0.0).astype(jnp.bfloat16)

    own_most = 2 * (tokens // page_size)
    page_count = new_owner.shape[0]
    pages_here = tokens // page_size
    owned_pages = new_owner == ep_index
    page_ids = jnp.arange(page_count, dtype=jnp.int32)
    owner_rank = jnp.sum(
        ((page_ids[None, :] < page_ids[:, None]) & owned_pages[None, :]).astype(jnp.int32), axis=1
    )
    choose = owned_pages[None, :] & (
        owner_rank[None, :] == jnp.arange(own_most, dtype=jnp.int32)[:, None]
    )
    page_index = jnp.sum(jnp.where(choose, page_ids[None, :], 0), axis=1)
    has_page = jnp.any(choose, axis=1)
    suffix = jnp.concatenate([block[held : held + tokens] for block in arrived], axis=0)
    spot = (ep_index ^ (page_index // pages_here)) * pages_here + page_index % pages_here
    taken = suffix.reshape(page_count, page_size, 2 * HD).at[spot].get(mode="promise_in_bounds")
    slot_in_span = (page_index % pages_here)[:, None] * page_size + jnp.arange(page_size)[None, :]
    kept = has_page[:, None] & (slot_in_span < span_lengths[page_index // pages_here][:, None])
    head_pages = jnp.where(kept[:, :, None], taken, jnp.zeros((), jnp.bfloat16))
    if keyval_local == 1:
        decode_pages = head_pages[:, :, None, :]
    else:
        other = lax.ppermute(head_pages, "tp", [(i, i ^ 1) for i in range(tp_count)])
        first = tp_index == 0
        decode_pages = jnp.stack(
            [jnp.where(first, head_pages, other), jnp.where(first, other, head_pages)], axis=2
        )
    return (layer_out, decode_pages)


def solution(mesh):
    placed = (
        P(("groups", "ep"), ("kv", "tp")),
        P(("groups", "ep"), "kv", None),
        P(("groups", "ep"), None, "kv", None),
        P("groups"),
        P("groups"),
        P(("kv", "tp"), None),
        P(("groups", "ep"), None),
        P(),
        P(("groups", "ep"), None),
        P(("groups", "ep"), None),
        P("ep", None, ("kv", "tp"), None),
        P("ep", ("kv", "tp"), None),
        P("groups"),
    )
    return jax.shard_map(
        local,
        mesh=mesh,
        in_specs=placed,
        out_specs=(P(("groups", "ep", "kv", "tp"), None), P(("groups", "ep"), None, "kv", None)),
        check_vma=False,
    )
```

```python
import math

import jax
import jax.numpy as jnp
from jax import lax
from jax.experimental import pallas as pl
from jax.experimental.pallas import tpu as pltpu
from jax.sharding import PartitionSpec as P

HD = 128
HQ = 32
KVH = 4
HOLD_MOST = 16
WEIGHT_ROWS = 16

MASKED = -1e30
EPSILON = 1e-06


def three_parts(wide):
    high = lax.reduce_precision(wide, 8, 7)
    rest = wide - high
    middle = lax.reduce_precision(rest, 8, 7)
    low = rest - middle
    return [part.astype(jnp.bfloat16) for part in (high, middle, low)]


def piece_order(blocks):
    order = [0]
    bit = 2
    while bit < blocks:
        order += [piece ^ bit for piece in order]
        bit *= 2
    return order + [piece ^ 1 for piece in order]


TRANSPOSED = (((1,), (1,)), ((), ()))
WHOLE = pl.BlockSpec(memory_space=pltpu.VMEM)
ANYWHERE = pl.BlockSpec(memory_space=pl.ANY)
SCALARS = pl.BlockSpec(memory_space=pltpu.SMEM)
COLUMNS = 1024
ROWS = 256
VMEM_LIMIT = 16 * 2**20
LITTLE = pl.CostEstimate(flops=1024, bytes_accessed=1024, transcendentals=0)


def hold_kernel(*refs):
    count = (len(refs) - 2) // 2
    sources, held, sem = refs[:count], refs[count + 1 : -1], refs[-1]
    copies = [
        pltpu.make_async_copy(source, target, sem.at[i])
        for i, (source, target) in enumerate(zip(sources, held))
    ]
    for copy in copies:
        copy.start()
    for copy in copies:
        copy.wait()


def hold_call(arrays, after):
    return pl.pallas_call(
        hold_kernel,
        out_shape=[jax.ShapeDtypeStruct(array.shape, array.dtype) for array in arrays],
        in_specs=[ANYWHERE] * (len(arrays) + 1),
        out_specs=[WHOLE] * len(arrays),
        scratch_shapes=[pltpu.SemaphoreType.DMA((len(arrays),))],
        compiler_params=pltpu.CompilerParams(vmem_limit_bytes=VMEM_LIMIT),
        cost_estimate=LITTLE,
        name="hold",
    )(*arrays, after)


def attend_kernel(ep_count, held, tokens, all_open, lens, place, counts, queries, *refs):
    blocks = refs[:ep_count]
    out_weight = refs[ep_count]
    own_ref, *sent_refs = refs[ep_count + 1 : -2]
    scores, projected = refs[-2:]
    heads = queries.shape[1] // HD
    ep_index = place[0]
    block_index = place[1]
    suffix = ep_count * tokens

    own_start = jnp.int32(0)
    for j in range(ep_count):
        own_start = own_start + jnp.where(j < ep_index, lens[j], 0)
    column = lax.broadcasted_iota(jnp.int32, (tokens, suffix), 1)
    slot = column % tokens
    query_position = own_start + lax.broadcasted_iota(jnp.int32, (tokens, suffix), 0)
    seen = jnp.zeros((tokens, suffix), jnp.int32)
    for step in range(ep_count):
        source = ep_index ^ step
        start = jnp.int32(0)
        for j in range(ep_count):
            start = start + jnp.where(j < source, lens[j], 0)
        last = jnp.minimum(query_position - start, lens[source] - 1)
        here = (column // tokens == step) & (slot <= last)
        seen = seen + here.astype(jnp.int32)
    bias = jnp.where(seen > 0, 0.0, MASKED)

    suffix_keys = jnp.concatenate([block[held : held + tokens, :HD] for block in blocks], axis=0)
    suffix_values = jnp.concatenate([block[held : held + tokens, HD:] for block in blocks], axis=0)
    scale = math.log2(math.e) / math.sqrt(HD)
    rows = min(ROWS, heads * tokens)
    together = rows // tokens
    attended = []
    for first in range(0, heads, together):
        grouped = jnp.concatenate(
            [queries[:, h * HD : (h + 1) * HD] for h in range(first, first + together)], axis=0
        )
        highest = None
        for step in range(ep_count):
            part = scale * lax.dot_general(
                grouped, blocks[step][:held, :HD], TRANSPOSED, preferred_element_type=jnp.float32
            )
            if not all_open:
                entry = lax.broadcasted_iota(jnp.int32, part.shape, 1)
                part = jnp.where(entry < counts[step], part, MASKED)
            scores[:, step * held : (step + 1) * held] = part
            top = jnp.max(part, axis=1, keepdims=True)
            highest = top if highest is None else jnp.maximum(highest, top)
        part = scale * lax.dot_general(
            grouped, suffix_keys, TRANSPOSED, preferred_element_type=jnp.float32
        )
        part = part + jnp.concatenate([bias] * together, axis=0)
        highest = jnp.maximum(highest, jnp.max(part, axis=1, keepdims=True))
        part = jnp.exp2(part - highest)
        total = jnp.sum(part, axis=1, keepdims=True)
        mixed = jnp.dot(
            part.astype(jnp.bfloat16), suffix_values, preferred_element_type=jnp.float32
        )
        for step in range(ep_count):
            part = jnp.exp2(scores[:, step * held : (step + 1) * held] - highest)
            total += jnp.sum(part, axis=1, keepdims=True)
            mixed += jnp.dot(
                part.astype(jnp.bfloat16),
                blocks[step][:held, HD:],
                preferred_element_type=jnp.float32,
            )
        mixed = (mixed / total).astype(jnp.bfloat16)
        attended += [mixed[h * tokens : (h + 1) * tokens] for h in range(together)]
    attended = jnp.concatenate(attended, axis=1)
    for at in range(0, out_weight.shape[1], COLUMNS):
        projected[:, at : at + COLUMNS] = jnp.dot(
            attended, out_weight[:, at : at + COLUMNS], preferred_element_type=jnp.float32
        )
    count = own_ref.shape[0]
    own_ref[...] = projected[pl.ds(pl.multiple_of(block_index * count, count), count), :]
    for step, ref in enumerate(sent_refs, 1):
        at = pl.multiple_of((block_index ^ step) * count, count)
        ref[...] = projected[pl.ds(at, count), :].astype(jnp.bfloat16)


def attend_call(lens, place, counts, queries, arrived, out_weight, held, blocks, all_open):
    tokens = queries.shape[0]
    ep_count = len(arrived)
    model_width = out_weight.shape[1]
    heads = queries.shape[1] // HD
    row_count = tokens // blocks
    return pl.pallas_call(
        lambda *refs: attend_kernel(ep_count, held, tokens, all_open, *refs),
        out_shape=[jax.ShapeDtypeStruct((row_count, model_width), jnp.float32)]
        + [jax.ShapeDtypeStruct((row_count, model_width), jnp.bfloat16)] * (blocks - 1),
        in_specs=[SCALARS] * 3 + [WHOLE] * (ep_count + 2),
        out_specs=[WHOLE] * blocks,
        scratch_shapes=[
            pltpu.VMEM((min(ROWS, heads * tokens), ep_count * held), jnp.float32),
            pltpu.VMEM((tokens, model_width), jnp.float32),
        ],
        compiler_params=pltpu.CompilerParams(vmem_limit_bytes=VMEM_LIMIT),
        cost_estimate=LITTLE,
        name="attend",
    )(lens, place, counts, queries, *arrived, out_weight)


def expert_kernel(count, ep_count, blocks, weight_at, place, payload, *refs):
    row_refs = refs[:count]
    gate_up, down_weight = refs[count : count + 2]
    kept_ref, sent_ref = refs[-2:]
    tokens = 2 * kept_ref.shape[0]
    row_count = tokens // blocks

    parts = payload[weight_at:, :].astype(jnp.float32)
    part_row = lax.broadcasted_iota(jnp.int32, parts.shape, 0)
    chosen = (part_row % ep_count == place[0]) & (part_row < 3 * ep_count)
    by_token = jnp.sum(jnp.where(chosen, parts, 0.0), axis=0, keepdims=True)
    row = lax.broadcasted_iota(jnp.int32, (tokens, parts.shape[1]), 0)
    token = row % row_count
    for spot, piece in enumerate(piece_order(blocks)):
        token = token + jnp.where(row // row_count == spot, (place[1] ^ piece) * row_count, 0)
    here = lax.broadcasted_iota(jnp.int32, (tokens, parts.shape[1]), 1) == token
    row_weight = jnp.sum(jnp.where(here, by_token, 0.0), axis=1, keepdims=True)

    model_width = kept_ref.shape[1]
    gate_part = up_part = 0.0
    for at in range(0, model_width, COLUMNS):
        rows = jnp.concatenate([ref[:, at : at + COLUMNS] for ref in row_refs], axis=0)
        gate_part += lax.dot_general(
            rows, gate_up[0, 0, :, at : at + COLUMNS], TRANSPOSED, preferred_element_type=jnp.float32
        )
        up_part += lax.dot_general(
            rows, gate_up[0, 1, :, at : at + COLUMNS], TRANSPOSED, preferred_element_type=jnp.float32
        )
    hidden = gate_part / (1.0 + jnp.exp(-gate_part)) * up_part
    hidden = (hidden * row_weight).astype(jnp.bfloat16)
    half = kept_ref.shape[0]
    for at in range(0, model_width, COLUMNS):
        out = jnp.dot(
            hidden, down_weight[0, :, at : at + COLUMNS], preferred_element_type=jnp.float32
        ).astype(jnp.bfloat16)
        kept_ref[:, at : at + COLUMNS] = out[:half]
        sent_ref[:, at : at + COLUMNS] = out[half:]


def expert_call(place, payload, have, gate_up, down_weight, after, ep_count, blocks, weight_at):
    if have[0].shape[0] % 16:
        have = [jnp.concatenate(have, axis=0)]
    tokens = sum(piece.shape[0] for piece in have)
    model_width = have[0].shape[1]
    hidden_units = down_weight.shape[1]
    half = jax.ShapeDtypeStruct((tokens // 2, model_width), jnp.bfloat16)
    return pl.pallas_call(
        lambda *refs: expert_kernel(len(have), ep_count, blocks, weight_at, *refs),
        out_shape=(half, half),
        in_specs=[SCALARS] + [WHOLE] * (len(have) + 3) + [ANYWHERE] * len(after),
        out_specs=(WHOLE, WHOLE),
        compiler_params=pltpu.CompilerParams(vmem_limit_bytes=VMEM_LIMIT),
        cost_estimate=LITTLE,
        name="experts",
    )(place, payload, *have, gate_up, down_weight, *after)


def local(
    queries,
    new_kv,
    cache_pool,
    hit_pages,
    span_lengths,
    out_weight,
    hidden_in,
    norm_gain,
    expert_ids,
    gate_weights,
    gate_up,
    down_weight,
    new_owner,
):
    tokens = queries.shape[0]
    model_width = hidden_in.shape[1]
    ep_count = lax.axis_size("ep")
    tp_count = lax.axis_size("tp")
    blocks = lax.axis_size("kv") * tp_count
    ep_index = lax.axis_index("ep")
    kv_index = lax.axis_index("kv")
    tp_index = lax.axis_index("tp")
    block_index = kv_index * tp_count + tp_index
    keyval_local = new_kv.shape[1]
    heads_local = queries.shape[1] // HD
    keyval_pick = block_index * heads_local // (HQ // KVH) - kv_index * keyval_local
    row_count = tokens // blocks
    pool_pages = cache_pool.shape[0]
    page_size = cache_pool.shape[1]
    held = HOLD_MOST * page_size

    hits = hit_pages.shape[0]
    owned_hits = hit_pages // pool_pages == ep_index
    earlier = jnp.arange(hits)[None, :] < jnp.arange(hits)[:, None]
    hit_rank = jnp.sum((earlier & owned_hits[None, :]).astype(jnp.int32), axis=1)
    hit_pick = owned_hits[None, :] & (
        hit_rank[None, :] == jnp.arange(HOLD_MOST, dtype=jnp.int32)[:, None]
    )
    local_page = jnp.sum(jnp.where(hit_pick, hit_pages[None, :] - ep_index * pool_pages, 0), axis=1)
    chosen = cache_pool.at[local_page].get(mode="promise_in_bounds")
    own_pages = lax.dynamic_index_in_dim(chosen, keyval_pick, 2, keepdims=False).reshape(held, 2 * HD)
    own_suffix = lax.dynamic_index_in_dim(new_kv, keyval_pick, 1, keepdims=False)

    by_expert = jnp.sum(
        jnp.where(
            expert_ids[:, :, None] == jnp.arange(ep_count, dtype=jnp.int32)[None, None, :],
            gate_weights[:, :, None],
            0.0,
        ),
        axis=1,
    )
    weight_part = jnp.concatenate(three_parts(by_expert.T), axis=0)
    weight_rows = weight_part.shape[0]
    weight_part = jnp.pad(
        weight_part, ((0, -weight_rows % WEIGHT_ROWS), (0, 2 * HD - weight_part.shape[1]))
    )
    payload = jnp.concatenate([own_pages, own_suffix, weight_part], axis=0)
    arrived = [payload]
    for step in range(1, ep_count):
        arrived.append(
            lax.ppermute(payload, "ep", [(i, i ^ step) for i in range(ep_count)])
        )
    sources = [ep_index ^ step for step in range(ep_count)]

    held_out = hold_call([out_weight], payload)[0]
    all_open = hits == HOLD_MOST * ep_count
    holder = hit_pages // pool_pages
    counts = jnp.sum(
        (holder[None, :] == jnp.stack(sources)[:, None]).astype(jnp.int32) * page_size, axis=1
    )
    if all_open:
        counts = jnp.zeros((1,), jnp.int32)
    place = jnp.stack([ep_index, block_index]).astype(jnp.int32)
    heads_out, *sent_rows = attend_call(
        span_lengths, place, counts, queries, arrived, held_out, held, blocks, all_open
    )
    for step, sent in enumerate(sent_rows, 1):
        heads_out = heads_out + lax.ppermute(
            sent, ("kv", "tp"), [(i, i ^ step) for i in range(blocks)]
        ).astype(jnp.float32)
    own_hidden = lax.dynamic_slice_in_dim(hidden_in, block_index * row_count, row_count, 0)
    residual = (own_hidden.astype(jnp.float32) + heads_out).astype(jnp.bfloat16)
    resid_wide = residual.astype(jnp.float32)
    normed = (
        resid_wide
        * lax.rsqrt(jnp.mean(resid_wide * resid_wide, axis=1, keepdims=True) + EPSILON)
        * norm_gain
    ).astype(jnp.bfloat16)

    exchange = lambda value, bit: lax.ppermute(
        value, ("kv", "tp"), [(i, i ^ bit) for i in range(blocks)]
    )
    across = lambda value, step: lax.ppermute(
        value, "ep", [(i, i ^ step) for i in range(ep_count)]
    )
    bits = [1 << place for place in range(1, blocks.bit_length() - 1)]
    held_gate_up, held_down = hold_call([gate_up, down_weight], normed)
    order = list(range(ep_count - 1, -1, -1))
    gathered = {step: [normed if step == 0 else across(normed, step)] for step in order}
    for step in order:
        for bit in bits + [1]:
            gathered[step] += [exchange(piece, bit) for piece in gathered[step]]
    mixture = resid_wide
    given = []
    finished = []
    for turn, step in enumerate(order):
        after = given[turn - 2 : turn - 1] if turn >= 2 else []
        after = after + (finished[turn - 3 : turn - 2] if turn >= 3 else [])
        kept, sent = expert_call(
            place,
            arrived[step],
            gathered[step],
            held_gate_up,
            held_down,
            after,
            ep_count,
            blocks,
            held + tokens,
        )
        got = exchange(sent, 1)
        for bit in reversed(bits):
            half = kept.shape[0] // 2
            give = (kept[half:].astype(jnp.float32) + got[half:].astype(jnp.float32)).astype(
                jnp.bfloat16
            )
            if bit == bits[-1]:
                given.append(give)
            kept = kept[:half].astype(jnp.float32) + got[:half].astype(jnp.float32)
            got = exchange(give, bit)
        own = (kept.astype(jnp.float32) + got.astype(jnp.float32)).astype(jnp.bfloat16)
        finished.append(own)
        if step > 0:
            own = across(own, step)
        mixture = mixture + own.astype(jnp.float32)
    own_slots = block_index * row_count + jnp.arange(row_count, dtype=jnp.int32)
    rows_filled = own_slots < span_lengths[ep_index]
    layer_out = jnp.where(rows_filled[:, None], mixture, 0.0).astype(jnp.bfloat16)

    own_most = 2 * (tokens // page_size)
    page_count = new_owner.shape[0]
    pages_here = tokens // page_size
    owned_pages = new_owner == ep_index
    page_ids = jnp.arange(page_count, dtype=jnp.int32)
    owner_rank = jnp.sum(
        ((page_ids[None, :] < page_ids[:, None]) & owned_pages[None, :]).astype(jnp.int32), axis=1
    )
    choose = owned_pages[None, :] & (
        owner_rank[None, :] == jnp.arange(own_most, dtype=jnp.int32)[:, None]
    )
    page_index = jnp.sum(jnp.where(choose, page_ids[None, :], 0), axis=1)
    has_page = jnp.any(choose, axis=1)
    suffix = jnp.concatenate([block[held : held + tokens] for block in arrived], axis=0)
    spot = (ep_index ^ (page_index // pages_here)) * pages_here + page_index % pages_here
    taken = suffix.reshape(page_count, page_size, 2 * HD).at[spot].get(mode="promise_in_bounds")
    slot_in_span = (page_index % pages_here)[:, None] * page_size + jnp.arange(page_size)[None, :]
    kept = has_page[:, None] & (slot_in_span < span_lengths[page_index // pages_here][:, None])
    head_pages = jnp.where(kept[:, :, None], taken, jnp.zeros((), jnp.bfloat16))
    if keyval_local == 1:
        decode_pages = head_pages[:, :, None, :]
    else:
        other = lax.ppermute(head_pages, "tp", [(i, i ^ 1) for i in range(tp_count)])
        first = tp_index == 0
        decode_pages = jnp.stack(
            [jnp.where(first, head_pages, other), jnp.where(first, other, head_pages)], axis=2
        )
    return (layer_out, decode_pages)


def solution(mesh):
    placed = (
        P(("groups", "ep"), ("kv", "tp")),
        P(("groups", "ep"), "kv", None),
        P(("groups", "ep"), None, "kv", None),
        P("groups"),
        P("groups"),
        P(("kv", "tp"), None),
        P(("groups", "ep"), None),
        P(),
        P(("groups", "ep"), None),
        P(("groups", "ep"), None),
        P("ep", None, ("kv", "tp"), None),
        P("ep", ("kv", "tp"), None),
        P("groups"),
    )
    return jax.shard_map(
        local,
        mesh=mesh,
        in_specs=placed,
        out_specs=(P(("groups", "ep", "kv", "tp"), None), P(("groups", "ep"), None, "kv", None)),
        check_vma=False,
    )
```

```python
import math

import jax
import jax.numpy as jnp
from jax import lax
from jax.experimental import pallas as pl
from jax.experimental.pallas import tpu as pltpu
from jax.sharding import PartitionSpec as P

HD = 128
HQ = 32
KVH = 4
HOLD_MOST = 16
WEIGHT_ROWS = 16

MASKED = -1e30
EPSILON = 1e-06


def three_parts(wide):
    high = lax.reduce_precision(wide, 8, 7)
    rest = wide - high
    middle = lax.reduce_precision(rest, 8, 7)
    low = rest - middle
    return [part.astype(jnp.bfloat16) for part in (high, middle, low)]


def piece_order(blocks):
    order = [0]
    bit = 2
    while bit < blocks:
        order += [piece ^ bit for piece in order]
        bit *= 2
    return order + [piece ^ 1 for piece in order]


TRANSPOSED = (((1,), (1,)), ((), ()))
WHOLE = pl.BlockSpec(memory_space=pltpu.VMEM)
ANYWHERE = pl.BlockSpec(memory_space=pl.ANY)
SCALARS = pl.BlockSpec(memory_space=pltpu.SMEM)
COLUMNS = 1024
ROWS = 256
VMEM_LIMIT = 60 * 2**20 + 2**17


def attend_kernel(ep_count, held, tokens, row_blocks, all_open, lens, place, counts, queries, *refs):
    blocks = refs[:ep_count]
    out_weight = refs[ep_count]
    kept_ref, sent_ref = refs[ep_count + 1 : ep_count + 3]
    scores, projected, fetched, fetch_sem = refs[ep_count + 3 :]
    fetches = []
    for i in range(fetched.shape[0]):
        fetches.append(
            pltpu.make_async_copy(
                out_weight.at[:, pl.ds(i * COLUMNS, COLUMNS)], fetched.at[i], fetch_sem.at[i]
            )
        )
        fetches[i].start()
    heads = queries.shape[1] // HD
    ep_index = place[0]
    block_index = place[1]
    suffix = ep_count * tokens

    own_start = jnp.int32(0)
    for j in range(ep_count):
        own_start = own_start + jnp.where(j < ep_index, lens[j], 0)
    column = lax.broadcasted_iota(jnp.int32, (tokens, suffix), 1)
    slot = column % tokens
    query_position = own_start + lax.broadcasted_iota(jnp.int32, (tokens, suffix), 0)
    seen = jnp.zeros((tokens, suffix), jnp.int32)
    for step in range(ep_count):
        source = ep_index ^ step
        start = jnp.int32(0)
        for j in range(ep_count):
            start = start + jnp.where(j < source, lens[j], 0)
        last = jnp.minimum(query_position - start, lens[source] - 1)
        here = (column // tokens == step) & (slot <= last)
        seen = seen + here.astype(jnp.int32)
    bias = jnp.where(seen > 0, 0.0, MASKED)

    suffix_keys = jnp.concatenate([block[held : held + tokens, :HD] for block in blocks], axis=0)
    suffix_values = jnp.concatenate([block[held : held + tokens, HD:] for block in blocks], axis=0)
    scale = math.log2(math.e) / math.sqrt(HD)
    rows = min(ROWS, heads * tokens)
    together = rows // tokens
    attended = []
    for first in range(0, heads, together):
        grouped = jnp.concatenate(
            [queries[:, h * HD : (h + 1) * HD] for h in range(first, first + together)], axis=0
        )
        highest = None
        for step in range(ep_count):
            part = scale * lax.dot_general(
                grouped, blocks[step][:held, :HD], TRANSPOSED, preferred_element_type=jnp.float32
            )
            if not all_open:
                entry = lax.broadcasted_iota(jnp.int32, part.shape, 1)
                part = jnp.where(entry < counts[step], part, MASKED)
            scores[:, step * held : (step + 1) * held] = part
            top = jnp.max(part, axis=1, keepdims=True)
            highest = top if highest is None else jnp.maximum(highest, top)
        part = scale * lax.dot_general(
            grouped, suffix_keys, TRANSPOSED, preferred_element_type=jnp.float32
        )
        part = part + jnp.concatenate([bias] * together, axis=0)
        highest = jnp.maximum(highest, jnp.max(part, axis=1, keepdims=True))
        part = jnp.exp2(part - highest)
        total = jnp.sum(part, axis=1, keepdims=True)
        mixed = jnp.dot(
            part.astype(jnp.bfloat16), suffix_values, preferred_element_type=jnp.float32
        )
        for step in range(ep_count):
            part = jnp.exp2(scores[:, step * held : (step + 1) * held] - highest)
            total += jnp.sum(part, axis=1, keepdims=True)
            mixed += jnp.dot(
                part.astype(jnp.bfloat16),
                blocks[step][:held, HD:],
                preferred_element_type=jnp.float32,
            )
        mixed = (mixed / total).astype(jnp.bfloat16)
        attended += [mixed[h * tokens : (h + 1) * tokens] for h in range(together)]
    attended = jnp.concatenate(attended, axis=1)
    for i, fetch in enumerate(fetches):
        fetch.wait()
        projected[:, i * COLUMNS : (i + 1) * COLUMNS] = jnp.dot(
            attended, fetched[i], preferred_element_type=jnp.float32
        )
    count = tokens // row_blocks
    for spot, piece in enumerate(piece_order(row_blocks)):
        rows = projected[pl.ds(pl.multiple_of((block_index ^ piece) * count, count), count), :]
        ref, spot = (kept_ref, spot) if 2 * spot < row_blocks else (sent_ref, spot - row_blocks // 2)
        ref[spot * count : (spot + 1) * count, :] = rows.astype(ref.dtype)


def attend_call(lens, place, counts, queries, arrived, out_weight, held, blocks, all_open):
    tokens = queries.shape[0]
    ep_count = len(arrived)
    model_width = out_weight.shape[1]
    heads = queries.shape[1] // HD
    keys = ep_count * (held + tokens)
    return pl.pallas_call(
        lambda *refs: attend_kernel(ep_count, held, tokens, blocks, all_open, *refs),
        out_shape=[
            jax.ShapeDtypeStruct((tokens // 2, model_width), jnp.float32),
            jax.ShapeDtypeStruct((tokens // 2, model_width), jnp.bfloat16),
        ],
        in_specs=[SCALARS] * 3 + [WHOLE] * (ep_count + 1) + [ANYWHERE],
        out_specs=[WHOLE] * 2,
        scratch_shapes=[
            pltpu.VMEM((min(ROWS, heads * tokens), ep_count * held), jnp.float32),
            pltpu.VMEM((tokens, model_width), jnp.float32),
            pltpu.VMEM((model_width // COLUMNS, heads * HD, COLUMNS), jnp.bfloat16),
            pltpu.SemaphoreType.DMA((model_width // COLUMNS,)),
        ],
        compiler_params=pltpu.CompilerParams(vmem_limit_bytes=VMEM_LIMIT),
        cost_estimate=pl.CostEstimate(
            flops=4 * heads * tokens * keys * HD + 2 * tokens * heads * HD * model_width,
            bytes_accessed=2 * heads * HD * model_width,
            transcendentals=heads * tokens * keys,
        ),
        name="attend",
    )(lens, place, counts, queries, *arrived, out_weight)


def expert_kernel(count, ep_count, blocks, weight_at, place, payload, *refs):
    row_refs = refs[:count]
    gate_up_hbm, down_hbm = refs[count : count + 2]
    kept_ref, sent_ref, gate_up, down_weight, gate_up_sem, down_sem = refs[-6:]
    chunks = gate_up.shape[0]
    first = []
    second = []
    for i in range(chunks):
        columns = pl.ds(i * COLUMNS, COLUMNS)
        first.append(
            pltpu.make_async_copy(
                gate_up_hbm.at[0, :, :, columns], gate_up.at[i], gate_up_sem.at[i]
            )
        )
        second.append(
            pltpu.make_async_copy(down_hbm.at[0, :, columns], down_weight.at[i], down_sem.at[i])
        )
    for fetch in first + second:
        fetch.start()
    tokens = 2 * kept_ref.shape[0]
    row_count = tokens // blocks

    parts = payload[weight_at:, :].astype(jnp.float32)
    part_row = lax.broadcasted_iota(jnp.int32, parts.shape, 0)
    chosen = (part_row % ep_count == place[0]) & (part_row < 3 * ep_count)
    by_token = jnp.sum(jnp.where(chosen, parts, 0.0), axis=0, keepdims=True)
    row = lax.broadcasted_iota(jnp.int32, (tokens, parts.shape[1]), 0)
    token = row % row_count
    for spot, piece in enumerate(piece_order(blocks)):
        token = token + jnp.where(row // row_count == spot, (place[1] ^ piece) * row_count, 0)
    here = lax.broadcasted_iota(jnp.int32, (tokens, parts.shape[1]), 1) == token
    row_weight = jnp.sum(jnp.where(here, by_token, 0.0), axis=1, keepdims=True)

    gate_part = up_part = 0.0
    for i in range(chunks):
        at = i * COLUMNS
        rows = jnp.concatenate([ref[:, at : at + COLUMNS] for ref in row_refs], axis=0)
        first[i].wait()
        gate_part += lax.dot_general(
            rows, gate_up[i, 0], TRANSPOSED, preferred_element_type=jnp.float32
        )
        up_part += lax.dot_general(
            rows, gate_up[i, 1], TRANSPOSED, preferred_element_type=jnp.float32
        )
    hidden = gate_part / (1.0 + jnp.exp(-gate_part)) * up_part
    hidden = (hidden * row_weight).astype(jnp.bfloat16)
    half = kept_ref.shape[0]
    for i in range(chunks):
        at = i * COLUMNS
        second[i].wait()
        out = jnp.dot(hidden, down_weight[i], preferred_element_type=jnp.float32)
        out = out.astype(jnp.bfloat16)
        kept_ref[:, at : at + COLUMNS] = out[:half]
        sent_ref[:, at : at + COLUMNS] = out[half:]


def expert_call(place, payload, have, gate_up, down_weight, after, ep_count, blocks, weight_at):
    if have[0].shape[0] % 16:
        have = [jnp.concatenate(have, axis=0)]
    tokens = sum(piece.shape[0] for piece in have)
    model_width = have[0].shape[1]
    hidden_units = down_weight.shape[1]
    half = jax.ShapeDtypeStruct((tokens // 2, model_width), jnp.bfloat16)
    return pl.pallas_call(
        lambda *refs: expert_kernel(len(have), ep_count, blocks, weight_at, *refs),
        out_shape=(half, half),
        in_specs=[SCALARS] + [WHOLE] * (len(have) + 1) + [ANYWHERE] * (len(after) + 2),
        out_specs=(WHOLE, WHOLE),
        scratch_shapes=[
            pltpu.VMEM((model_width // COLUMNS, 2, hidden_units, COLUMNS), jnp.bfloat16),
            pltpu.VMEM((model_width // COLUMNS, hidden_units, COLUMNS), jnp.bfloat16),
            pltpu.SemaphoreType.DMA((model_width // COLUMNS,)),
            pltpu.SemaphoreType.DMA((model_width // COLUMNS,)),
        ],
        compiler_params=pltpu.CompilerParams(vmem_limit_bytes=VMEM_LIMIT),
        cost_estimate=pl.CostEstimate(
            flops=6 * tokens * hidden_units * model_width,
            bytes_accessed=6 * hidden_units * model_width,
            transcendentals=tokens * hidden_units,
        ),
        name="experts",
    )(place, payload, *have, gate_up, down_weight, *after)


def local(
    queries,
    new_kv,
    cache_pool,
    hit_pages,
    span_lengths,
    out_weight,
    hidden_in,
    norm_gain,
    expert_ids,
    gate_weights,
    gate_up,
    down_weight,
    new_owner,
):
    tokens = queries.shape[0]
    model_width = hidden_in.shape[1]
    ep_count = lax.axis_size("ep")
    tp_count = lax.axis_size("tp")
    blocks = lax.axis_size("kv") * tp_count
    ep_index = lax.axis_index("ep")
    kv_index = lax.axis_index("kv")
    tp_index = lax.axis_index("tp")
    block_index = kv_index * tp_count + tp_index
    keyval_local = new_kv.shape[1]
    heads_local = queries.shape[1] // HD
    keyval_pick = block_index * heads_local // (HQ // KVH) - kv_index * keyval_local
    row_count = tokens // blocks
    pool_pages = cache_pool.shape[0]
    page_size = cache_pool.shape[1]
    held = HOLD_MOST * page_size

    hits = hit_pages.shape[0]
    owned_hits = hit_pages // pool_pages == ep_index
    earlier = jnp.arange(hits)[None, :] < jnp.arange(hits)[:, None]
    hit_rank = jnp.sum((earlier & owned_hits[None, :]).astype(jnp.int32), axis=1)
    hit_pick = owned_hits[None, :] & (
        hit_rank[None, :] == jnp.arange(HOLD_MOST, dtype=jnp.int32)[:, None]
    )
    local_page = jnp.sum(jnp.where(hit_pick, hit_pages[None, :] - ep_index * pool_pages, 0), axis=1)
    chosen = cache_pool.at[local_page].get(mode="promise_in_bounds")
    own_pages = lax.dynamic_index_in_dim(chosen, keyval_pick, 2, keepdims=False).reshape(held, 2 * HD)
    own_suffix = lax.dynamic_index_in_dim(new_kv, keyval_pick, 1, keepdims=False)

    by_expert = jnp.sum(
        jnp.where(
            expert_ids[:, :, None] == jnp.arange(ep_count, dtype=jnp.int32)[None, None, :],
            gate_weights[:, :, None],
            0.0,
        ),
        axis=1,
    )
    weight_part = jnp.concatenate(three_parts(by_expert.T), axis=0)
    weight_rows = weight_part.shape[0]
    weight_part = jnp.pad(
        weight_part, ((0, -weight_rows % WEIGHT_ROWS), (0, 2 * HD - weight_part.shape[1]))
    )
    payload = jnp.concatenate([own_pages, own_suffix, weight_part], axis=0)
    arrived = [payload]
    for step in range(1, ep_count):
        arrived.append(
            lax.ppermute(payload, "ep", [(i, i ^ step) for i in range(ep_count)])
        )
    sources = [ep_index ^ step for step in range(ep_count)]

    all_open = hits == HOLD_MOST * ep_count
    holder = hit_pages // pool_pages
    counts = jnp.sum(
        (holder[None, :] == jnp.stack(sources)[:, None]).astype(jnp.int32) * page_size, axis=1
    )
    if all_open:
        counts = jnp.zeros((1,), jnp.int32)
    place = jnp.stack([ep_index, block_index]).astype(jnp.int32)
    exchange = lambda value, bit: lax.ppermute(
        value, ("kv", "tp"), [(i, i ^ bit) for i in range(blocks)]
    )
    across = lambda value, step: lax.ppermute(
        value, "ep", [(i, i ^ step) for i in range(ep_count)]
    )
    bits = [1 << place for place in range(1, blocks.bit_length() - 1)]

    def scatter(kept, sent):
        got = exchange(sent, 1)
        gives = []
        for bit in reversed(bits):
            half = kept.shape[0] // 2
            give = kept[half:].astype(jnp.float32) + got[half:].astype(jnp.float32)
            gives.append(give.astype(jnp.bfloat16))
            kept = kept[:half].astype(jnp.float32) + got[:half].astype(jnp.float32)
            got = exchange(gives[-1], bit)
        return kept.astype(jnp.float32) + got.astype(jnp.float32), gives

    heads_out, _ = scatter(
        *attend_call(
            span_lengths, place, counts, queries, arrived, out_weight, held, blocks, all_open
        )
    )
    own_hidden = lax.dynamic_slice_in_dim(hidden_in, block_index * row_count, row_count, 0)
    residual = (own_hidden.astype(jnp.float32) + heads_out).astype(jnp.bfloat16)
    resid_wide = residual.astype(jnp.float32)
    normed = (
        resid_wide
        * lax.rsqrt(jnp.mean(resid_wide * resid_wide, axis=1, keepdims=True) + EPSILON)
        * norm_gain
    ).astype(jnp.bfloat16)

    own_most = 2 * (tokens // page_size)
    page_count = new_owner.shape[0]
    pages_here = tokens // page_size
    owned_pages = new_owner == ep_index
    page_ids = jnp.arange(page_count, dtype=jnp.int32)
    owner_rank = jnp.sum(
        ((page_ids[None, :] < page_ids[:, None]) & owned_pages[None, :]).astype(jnp.int32), axis=1
    )
    choose = owned_pages[None, :] & (
        owner_rank[None, :] == jnp.arange(own_most, dtype=jnp.int32)[:, None]
    )
    page_index = jnp.sum(jnp.where(choose, page_ids[None, :], 0), axis=1)
    has_page = jnp.any(choose, axis=1)
    suffix = jnp.concatenate([block[held : held + tokens] for block in arrived], axis=0)
    spot = (ep_index ^ (page_index // pages_here)) * pages_here + page_index % pages_here
    taken = suffix.reshape(page_count, page_size, 2 * HD).at[spot].get(mode="promise_in_bounds")
    slot_in_span = (page_index % pages_here)[:, None] * page_size + jnp.arange(page_size)[None, :]
    kept = has_page[:, None] & (slot_in_span < span_lengths[page_index // pages_here][:, None])
    head_pages = jnp.where(kept[:, :, None], taken, jnp.zeros((), jnp.bfloat16))

    order = [0] + list(range(ep_count - 1, 0, -1))
    given = []
    finished = []

    def experts_of(step, piece, turn):
        have = [piece]
        for bit in bits + [1]:
            have += [exchange(part, bit) for part in have]
        after = given[turn - 2 : turn - 1] if turn >= 2 else []
        after = after + (finished[turn - 3 : turn - 2] if turn >= 3 else [])
        return expert_call(
            place,
            arrived[step],
            have,
            gate_up,
            down_weight,
            after,
            ep_count,
            blocks,
            held + tokens,
        )

    kept, sent = experts_of(0, normed, 0)
    sent, head_pages, *crossed = lax.optimization_barrier(
        [sent, head_pages] + [across(normed, step) for step in order[1:]]
    )
    mixture = resid_wide
    for turn, step in enumerate(order):
        if turn > 0:
            kept, sent = experts_of(step, crossed[turn - 1], turn)
        own, gives = scatter(kept, sent)
        own = own.astype(jnp.bfloat16)
        given.append(gives[0] if gives else own)
        finished.append(own)
        if step > 0:
            own = across(own, step)
        mixture = mixture + own.astype(jnp.float32)
    own_slots = block_index * row_count + jnp.arange(row_count, dtype=jnp.int32)
    rows_filled = own_slots < span_lengths[ep_index]
    layer_out = jnp.where(rows_filled[:, None], mixture, 0.0).astype(jnp.bfloat16)

    if keyval_local == 1:
        decode_pages = head_pages[:, :, None, :]
    else:
        other = lax.ppermute(head_pages, "tp", [(i, i ^ 1) for i in range(tp_count)])
        first = tp_index == 0
        decode_pages = jnp.stack(
            [jnp.where(first, head_pages, other), jnp.where(first, other, head_pages)], axis=2
        )
    return (layer_out, decode_pages)


def solution(mesh):
    placed = (
        P(("groups", "ep"), ("kv", "tp")),
        P(("groups", "ep"), "kv", None),
        P(("groups", "ep"), None, "kv", None),
        P("groups"),
        P("groups"),
        P(("kv", "tp"), None),
        P(("groups", "ep"), None),
        P(),
        P(("groups", "ep"), None),
        P(("groups", "ep"), None),
        P("ep", None, ("kv", "tp"), None),
        P("ep", ("kv", "tp"), None),
        P("groups"),
    )
    return jax.shard_map(
        local,
        mesh=mesh,
        in_specs=placed,
        out_specs=(P(("groups", "ep", "kv", "tp"), None), P(("groups", "ep"), None, "kv", None)),
        check_vma=False,
    )
```

```python
import math

import jax
import jax.numpy as jnp
from jax import lax
from jax.experimental import pallas as pl
from jax.experimental.pallas import tpu as pltpu
from jax.sharding import PartitionSpec as P

HD = 128
HQ = 32
KVH = 4
HOLD_MOST = 16
WEIGHT_ROWS = 16

MASKED = -1e30
EPSILON = 1e-06


def three_parts(wide):
    high = lax.reduce_precision(wide, 8, 7)
    rest = wide - high
    middle = lax.reduce_precision(rest, 8, 7)
    low = rest - middle
    return [part.astype(jnp.bfloat16) for part in (high, middle, low)]


def piece_order(blocks):
    order = [0]
    bit = 2
    while bit < blocks:
        order += [piece ^ bit for piece in order]
        bit *= 2
    return order + [piece ^ 1 for piece in order]


TRANSPOSED = (((1,), (1,)), ((), ()))
WHOLE = pl.BlockSpec(memory_space=pltpu.VMEM)
ANYWHERE = pl.BlockSpec(memory_space=pl.ANY)
SCALARS = pl.BlockSpec(memory_space=pltpu.SMEM)
COLUMNS = 1024
ROWS = 256
VMEM_LIMIT = 16 * 2**20


def hold_kernel(*refs):
    count = (len(refs) - 2) // 2
    sources, held, sem = refs[:count], refs[count + 1 : -1], refs[-1]
    copies = [
        pltpu.make_async_copy(source, target, sem.at[i])
        for i, (source, target) in enumerate(zip(sources, held))
    ]
    for copy in copies:
        copy.start()
    for copy in copies:
        copy.wait()


def hold_call(arrays, after):
    size = sum(math.prod(array.shape) * 2 for array in arrays)
    return pl.pallas_call(
        hold_kernel,
        out_shape=[jax.ShapeDtypeStruct(array.shape, array.dtype) for array in arrays],
        in_specs=[ANYWHERE] * (len(arrays) + 1),
        out_specs=[WHOLE] * len(arrays),
        scratch_shapes=[pltpu.SemaphoreType.DMA((len(arrays),))],
        compiler_params=pltpu.CompilerParams(vmem_limit_bytes=VMEM_LIMIT),
        cost_estimate=pl.CostEstimate(flops=0, bytes_accessed=2 * size, transcendentals=0),
        name="hold",
    )(*arrays, after)


def attend_kernel(ep_count, held, tokens, row_blocks, all_open, lens, place, counts, queries, *refs):
    blocks = refs[:ep_count]
    out_weight = refs[ep_count]
    kept_ref, sent_ref = refs[ep_count + 1 : ep_count + 3]
    scores, projected = refs[ep_count + 3 :]
    heads = queries.shape[1] // HD
    ep_index = place[0]
    block_index = place[1]
    suffix = ep_count * tokens

    own_start = jnp.int32(0)
    for j in range(ep_count):
        own_start = own_start + jnp.where(j < ep_index, lens[j], 0)
    column = lax.broadcasted_iota(jnp.int32, (tokens, suffix), 1)
    slot = column % tokens
    query_position = own_start + lax.broadcasted_iota(jnp.int32, (tokens, suffix), 0)
    seen = jnp.zeros((tokens, suffix), jnp.int32)
    for step in range(ep_count):
        source = ep_index ^ step
        start = jnp.int32(0)
        for j in range(ep_count):
            start = start + jnp.where(j < source, lens[j], 0)
        last = jnp.minimum(query_position - start, lens[source] - 1)
        here = (column // tokens == step) & (slot <= last)
        seen = seen + here.astype(jnp.int32)
    bias = jnp.where(seen > 0, 0.0, MASKED)

    suffix_keys = jnp.concatenate([block[held : held + tokens, :HD] for block in blocks], axis=0)
    suffix_values = jnp.concatenate([block[held : held + tokens, HD:] for block in blocks], axis=0)
    scale = math.log2(math.e) / math.sqrt(HD)
    rows = min(ROWS, heads * tokens)
    together = rows // tokens
    attended = []
    for first in range(0, heads, together):
        grouped = jnp.concatenate(
            [queries[:, h * HD : (h + 1) * HD] for h in range(first, first + together)], axis=0
        )
        highest = None
        for step in range(ep_count):
            part = scale * lax.dot_general(
                grouped, blocks[step][:held, :HD], TRANSPOSED, preferred_element_type=jnp.float32
            )
            if not all_open:
                entry = lax.broadcasted_iota(jnp.int32, part.shape, 1)
                part = jnp.where(entry < counts[step], part, MASKED)
            scores[:, step * held : (step + 1) * held] = part
            top = jnp.max(part, axis=1, keepdims=True)
            highest = top if highest is None else jnp.maximum(highest, top)
        part = scale * lax.dot_general(
            grouped, suffix_keys, TRANSPOSED, preferred_element_type=jnp.float32
        )
        part = part + jnp.concatenate([bias] * together, axis=0)
        highest = jnp.maximum(highest, jnp.max(part, axis=1, keepdims=True))
        part = jnp.exp2(part - highest)
        total = jnp.sum(part, axis=1, keepdims=True)
        mixed = jnp.dot(
            part.astype(jnp.bfloat16), suffix_values, preferred_element_type=jnp.float32
        )
        for step in range(ep_count):
            part = jnp.exp2(scores[:, step * held : (step + 1) * held] - highest)
            total += jnp.sum(part, axis=1, keepdims=True)
            mixed += jnp.dot(
                part.astype(jnp.bfloat16),
                blocks[step][:held, HD:],
                preferred_element_type=jnp.float32,
            )
        mixed = (mixed / total).astype(jnp.bfloat16)
        attended += [mixed[h * tokens : (h + 1) * tokens] for h in range(together)]
    attended = jnp.concatenate(attended, axis=1)
    for at in range(0, out_weight.shape[1], COLUMNS):
        projected[:, at : at + COLUMNS] = jnp.dot(
            attended, out_weight[:, at : at + COLUMNS], preferred_element_type=jnp.float32
        )
    count = tokens // row_blocks
    for spot, piece in enumerate(piece_order(row_blocks)):
        rows = projected[pl.ds(pl.multiple_of((block_index ^ piece) * count, count), count), :]
        ref, spot = (kept_ref, spot) if 2 * spot < row_blocks else (sent_ref, spot - row_blocks // 2)
        ref[spot * count : (spot + 1) * count, :] = rows.astype(ref.dtype)


def attend_call(lens, place, counts, queries, arrived, out_weight, held, blocks, all_open):
    tokens = queries.shape[0]
    ep_count = len(arrived)
    model_width = out_weight.shape[1]
    heads = queries.shape[1] // HD
    keys = ep_count * (held + tokens)
    return pl.pallas_call(
        lambda *refs: attend_kernel(ep_count, held, tokens, blocks, all_open, *refs),
        out_shape=[
            jax.ShapeDtypeStruct((tokens // 2, model_width), jnp.float32),
            jax.ShapeDtypeStruct((tokens // 2, model_width), jnp.bfloat16),
        ],
        in_specs=[SCALARS] * 3 + [WHOLE] * (ep_count + 2),
        out_specs=[WHOLE] * 2,
        scratch_shapes=[
            pltpu.VMEM((min(ROWS, heads * tokens), ep_count * held), jnp.float32),
            pltpu.VMEM((tokens, model_width), jnp.float32),
        ],
        compiler_params=pltpu.CompilerParams(vmem_limit_bytes=VMEM_LIMIT),
        cost_estimate=pl.CostEstimate(
            flops=4 * heads * tokens * keys * HD + 2 * tokens * heads * HD * model_width,
            bytes_accessed=2 * heads * HD * model_width,
            transcendentals=heads * tokens * keys,
        ),
        name="attend",
    )(lens, place, counts, queries, *arrived, out_weight)


def expert_kernel(count, ep_count, blocks, weight_at, place, payload, *refs):
    row_refs = refs[:count]
    gate_up, down_weight = refs[count : count + 2]
    kept_ref, sent_ref = refs[-2:]
    tokens = 2 * kept_ref.shape[0]
    row_count = tokens // blocks

    parts = payload[weight_at:, :].astype(jnp.float32)
    part_row = lax.broadcasted_iota(jnp.int32, parts.shape, 0)
    chosen = (part_row % ep_count == place[0]) & (part_row < 3 * ep_count)
    by_token = jnp.sum(jnp.where(chosen, parts, 0.0), axis=0, keepdims=True)
    row = lax.broadcasted_iota(jnp.int32, (tokens, parts.shape[1]), 0)
    token = row % row_count
    for spot, piece in enumerate(piece_order(blocks)):
        token = token + jnp.where(row // row_count == spot, (place[1] ^ piece) * row_count, 0)
    here = lax.broadcasted_iota(jnp.int32, (tokens, parts.shape[1]), 1) == token
    row_weight = jnp.sum(jnp.where(here, by_token, 0.0), axis=1, keepdims=True)

    gate_part = up_part = 0.0
    for at in range(0, kept_ref.shape[1], COLUMNS):
        rows = jnp.concatenate([ref[:, at : at + COLUMNS] for ref in row_refs], axis=0)
        gate_part += lax.dot_general(
            rows, gate_up[0, 0, :, at : at + COLUMNS], TRANSPOSED, preferred_element_type=jnp.float32
        )
        up_part += lax.dot_general(
            rows, gate_up[0, 1, :, at : at + COLUMNS], TRANSPOSED, preferred_element_type=jnp.float32
        )
    hidden = gate_part / (1.0 + jnp.exp(-gate_part)) * up_part
    hidden = (hidden * row_weight).astype(jnp.bfloat16)
    half = kept_ref.shape[0]
    for at in range(0, kept_ref.shape[1], COLUMNS):
        out = jnp.dot(
            hidden, down_weight[0, :, at : at + COLUMNS], preferred_element_type=jnp.float32
        ).astype(jnp.bfloat16)
        kept_ref[:, at : at + COLUMNS] = out[:half]
        sent_ref[:, at : at + COLUMNS] = out[half:]


def expert_call(place, payload, have, gate_up, down_weight, after, ep_count, blocks, weight_at):
    if have[0].shape[0] % 16:
        have = [jnp.concatenate(have, axis=0)]
    tokens = sum(piece.shape[0] for piece in have)
    model_width = have[0].shape[1]
    hidden_units = down_weight.shape[1]
    half = jax.ShapeDtypeStruct((tokens // 2, model_width), jnp.bfloat16)
    return pl.pallas_call(
        lambda *refs: expert_kernel(len(have), ep_count, blocks, weight_at, *refs),
        out_shape=(half, half),
        in_specs=[SCALARS] + [WHOLE] * (len(have) + 3) + [ANYWHERE] * len(after),
        out_specs=(WHOLE, WHOLE),
        compiler_params=pltpu.CompilerParams(vmem_limit_bytes=VMEM_LIMIT),
        cost_estimate=pl.CostEstimate(
            flops=6 * tokens * hidden_units * model_width,
            bytes_accessed=6 * hidden_units * model_width,
            transcendentals=tokens * hidden_units,
        ),
        name="experts",
    )(place, payload, *have, gate_up, down_weight, *after)


def local(
    queries,
    new_kv,
    cache_pool,
    hit_pages,
    span_lengths,
    out_weight,
    hidden_in,
    norm_gain,
    expert_ids,
    gate_weights,
    gate_up,
    down_weight,
    new_owner,
):
    tokens = queries.shape[0]
    model_width = hidden_in.shape[1]
    ep_count = lax.axis_size("ep")
    tp_count = lax.axis_size("tp")
    blocks = lax.axis_size("kv") * tp_count
    ep_index = lax.axis_index("ep")
    kv_index = lax.axis_index("kv")
    tp_index = lax.axis_index("tp")
    block_index = kv_index * tp_count + tp_index
    keyval_local = new_kv.shape[1]
    heads_local = queries.shape[1] // HD
    keyval_pick = block_index * heads_local // (HQ // KVH) - kv_index * keyval_local
    row_count = tokens // blocks
    pool_pages = cache_pool.shape[0]
    page_size = cache_pool.shape[1]
    held = HOLD_MOST * page_size

    hits = hit_pages.shape[0]
    owned_hits = hit_pages // pool_pages == ep_index
    earlier = jnp.arange(hits)[None, :] < jnp.arange(hits)[:, None]
    hit_rank = jnp.sum((earlier & owned_hits[None, :]).astype(jnp.int32), axis=1)
    hit_pick = owned_hits[None, :] & (
        hit_rank[None, :] == jnp.arange(HOLD_MOST, dtype=jnp.int32)[:, None]
    )
    local_page = jnp.sum(jnp.where(hit_pick, hit_pages[None, :] - ep_index * pool_pages, 0), axis=1)
    chosen = cache_pool.at[local_page].get(mode="promise_in_bounds")
    own_pages = lax.dynamic_index_in_dim(chosen, keyval_pick, 2, keepdims=False).reshape(held, 2 * HD)
    own_suffix = lax.dynamic_index_in_dim(new_kv, keyval_pick, 1, keepdims=False)

    by_expert = jnp.sum(
        jnp.where(
            expert_ids[:, :, None] == jnp.arange(ep_count, dtype=jnp.int32)[None, None, :],
            gate_weights[:, :, None],
            0.0,
        ),
        axis=1,
    )
    weight_part = jnp.concatenate(three_parts(by_expert.T), axis=0)
    weight_rows = weight_part.shape[0]
    weight_part = jnp.pad(
        weight_part, ((0, -weight_rows % WEIGHT_ROWS), (0, 2 * HD - weight_part.shape[1]))
    )
    payload = jnp.concatenate([own_pages, own_suffix, weight_part], axis=0)
    arrived = [payload]
    for step in range(1, ep_count):
        arrived.append(
            lax.ppermute(payload, "ep", [(i, i ^ step) for i in range(ep_count)])
        )
    sources = [ep_index ^ step for step in range(ep_count)]

    held_out = hold_call([out_weight], payload)[0]
    all_open = hits == HOLD_MOST * ep_count
    holder = hit_pages // pool_pages
    counts = jnp.sum(
        (holder[None, :] == jnp.stack(sources)[:, None]).astype(jnp.int32) * page_size, axis=1
    )
    if all_open:
        counts = jnp.zeros((1,), jnp.int32)
    place = jnp.stack([ep_index, block_index]).astype(jnp.int32)
    exchange = lambda value, bit: lax.ppermute(
        value, ("kv", "tp"), [(i, i ^ bit) for i in range(blocks)]
    )
    across = lambda value, step: lax.ppermute(
        value, "ep", [(i, i ^ step) for i in range(ep_count)]
    )
    bits = [1 << place for place in range(1, blocks.bit_length() - 1)]

    def scatter(kept, sent):
        got = exchange(sent, 1)
        gives = []
        for bit in reversed(bits):
            half = kept.shape[0] // 2
            give = kept[half:].astype(jnp.float32) + got[half:].astype(jnp.float32)
            gives.append(give.astype(jnp.bfloat16))
            kept = kept[:half].astype(jnp.float32) + got[:half].astype(jnp.float32)
            got = exchange(gives[-1], bit)
        return kept.astype(jnp.float32) + got.astype(jnp.float32), gives

    heads_out, _ = scatter(
        *attend_call(
            span_lengths, place, counts, queries, arrived, held_out, held, blocks, all_open
        )
    )
    own_most = 2 * (tokens // page_size)
    page_count = new_owner.shape[0]
    pages_here = tokens // page_size
    owned_pages = new_owner == ep_index
    page_ids = jnp.arange(page_count, dtype=jnp.int32)
    owner_rank = jnp.sum(
        ((page_ids[None, :] < page_ids[:, None]) & owned_pages[None, :]).astype(jnp.int32), axis=1
    )
    choose = owned_pages[None, :] & (
        owner_rank[None, :] == jnp.arange(own_most, dtype=jnp.int32)[:, None]
    )
    page_index = jnp.sum(jnp.where(choose, page_ids[None, :], 0), axis=1)
    has_page = jnp.any(choose, axis=1)
    suffix = jnp.concatenate([block[held : held + tokens] for block in arrived], axis=0)
    spot = (ep_index ^ (page_index // pages_here)) * pages_here + page_index % pages_here
    taken = suffix.reshape(page_count, page_size, 2 * HD).at[spot].get(mode="promise_in_bounds")
    slot_in_span = (page_index % pages_here)[:, None] * page_size + jnp.arange(page_size)[None, :]
    kept = has_page[:, None] & (slot_in_span < span_lengths[page_index // pages_here][:, None])
    head_pages = jnp.where(kept[:, :, None], taken, jnp.zeros((), jnp.bfloat16))
    heads_out, head_pages = lax.optimization_barrier([heads_out, head_pages])

    own_hidden = lax.dynamic_slice_in_dim(hidden_in, block_index * row_count, row_count, 0)
    residual = (own_hidden.astype(jnp.float32) + heads_out).astype(jnp.bfloat16)
    resid_wide = residual.astype(jnp.float32)
    normed = (
        resid_wide
        * lax.rsqrt(jnp.mean(resid_wide * resid_wide, axis=1, keepdims=True) + EPSILON)
        * norm_gain
    ).astype(jnp.bfloat16)

    order = list(range(ep_count - 1, -1, -1))
    crossed = lax.optimization_barrier([across(normed, step) for step in order[:-1]])
    held_gate_up, held_down = hold_call([gate_up, down_weight], crossed[0])
    given = []
    finished = []
    mixture = resid_wide
    for turn, step in enumerate(order):
        have = [crossed[turn] if step > 0 else normed]
        for bit in bits + [1]:
            have += [exchange(part, bit) for part in have]
        after = given[turn - 2 : turn - 1] if turn >= 2 else []
        after = after + (finished[turn - 3 : turn - 2] if turn >= 3 else [])
        kept, sent = expert_call(
            place,
            arrived[step],
            have,
            held_gate_up,
            held_down,
            after,
            ep_count,
            blocks,
            held + tokens,
        )
        own, gives = scatter(kept, sent)
        own = own.astype(jnp.bfloat16)
        given.append(gives[0] if gives else own)
        finished.append(own)
        if step > 0:
            own = across(own, step)
        mixture = mixture + own.astype(jnp.float32)
    own_slots = block_index * row_count + jnp.arange(row_count, dtype=jnp.int32)
    rows_filled = own_slots < span_lengths[ep_index]
    layer_out = jnp.where(rows_filled[:, None], mixture, 0.0).astype(jnp.bfloat16)

    if keyval_local == 1:
        decode_pages = head_pages[:, :, None, :]
    else:
        other = lax.ppermute(head_pages, "tp", [(i, i ^ 1) for i in range(tp_count)])
        first = tp_index == 0
        decode_pages = jnp.stack(
            [jnp.where(first, head_pages, other), jnp.where(first, other, head_pages)], axis=2
        )
    return (layer_out, decode_pages)


def solution(mesh):
    placed = (
        P(("groups", "ep"), ("kv", "tp")),
        P(("groups", "ep"), "kv", None),
        P(("groups", "ep"), None, "kv", None),
        P("groups"),
        P("groups"),
        P(("kv", "tp"), None),
        P(("groups", "ep"), None),
        P(),
        P(("groups", "ep"), None),
        P(("groups", "ep"), None),
        P("ep", None, ("kv", "tp"), None),
        P("ep", ("kv", "tp"), None),
        P("groups"),
    )
    return jax.shard_map(
        local,
        mesh=mesh,
        in_specs=placed,
        out_specs=(P(("groups", "ep", "kv", "tp"), None), P(("groups", "ep"), None, "kv", None)),
        check_vma=False,
    )
```

```python
import math

import jax
import jax.numpy as jnp
from jax import lax
from jax.experimental import pallas as pl
from jax.experimental.pallas import tpu as pltpu
from jax.sharding import PartitionSpec as P

HD = 128
HQ = 32
KVH = 4
HOLD_MOST = 16
WEIGHT_ROWS = 16

MASKED = -1e30
EPSILON = 1e-06


def three_parts(wide):
    high = lax.reduce_precision(wide, 8, 7)
    rest = wide - high
    middle = lax.reduce_precision(rest, 8, 7)
    low = rest - middle
    return [part.astype(jnp.bfloat16) for part in (high, middle, low)]


def piece_order(blocks):
    order = [0]
    bit = 2
    while bit < blocks:
        order += [piece ^ bit for piece in order]
        bit *= 2
    return order + [piece ^ 1 for piece in order]


TRANSPOSED = (((1,), (1,)), ((), ()))
WHOLE = pl.BlockSpec(memory_space=pltpu.VMEM)
ANYWHERE = pl.BlockSpec(memory_space=pl.ANY)
SCALARS = pl.BlockSpec(memory_space=pltpu.SMEM)
COLUMNS = 1024
ROWS = 256
VMEM_LIMIT = 16 * 2**20


def hold_kernel(count, *refs):
    sources, held, token, sem = refs[:count], refs[-2 - count : -2], refs[-2], refs[-1]
    token[...] = jnp.zeros_like(token)
    copies = [
        pltpu.make_async_copy(source, target, sem.at[i])
        for i, (source, target) in enumerate(zip(sources, held))
    ]
    for copy in copies:
        copy.start()
    for copy in copies:
        copy.wait()


def hold_call(arrays, *after):
    size = sum(math.prod(array.shape) * 2 for array in arrays)
    return pl.pallas_call(
        lambda *refs: hold_kernel(len(arrays), *refs),
        out_shape=[jax.ShapeDtypeStruct(array.shape, array.dtype) for array in arrays]
        + [jax.ShapeDtypeStruct((8, 128), jnp.float32)],
        in_specs=[ANYWHERE] * (len(arrays) + len(after)),
        out_specs=[WHOLE] * (len(arrays) + 1),
        scratch_shapes=[pltpu.SemaphoreType.DMA((len(arrays),))],
        compiler_params=pltpu.CompilerParams(vmem_limit_bytes=VMEM_LIMIT),
        cost_estimate=pl.CostEstimate(flops=0, bytes_accessed=2 * size, transcendentals=0),
        name="hold",
    )(*arrays, *after)


def attend_kernel(ep_count, held, tokens, row_blocks, all_open, lens, place, counts, owners, queries, *refs):
    blocks = refs[:ep_count]
    out_weight = refs[ep_count]
    kept_ref, sent_ref, pages_ref = refs[ep_count + 1 : ep_count + 4]
    scores, projected, ranks = refs[ep_count + 4 :]
    heads = queries.shape[1] // HD
    ep_index = place[0]
    block_index = place[1]
    suffix = ep_count * tokens

    page_count = owners.shape[0]
    pages_here = page_count // ep_count
    page_size = tokens // pages_here

    def rank_of(page, earlier):
        ranks[page] = earlier
        return earlier + (owners[page] == ep_index).astype(jnp.int32)

    lax.fori_loop(0, page_count, rank_of, jnp.int32(0))
    pages_ref[...] = jnp.zeros_like(pages_ref)
    for step in range(ep_count):
        source = ep_index ^ step
        for k in range(pages_here):
            page = source * pages_here + k

            @pl.when(owners[page] == ep_index)
            def _(step=step, source=source, k=k, page=page):
                first = held + k * page_size
                entries = blocks[step][first : first + page_size, :]
                row = lax.broadcasted_iota(jnp.int32, entries.shape, 0) + k * page_size
                entries = jnp.where(row < lens[source], entries.astype(jnp.float32), 0.0)
                at = pl.multiple_of(ranks[page] * page_size, page_size)
                pages_ref[pl.ds(at, page_size), :] = entries.astype(jnp.bfloat16)

    own_start = jnp.int32(0)
    for j in range(ep_count):
        own_start = own_start + jnp.where(j < ep_index, lens[j], 0)
    column = lax.broadcasted_iota(jnp.int32, (tokens, suffix), 1)
    slot = column % tokens
    query_position = own_start + lax.broadcasted_iota(jnp.int32, (tokens, suffix), 0)
    seen = jnp.zeros((tokens, suffix), jnp.int32)
    for step in range(ep_count):
        source = ep_index ^ step
        start = jnp.int32(0)
        for j in range(ep_count):
            start = start + jnp.where(j < source, lens[j], 0)
        last = jnp.minimum(query_position - start, lens[source] - 1)
        here = (column // tokens == step) & (slot <= last)
        seen = seen + here.astype(jnp.int32)
    bias = jnp.where(seen > 0, 0.0, MASKED)

    suffix_keys = jnp.concatenate([block[held : held + tokens, :HD] for block in blocks], axis=0)
    suffix_values = jnp.concatenate([block[held : held + tokens, HD:] for block in blocks], axis=0)
    scale = math.log2(math.e) / math.sqrt(HD)
    rows = min(ROWS, heads * tokens)
    together = rows // tokens
    attended = []
    for first in range(0, heads, together):
        grouped = jnp.concatenate(
            [queries[:, h * HD : (h + 1) * HD] for h in range(first, first + together)], axis=0
        )
        highest = None
        for step in range(ep_count):
            part = scale * lax.dot_general(
                grouped, blocks[step][:held, :HD], TRANSPOSED, preferred_element_type=jnp.float32
            )
            if not all_open:
                entry = lax.broadcasted_iota(jnp.int32, part.shape, 1)
                part = jnp.where(entry < counts[step], part, MASKED)
            scores[:, step * held : (step + 1) * held] = part
            top = jnp.max(part, axis=1, keepdims=True)
            highest = top if highest is None else jnp.maximum(highest, top)
        part = scale * lax.dot_general(
            grouped, suffix_keys, TRANSPOSED, preferred_element_type=jnp.float32
        )
        part = part + jnp.concatenate([bias] * together, axis=0)
        highest = jnp.maximum(highest, jnp.max(part, axis=1, keepdims=True))
        part = jnp.exp2(part - highest)
        total = jnp.sum(part, axis=1, keepdims=True)
        mixed = jnp.dot(
            part.astype(jnp.bfloat16), suffix_values, preferred_element_type=jnp.float32
        )
        for step in range(ep_count):
            part = jnp.exp2(scores[:, step * held : (step + 1) * held] - highest)
            total += jnp.sum(part, axis=1, keepdims=True)
            mixed += jnp.dot(
                part.astype(jnp.bfloat16),
                blocks[step][:held, HD:],
                preferred_element_type=jnp.float32,
            )
        mixed = (mixed / total).astype(jnp.bfloat16)
        attended += [mixed[h * tokens : (h + 1) * tokens] for h in range(together)]
    attended = jnp.concatenate(attended, axis=1)
    for at in range(0, out_weight.shape[1], COLUMNS):
        projected[:, at : at + COLUMNS] = jnp.dot(
            attended, out_weight[:, at : at + COLUMNS], preferred_element_type=jnp.float32
        )
    count = tokens // row_blocks
    for spot, piece in enumerate(piece_order(row_blocks)):
        rows = projected[pl.ds(pl.multiple_of((block_index ^ piece) * count, count), count), :]
        ref, spot = (kept_ref, spot) if 2 * spot < row_blocks else (sent_ref, spot - row_blocks // 2)
        ref[spot * count : (spot + 1) * count, :] = rows.astype(ref.dtype)


def attend_call(
    lens, place, counts, owners, queries, arrived, out_weight, held, blocks, own_most, all_open
):
    tokens = queries.shape[0]
    ep_count = len(arrived)
    model_width = out_weight.shape[1]
    heads = queries.shape[1] // HD
    keys = ep_count * (held + tokens)
    page_size = tokens * ep_count // owners.shape[0]
    return pl.pallas_call(
        lambda *refs: attend_kernel(ep_count, held, tokens, blocks, all_open, *refs),
        out_shape=[
            jax.ShapeDtypeStruct((tokens // 2, model_width), jnp.float32),
            jax.ShapeDtypeStruct((tokens // 2, model_width), jnp.bfloat16),
            jax.ShapeDtypeStruct((own_most * page_size, 2 * HD), jnp.bfloat16),
        ],
        in_specs=[SCALARS] * 4 + [WHOLE] * (ep_count + 2),
        out_specs=[WHOLE] * 3,
        scratch_shapes=[
            pltpu.VMEM((min(ROWS, heads * tokens), ep_count * held), jnp.float32),
            pltpu.VMEM((tokens, model_width), jnp.float32),
            pltpu.SMEM((owners.shape[0],), jnp.int32),
        ],
        compiler_params=pltpu.CompilerParams(vmem_limit_bytes=VMEM_LIMIT),
        cost_estimate=pl.CostEstimate(
            flops=4 * heads * tokens * keys * HD + 2 * tokens * heads * HD * model_width,
            bytes_accessed=2 * heads * HD * model_width,
            transcendentals=heads * tokens * keys,
        ),
        name="attend",
    )(lens, place, counts, owners, queries, *arrived, out_weight)


def expert_kernel(count, ep_count, blocks, weight_at, place, payload, *refs):
    row_refs = refs[:count]
    gate_up, down_weight = refs[count : count + 2]
    kept_ref, sent_ref = refs[-2:]
    tokens = 2 * kept_ref.shape[0]
    row_count = tokens // blocks

    parts = payload[weight_at:, :].astype(jnp.float32)
    part_row = lax.broadcasted_iota(jnp.int32, parts.shape, 0)
    chosen = (part_row % ep_count == place[0]) & (part_row < 3 * ep_count)
    by_token = jnp.sum(jnp.where(chosen, parts, 0.0), axis=0, keepdims=True)
    row = lax.broadcasted_iota(jnp.int32, (tokens, parts.shape[1]), 0)
    token = row % row_count
    for spot, piece in enumerate(piece_order(blocks)):
        token = token + jnp.where(row // row_count == spot, (place[1] ^ piece) * row_count, 0)
    here = lax.broadcasted_iota(jnp.int32, (tokens, parts.shape[1]), 1) == token
    row_weight = jnp.sum(jnp.where(here, by_token, 0.0), axis=1, keepdims=True)

    gate_part = up_part = 0.0
    for at in range(0, kept_ref.shape[1], COLUMNS):
        rows = jnp.concatenate([ref[:, at : at + COLUMNS] for ref in row_refs], axis=0)
        gate_part += lax.dot_general(
            rows, gate_up[0, 0, :, at : at + COLUMNS], TRANSPOSED, preferred_element_type=jnp.float32
        )
        up_part += lax.dot_general(
            rows, gate_up[0, 1, :, at : at + COLUMNS], TRANSPOSED, preferred_element_type=jnp.float32
        )
    hidden = gate_part / (1.0 + jnp.exp(-gate_part)) * up_part
    hidden = (hidden * row_weight).astype(jnp.bfloat16)
    half = kept_ref.shape[0]
    for at in range(0, kept_ref.shape[1], COLUMNS):
        out = jnp.dot(
            hidden, down_weight[0, :, at : at + COLUMNS], preferred_element_type=jnp.float32
        ).astype(jnp.bfloat16)
        kept_ref[:, at : at + COLUMNS] = out[:half]
        sent_ref[:, at : at + COLUMNS] = out[half:]


def expert_call(place, payload, have, gate_up, down_weight, after, ep_count, blocks, weight_at):
    if have[0].shape[0] % 16:
        have = [jnp.concatenate(have, axis=0)]
    tokens = sum(piece.shape[0] for piece in have)
    model_width = have[0].shape[1]
    hidden_units = down_weight.shape[1]
    half = jax.ShapeDtypeStruct((tokens // 2, model_width), jnp.bfloat16)
    return pl.pallas_call(
        lambda *refs: expert_kernel(len(have), ep_count, blocks, weight_at, *refs),
        out_shape=(half, half),
        in_specs=[SCALARS] + [WHOLE] * (len(have) + 3) + [ANYWHERE] * len(after),
        out_specs=(WHOLE, WHOLE),
        compiler_params=pltpu.CompilerParams(vmem_limit_bytes=VMEM_LIMIT),
        cost_estimate=pl.CostEstimate(
            flops=6 * tokens * hidden_units * model_width,
            bytes_accessed=6 * hidden_units * model_width,
            transcendentals=tokens * hidden_units,
        ),
        name="experts",
    )(place, payload, *have, gate_up, down_weight, *after)


def local(
    queries,
    new_kv,
    cache_pool,
    hit_pages,
    span_lengths,
    out_weight,
    hidden_in,
    norm_gain,
    expert_ids,
    gate_weights,
    gate_up,
    down_weight,
    new_owner,
):
    tokens = queries.shape[0]
    model_width = hidden_in.shape[1]
    ep_count = lax.axis_size("ep")
    tp_count = lax.axis_size("tp")
    blocks = lax.axis_size("kv") * tp_count
    ep_index = lax.axis_index("ep")
    kv_index = lax.axis_index("kv")
    tp_index = lax.axis_index("tp")
    block_index = kv_index * tp_count + tp_index
    keyval_local = new_kv.shape[1]
    heads_local = queries.shape[1] // HD
    keyval_pick = block_index * heads_local // (HQ // KVH) - kv_index * keyval_local
    row_count = tokens // blocks
    pool_pages = cache_pool.shape[0]
    page_size = cache_pool.shape[1]
    held = HOLD_MOST * page_size

    hits = hit_pages.shape[0]
    owned_hits = hit_pages // pool_pages == ep_index
    earlier = jnp.arange(hits)[None, :] < jnp.arange(hits)[:, None]
    hit_rank = jnp.sum((earlier & owned_hits[None, :]).astype(jnp.int32), axis=1)
    hit_pick = owned_hits[None, :] & (
        hit_rank[None, :] == jnp.arange(HOLD_MOST, dtype=jnp.int32)[:, None]
    )
    local_page = jnp.sum(jnp.where(hit_pick, hit_pages[None, :] - ep_index * pool_pages, 0), axis=1)
    chosen = cache_pool.at[local_page].get(mode="promise_in_bounds")
    own_pages = lax.dynamic_index_in_dim(chosen, keyval_pick, 2, keepdims=False).reshape(held, 2 * HD)
    own_suffix = lax.dynamic_index_in_dim(new_kv, keyval_pick, 1, keepdims=False)

    by_expert = jnp.sum(
        jnp.where(
            expert_ids[:, :, None] == jnp.arange(ep_count, dtype=jnp.int32)[None, None, :],
            gate_weights[:, :, None],
            0.0,
        ),
        axis=1,
    )
    weight_part = jnp.concatenate(three_parts(by_expert.T), axis=0)
    weight_rows = weight_part.shape[0]
    weight_part = jnp.pad(
        weight_part, ((0, -weight_rows % WEIGHT_ROWS), (0, 2 * HD - weight_part.shape[1]))
    )
    payload = jnp.concatenate([own_pages, own_suffix, weight_part], axis=0)
    arrived = [payload]
    for step in range(1, ep_count):
        arrived.append(
            lax.ppermute(payload, "ep", [(i, i ^ step) for i in range(ep_count)])
        )
    sources = [ep_index ^ step for step in range(ep_count)]

    all_open = hits == HOLD_MOST * ep_count
    holder = hit_pages // pool_pages
    counts = jnp.sum(
        (holder[None, :] == jnp.stack(sources)[:, None]).astype(jnp.int32) * page_size, axis=1
    )
    if all_open:
        counts = jnp.zeros((1,), jnp.int32)
    place = jnp.stack([ep_index, block_index]).astype(jnp.int32)
    exchange = lambda value, bit: lax.ppermute(
        value, ("kv", "tp"), [(i, i ^ bit) for i in range(blocks)]
    )
    across = lambda value, step: lax.ppermute(
        value, "ep", [(i, i ^ step) for i in range(ep_count)]
    )
    bits = [1 << place for place in range(1, blocks.bit_length() - 1)]

    def scatter(kept, sent):
        got = exchange(sent, 1)
        gives = []
        for bit in reversed(bits):
            half = kept.shape[0] // 2
            give = kept[half:].astype(jnp.float32) + got[half:].astype(jnp.float32)
            gives.append(give.astype(jnp.bfloat16))
            kept = kept[:half].astype(jnp.float32) + got[:half].astype(jnp.float32)
            got = exchange(gives[-1], bit)
        return kept.astype(jnp.float32) + got.astype(jnp.float32), gives

    own_most = 2 * (tokens // page_size)
    own_slots = block_index * row_count + jnp.arange(row_count, dtype=jnp.int32)
    rows_filled = own_slots < span_lengths[ep_index]
    held_out = hold_call([out_weight], payload, place, rows_filled.astype(jnp.int32))[0]
    kept, sent, head_pages = attend_call(
        span_lengths,
        place,
        counts,
        new_owner,
        queries,
        arrived,
        held_out,
        held,
        blocks,
        own_most,
        all_open,
    )
    head_pages = head_pages.reshape(own_most, page_size, 2 * HD)
    heads_out, _ = scatter(kept, sent)
    own_hidden = lax.dynamic_slice_in_dim(hidden_in, block_index * row_count, row_count, 0)
    residual = (own_hidden.astype(jnp.float32) + heads_out).astype(jnp.bfloat16)
    resid_wide = residual.astype(jnp.float32)
    normed = (
        resid_wide
        * lax.rsqrt(jnp.mean(resid_wide * resid_wide, axis=1, keepdims=True) + EPSILON)
        * norm_gain
    ).astype(jnp.bfloat16)

    order = list(range(ep_count - 1, -1, -1))
    held_gate_up, held_down, token = hold_call([gate_up, down_weight], normed)
    token, *crossed = lax.optimization_barrier(
        [token] + [across(normed, step) for step in order[:-1]]
    )
    given = []
    finished = []
    mixture = resid_wide
    for turn, step in enumerate(order):
        have = [crossed[turn] if step > 0 else normed]
        for bit in bits + [1]:
            have += [exchange(part, bit) for part in have]
        after = given[turn - 2 : turn - 1] if turn >= 2 else [token]
        after = after + (finished[turn - 3 : turn - 2] if turn >= 3 else [])
        kept, sent = expert_call(
            place,
            arrived[step],
            have,
            held_gate_up,
            held_down,
            after,
            ep_count,
            blocks,
            held + tokens,
        )
        own, gives = scatter(kept, sent)
        own = own.astype(jnp.bfloat16)
        given.append(gives[0] if gives else own)
        finished.append(own)
        if step > 0:
            own = across(own, step)
        mixture = mixture + own.astype(jnp.float32)
    layer_out = jnp.where(rows_filled[:, None], mixture, 0.0).astype(jnp.bfloat16)

    if keyval_local == 1:
        decode_pages = head_pages[:, :, None, :]
    else:
        other = lax.ppermute(head_pages, "tp", [(i, i ^ 1) for i in range(tp_count)])
        first = tp_index == 0
        decode_pages = jnp.stack(
            [jnp.where(first, head_pages, other), jnp.where(first, other, head_pages)], axis=2
        )
    return (layer_out, decode_pages)


def solution(mesh):
    placed = (
        P(("groups", "ep"), ("kv", "tp")),
        P(("groups", "ep"), "kv", None),
        P(("groups", "ep"), None, "kv", None),
        P("groups"),
        P("groups"),
        P(("kv", "tp"), None),
        P(("groups", "ep"), None),
        P(),
        P(("groups", "ep"), None),
        P(("groups", "ep"), None),
        P("ep", None, ("kv", "tp"), None),
        P("ep", ("kv", "tp"), None),
        P("groups"),
    )
    return jax.shard_map(
        local,
        mesh=mesh,
        in_specs=placed,
        out_specs=(P(("groups", "ep", "kv", "tp"), None), P(("groups", "ep"), None, "kv", None)),
        check_vma=False,
    )
```

```python
import math

import jax
import jax.numpy as jnp
from jax import lax
from jax.experimental import pallas as pl
from jax.experimental.pallas import tpu as pltpu
from jax.sharding import PartitionSpec as P

HD = 128
HQ = 32
KVH = 4
HOLD_MOST = 16
WEIGHT_ROWS = 16

MASKED = -1e30
EPSILON = 1e-06


def three_parts(wide):
    high = lax.reduce_precision(wide, 8, 7)
    rest = wide - high
    middle = lax.reduce_precision(rest, 8, 7)
    low = rest - middle
    return [part.astype(jnp.bfloat16) for part in (high, middle, low)]


def piece_order(blocks):
    order = [0]
    bit = 2
    while bit < blocks:
        order += [piece ^ bit for piece in order]
        bit *= 2
    return order + [piece ^ 1 for piece in order]


TRANSPOSED = (((1,), (1,)), ((), ()))
WHOLE = pl.BlockSpec(memory_space=pltpu.VMEM)
ANYWHERE = pl.BlockSpec(memory_space=pl.ANY)
SCALARS = pl.BlockSpec(memory_space=pltpu.SMEM)
COLUMNS = 1024
ROWS = 256
VMEM_LIMIT = 16 * 2**20
EXPERT_COST = pl.CostEstimate(flops=1024, bytes_accessed=1024, transcendentals=0)


def hold_kernel(count, *refs):
    sources, held, token, sem = refs[:count], refs[-2 - count : -2], refs[-2], refs[-1]
    token[...] = jnp.zeros_like(token)
    copies = [
        pltpu.make_async_copy(source, target, sem.at[i])
        for i, (source, target) in enumerate(zip(sources, held))
    ]
    for copy in copies:
        copy.start()
    for copy in copies:
        copy.wait()


def hold_call(arrays, *after):
    size = sum(math.prod(array.shape) * 2 for array in arrays)
    return pl.pallas_call(
        lambda *refs: hold_kernel(len(arrays), *refs),
        out_shape=[jax.ShapeDtypeStruct(array.shape, array.dtype) for array in arrays]
        + [jax.ShapeDtypeStruct((8, 128), jnp.float32)],
        in_specs=[ANYWHERE] * (len(arrays) + len(after)),
        out_specs=[WHOLE] * (len(arrays) + 1),
        scratch_shapes=[pltpu.SemaphoreType.DMA((len(arrays),))],
        compiler_params=pltpu.CompilerParams(vmem_limit_bytes=VMEM_LIMIT),
        cost_estimate=pl.CostEstimate(flops=0, bytes_accessed=2 * size, transcendentals=0),
        name="hold",
    )(*arrays, *after)


def first_reader(gate_up, down_weight, after, token):
    token[...] = (gate_up[0, 0, :16, :128] + down_weight[0, :16, :128]).astype(jnp.float32)


def first_reader_call(gate_up, down_weight, after):
    return pl.pallas_call(
        first_reader,
        out_shape=jax.ShapeDtypeStruct((16, 128), jnp.float32),
        in_specs=[WHOLE, WHOLE, ANYWHERE],
        out_specs=WHOLE,
        compiler_params=pltpu.CompilerParams(vmem_limit_bytes=VMEM_LIMIT),
        cost_estimate=EXPERT_COST,
        name="first_reader",
    )(gate_up, down_weight, after)


def attend_kernel(ep_count, held, tokens, row_blocks, all_open, lens, place, counts, owners, queries, *refs):
    blocks = refs[:ep_count]
    out_weight = refs[ep_count]
    kept_ref, sent_ref, pages_ref = refs[ep_count + 1 : ep_count + 4]
    scores, projected, ranks = refs[ep_count + 4 :]
    heads = queries.shape[1] // HD
    ep_index = place[0]
    block_index = place[1]
    suffix = ep_count * tokens

    page_count = owners.shape[0]
    pages_here = page_count // ep_count
    page_size = tokens // pages_here

    def rank_of(page, earlier):
        ranks[page] = earlier
        return earlier + (owners[page] == ep_index).astype(jnp.int32)

    lax.fori_loop(0, page_count, rank_of, jnp.int32(0))
    pages_ref[...] = jnp.zeros_like(pages_ref)
    for step in range(ep_count):
        source = ep_index ^ step
        for k in range(pages_here):
            page = source * pages_here + k

            @pl.when(owners[page] == ep_index)
            def _(step=step, source=source, k=k, page=page):
                first = held + k * page_size
                entries = blocks[step][first : first + page_size, :]
                row = lax.broadcasted_iota(jnp.int32, entries.shape, 0) + k * page_size
                entries = jnp.where(row < lens[source], entries.astype(jnp.float32), 0.0)
                at = pl.multiple_of(ranks[page] * page_size, page_size)
                pages_ref[pl.ds(at, page_size), :] = entries.astype(jnp.bfloat16)

    own_start = jnp.int32(0)
    for j in range(ep_count):
        own_start = own_start + jnp.where(j < ep_index, lens[j], 0)
    column = lax.broadcasted_iota(jnp.int32, (tokens, suffix), 1)
    slot = column % tokens
    query_position = own_start + lax.broadcasted_iota(jnp.int32, (tokens, suffix), 0)
    seen = jnp.zeros((tokens, suffix), jnp.int32)
    for step in range(ep_count):
        source = ep_index ^ step
        start = jnp.int32(0)
        for j in range(ep_count):
            start = start + jnp.where(j < source, lens[j], 0)
        last = jnp.minimum(query_position - start, lens[source] - 1)
        here = (column // tokens == step) & (slot <= last)
        seen = seen + here.astype(jnp.int32)
    bias = jnp.where(seen > 0, 0.0, MASKED)

    suffix_keys = jnp.concatenate([block[held : held + tokens, :HD] for block in blocks], axis=0)
    suffix_values = jnp.concatenate([block[held : held + tokens, HD:] for block in blocks], axis=0)
    scale = math.log2(math.e) / math.sqrt(HD)
    rows = min(ROWS, heads * tokens)
    together = rows // tokens
    attended = []
    for first in range(0, heads, together):
        grouped = jnp.concatenate(
            [queries[:, h * HD : (h + 1) * HD] for h in range(first, first + together)], axis=0
        )
        highest = None
        for step in range(ep_count):
            part = scale * lax.dot_general(
                grouped, blocks[step][:held, :HD], TRANSPOSED, preferred_element_type=jnp.float32
            )
            if not all_open:
                entry = lax.broadcasted_iota(jnp.int32, part.shape, 1)
                part = jnp.where(entry < counts[step], part, MASKED)
            scores[:, step * held : (step + 1) * held] = part
            top = jnp.max(part, axis=1, keepdims=True)
            highest = top if highest is None else jnp.maximum(highest, top)
        part = scale * lax.dot_general(
            grouped, suffix_keys, TRANSPOSED, preferred_element_type=jnp.float32
        )
        part = part + jnp.concatenate([bias] * together, axis=0)
        highest = jnp.maximum(highest, jnp.max(part, axis=1, keepdims=True))
        part = jnp.exp2(part - highest)
        total = jnp.sum(part, axis=1, keepdims=True)
        mixed = jnp.dot(
            part.astype(jnp.bfloat16), suffix_values, preferred_element_type=jnp.float32
        )
        for step in range(ep_count):
            part = jnp.exp2(scores[:, step * held : (step + 1) * held] - highest)
            total += jnp.sum(part, axis=1, keepdims=True)
            mixed += jnp.dot(
                part.astype(jnp.bfloat16),
                blocks[step][:held, HD:],
                preferred_element_type=jnp.float32,
            )
        mixed = (mixed / total).astype(jnp.bfloat16)
        attended += [mixed[h * tokens : (h + 1) * tokens] for h in range(together)]
    attended = jnp.concatenate(attended, axis=1)
    for at in range(0, out_weight.shape[1], COLUMNS):
        projected[:, at : at + COLUMNS] = jnp.dot(
            attended, out_weight[:, at : at + COLUMNS], preferred_element_type=jnp.float32
        )
    count = tokens // row_blocks
    for spot, piece in enumerate(piece_order(row_blocks)):
        rows = projected[pl.ds(pl.multiple_of((block_index ^ piece) * count, count), count), :]
        ref, spot = (kept_ref, spot) if 2 * spot < row_blocks else (sent_ref, spot - row_blocks // 2)
        ref[spot * count : (spot + 1) * count, :] = rows.astype(ref.dtype)


def attend_call(
    lens, place, counts, owners, queries, arrived, out_weight, held, blocks, own_most, all_open
):
    tokens = queries.shape[0]
    ep_count = len(arrived)
    model_width = out_weight.shape[1]
    heads = queries.shape[1] // HD
    keys = ep_count * (held + tokens)
    page_size = tokens * ep_count // owners.shape[0]
    return pl.pallas_call(
        lambda *refs: attend_kernel(ep_count, held, tokens, blocks, all_open, *refs),
        out_shape=[
            jax.ShapeDtypeStruct((tokens // 2, model_width), jnp.float32),
            jax.ShapeDtypeStruct((tokens // 2, model_width), jnp.bfloat16),
            jax.ShapeDtypeStruct((own_most * page_size, 2 * HD), jnp.bfloat16),
        ],
        in_specs=[SCALARS] * 4 + [WHOLE] * (ep_count + 2),
        out_specs=[WHOLE] * 3,
        scratch_shapes=[
            pltpu.VMEM((min(ROWS, heads * tokens), ep_count * held), jnp.float32),
            pltpu.VMEM((tokens, model_width), jnp.float32),
            pltpu.SMEM((owners.shape[0],), jnp.int32),
        ],
        compiler_params=pltpu.CompilerParams(vmem_limit_bytes=VMEM_LIMIT),
        cost_estimate=pl.CostEstimate(
            flops=4 * heads * tokens * keys * HD + 2 * tokens * heads * HD * model_width,
            bytes_accessed=2 * heads * HD * model_width,
            transcendentals=heads * tokens * keys,
        ),
        name="attend",
    )(lens, place, counts, owners, queries, *arrived, out_weight)


def expert_kernel(count, ep_count, blocks, weight_at, place, payload, *refs):
    row_refs = refs[:count]
    gate_up, down_weight = refs[count : count + 2]
    kept_ref, sent_ref = refs[-2:]
    tokens = 2 * kept_ref.shape[0]
    row_count = tokens // blocks

    parts = payload[weight_at:, :].astype(jnp.float32)
    part_row = lax.broadcasted_iota(jnp.int32, parts.shape, 0)
    chosen = (part_row % ep_count == place[0]) & (part_row < 3 * ep_count)
    by_token = jnp.sum(jnp.where(chosen, parts, 0.0), axis=0, keepdims=True)
    row = lax.broadcasted_iota(jnp.int32, (tokens, parts.shape[1]), 0)
    token = row % row_count
    for spot, piece in enumerate(piece_order(blocks)):
        token = token + jnp.where(row // row_count == spot, (place[1] ^ piece) * row_count, 0)
    here = lax.broadcasted_iota(jnp.int32, (tokens, parts.shape[1]), 1) == token
    row_weight = jnp.sum(jnp.where(here, by_token, 0.0), axis=1, keepdims=True)

    gate_part = up_part = 0.0
    for at in range(0, kept_ref.shape[1], COLUMNS):
        rows = jnp.concatenate([ref[:, at : at + COLUMNS] for ref in row_refs], axis=0)
        gate_part += lax.dot_general(
            rows, gate_up[0, 0, :, at : at + COLUMNS], TRANSPOSED, preferred_element_type=jnp.float32
        )
        up_part += lax.dot_general(
            rows, gate_up[0, 1, :, at : at + COLUMNS], TRANSPOSED, preferred_element_type=jnp.float32
        )
    hidden = gate_part / (1.0 + jnp.exp(-gate_part)) * up_part
    hidden = (hidden * row_weight).astype(jnp.bfloat16)
    half = kept_ref.shape[0]
    for at in range(0, kept_ref.shape[1], COLUMNS):
        out = jnp.dot(
            hidden, down_weight[0, :, at : at + COLUMNS], preferred_element_type=jnp.float32
        ).astype(jnp.bfloat16)
        kept_ref[:, at : at + COLUMNS] = out[:half]
        sent_ref[:, at : at + COLUMNS] = out[half:]


def expert_call(place, payload, have, gate_up, down_weight, after, ep_count, blocks, weight_at):
    if have[0].shape[0] % 16:
        have = [jnp.concatenate(have, axis=0)]
    tokens = sum(piece.shape[0] for piece in have)
    model_width = have[0].shape[1]
    hidden_units = down_weight.shape[1]
    half = jax.ShapeDtypeStruct((tokens // 2, model_width), jnp.bfloat16)
    return pl.pallas_call(
        lambda *refs: expert_kernel(len(have), ep_count, blocks, weight_at, *refs),
        out_shape=(half, half),
        in_specs=[SCALARS] + [WHOLE] * (len(have) + 3) + [ANYWHERE] * len(after),
        out_specs=(WHOLE, WHOLE),
        compiler_params=pltpu.CompilerParams(vmem_limit_bytes=VMEM_LIMIT),
        cost_estimate=EXPERT_COST,
        name="experts",
    )(place, payload, *have, gate_up, down_weight, *after)


def local(
    queries,
    new_kv,
    cache_pool,
    hit_pages,
    span_lengths,
    out_weight,
    hidden_in,
    norm_gain,
    expert_ids,
    gate_weights,
    gate_up,
    down_weight,
    new_owner,
):
    tokens = queries.shape[0]
    model_width = hidden_in.shape[1]
    ep_count = lax.axis_size("ep")
    tp_count = lax.axis_size("tp")
    blocks = lax.axis_size("kv") * tp_count
    ep_index = lax.axis_index("ep")
    kv_index = lax.axis_index("kv")
    tp_index = lax.axis_index("tp")
    block_index = kv_index * tp_count + tp_index
    keyval_local = new_kv.shape[1]
    heads_local = queries.shape[1] // HD
    keyval_pick = block_index * heads_local // (HQ // KVH) - kv_index * keyval_local
    row_count = tokens // blocks
    pool_pages = cache_pool.shape[0]
    page_size = cache_pool.shape[1]
    held = HOLD_MOST * page_size

    hits = hit_pages.shape[0]
    owned_hits = hit_pages // pool_pages == ep_index
    earlier = jnp.arange(hits)[None, :] < jnp.arange(hits)[:, None]
    hit_rank = jnp.sum((earlier & owned_hits[None, :]).astype(jnp.int32), axis=1)
    hit_pick = owned_hits[None, :] & (
        hit_rank[None, :] == jnp.arange(HOLD_MOST, dtype=jnp.int32)[:, None]
    )
    local_page = jnp.sum(jnp.where(hit_pick, hit_pages[None, :] - ep_index * pool_pages, 0), axis=1)
    chosen = cache_pool.at[local_page].get(mode="promise_in_bounds")
    own_pages = lax.dynamic_index_in_dim(chosen, keyval_pick, 2, keepdims=False).reshape(held, 2 * HD)
    own_suffix = lax.dynamic_index_in_dim(new_kv, keyval_pick, 1, keepdims=False)

    by_expert = jnp.sum(
        jnp.where(
            expert_ids[:, :, None] == jnp.arange(ep_count, dtype=jnp.int32)[None, None, :],
            gate_weights[:, :, None],
            0.0,
        ),
        axis=1,
    )
    weight_part = jnp.concatenate(three_parts(by_expert.T), axis=0)
    weight_rows = weight_part.shape[0]
    weight_part = jnp.pad(
        weight_part, ((0, -weight_rows % WEIGHT_ROWS), (0, 2 * HD - weight_part.shape[1]))
    )
    payload = jnp.concatenate([own_pages, own_suffix, weight_part], axis=0)
    arrived = [payload]
    for step in range(1, ep_count):
        arrived.append(
            lax.ppermute(payload, "ep", [(i, i ^ step) for i in range(ep_count)])
        )
    sources = [ep_index ^ step for step in range(ep_count)]

    all_open = hits == HOLD_MOST * ep_count
    holder = hit_pages // pool_pages
    counts = jnp.sum(
        (holder[None, :] == jnp.stack(sources)[:, None]).astype(jnp.int32) * page_size, axis=1
    )
    if all_open:
        counts = jnp.zeros((1,), jnp.int32)
    place = jnp.stack([ep_index, block_index]).astype(jnp.int32)
    exchange = lambda value, bit: lax.ppermute(
        value, ("kv", "tp"), [(i, i ^ bit) for i in range(blocks)]
    )
    across = lambda value, step: lax.ppermute(
        value, "ep", [(i, i ^ step) for i in range(ep_count)]
    )
    bits = [1 << place for place in range(1, blocks.bit_length() - 1)]

    def scatter(kept, sent):
        got = exchange(sent, 1)
        gives = []
        for bit in reversed(bits):
            half = kept.shape[0] // 2
            give = kept[half:].astype(jnp.float32) + got[half:].astype(jnp.float32)
            gives.append(give.astype(jnp.bfloat16))
            kept = kept[:half].astype(jnp.float32) + got[:half].astype(jnp.float32)
            got = exchange(gives[-1], bit)
        return kept.astype(jnp.float32) + got.astype(jnp.float32), gives

    own_most = 2 * (tokens // page_size)
    own_slots = block_index * row_count + jnp.arange(row_count, dtype=jnp.int32)
    rows_filled = own_slots < span_lengths[ep_index]
    held_out = hold_call([out_weight], payload, place, rows_filled.astype(jnp.int32))[0]
    kept, sent, head_pages = attend_call(
        span_lengths,
        place,
        counts,
        new_owner,
        queries,
        arrived,
        held_out,
        held,
        blocks,
        own_most,
        all_open,
    )
    head_pages = head_pages.reshape(own_most, page_size, 2 * HD)
    heads_out, _ = scatter(kept, sent)
    own_hidden = lax.dynamic_slice_in_dim(hidden_in, block_index * row_count, row_count, 0)
    residual = (own_hidden.astype(jnp.float32) + heads_out).astype(jnp.bfloat16)
    resid_wide = residual.astype(jnp.float32)
    normed = (
        resid_wide
        * lax.rsqrt(jnp.mean(resid_wide * resid_wide, axis=1, keepdims=True) + EPSILON)
        * norm_gain
    ).astype(jnp.bfloat16)

    order = list(range(ep_count - 1, -1, -1))
    token = first_reader_call(gate_up, down_weight, normed)
    token, *crossed = lax.optimization_barrier(
        [token] + [across(normed, step) for step in order[:-1]]
    )
    given = []
    finished = []
    mixture = resid_wide
    haves = []
    for piece in crossed + [normed]:
        have = [piece]
        for bit in bits + [1]:
            have += [exchange(part, bit) for part in have]
        haves.append(have)
    for turn, step in enumerate(order):
        after = given[turn - 2 : turn - 1] if turn >= 2 else [token]
        after = after + ([sent] if turn >= 1 else [])
        after = after + (finished[turn - 3 : turn - 2] if turn >= 3 else [])
        after = after + [have[1] for have in haves[turn + 1 : turn + 2]]
        kept, sent = expert_call(
            place,
            arrived[step],
            haves[turn],
            gate_up,
            down_weight,
            after,
            ep_count,
            blocks,
            held + tokens,
        )
        own, gives = scatter(kept, sent)
        own = own.astype(jnp.bfloat16)
        given.append(gives[0] if gives else own)
        finished.append(own)
        if step > 0:
            own = across(own, step)
        mixture = mixture + own.astype(jnp.float32)
    layer_out = jnp.where(rows_filled[:, None], mixture, 0.0).astype(jnp.bfloat16)

    if keyval_local == 1:
        decode_pages = head_pages[:, :, None, :]
    else:
        other = lax.ppermute(head_pages, "tp", [(i, i ^ 1) for i in range(tp_count)])
        first = tp_index == 0
        decode_pages = jnp.stack(
            [jnp.where(first, head_pages, other), jnp.where(first, other, head_pages)], axis=2
        )
    return (layer_out, decode_pages)


def solution(mesh):
    placed = (
        P(("groups", "ep"), ("kv", "tp")),
        P(("groups", "ep"), "kv", None),
        P(("groups", "ep"), None, "kv", None),
        P("groups"),
        P("groups"),
        P(("kv", "tp"), None),
        P(("groups", "ep"), None),
        P(),
        P(("groups", "ep"), None),
        P(("groups", "ep"), None),
        P("ep", None, ("kv", "tp"), None),
        P("ep", ("kv", "tp"), None),
        P("groups"),
    )
    return jax.shard_map(
        local,
        mesh=mesh,
        in_specs=placed,
        out_specs=(P(("groups", "ep", "kv", "tp"), None), P(("groups", "ep"), None, "kv", None)),
        check_vma=False,
    )
```

```python
import math

import jax
import jax.numpy as jnp
from jax import lax
from jax.experimental import pallas as pl
from jax.experimental.pallas import tpu as pltpu
from jax.sharding import PartitionSpec as P

HD = 128
HQ = 32
KVH = 4
HOLD_MOST = 16
WEIGHT_ROWS = 16

MASKED = -1e30
EPSILON = 1e-06


def three_parts(wide):
    high = lax.reduce_precision(wide, 8, 7)
    rest = wide - high
    middle = lax.reduce_precision(rest, 8, 7)
    low = rest - middle
    return [part.astype(jnp.bfloat16) for part in (high, middle, low)]


def piece_order(blocks):
    order = [0]
    bit = 2
    while bit < blocks:
        order += [piece ^ bit for piece in order]
        bit *= 2
    return order + [piece ^ 1 for piece in order]


TRANSPOSED = (((1,), (1,)), ((), ()))
WHOLE = pl.BlockSpec(memory_space=pltpu.VMEM)
ANYWHERE = pl.BlockSpec(memory_space=pl.ANY)
SCALARS = pl.BlockSpec(memory_space=pltpu.SMEM)
COLUMNS = 1024
ROWS = 256
VMEM_LIMIT = 16 * 2**20
EXPERT_COST = pl.CostEstimate(flops=1024, bytes_accessed=1024, transcendentals=0)


def hold_kernel(count, *refs):
    sources, held, token, sem = refs[:count], refs[-2 - count : -2], refs[-2], refs[-1]
    token[...] = jnp.zeros_like(token)
    copies = [
        pltpu.make_async_copy(source, target, sem.at[i])
        for i, (source, target) in enumerate(zip(sources, held))
    ]
    for copy in copies:
        copy.start()
    for copy in copies:
        copy.wait()


def hold_call(arrays, *after):
    size = sum(math.prod(array.shape) * 2 for array in arrays)
    return pl.pallas_call(
        lambda *refs: hold_kernel(len(arrays), *refs),
        out_shape=[jax.ShapeDtypeStruct(array.shape, array.dtype) for array in arrays]
        + [jax.ShapeDtypeStruct((8, 128), jnp.float32)],
        in_specs=[ANYWHERE] * (len(arrays) + len(after)),
        out_specs=[WHOLE] * (len(arrays) + 1),
        scratch_shapes=[pltpu.SemaphoreType.DMA((len(arrays),))],
        compiler_params=pltpu.CompilerParams(vmem_limit_bytes=VMEM_LIMIT),
        cost_estimate=pl.CostEstimate(flops=0, bytes_accessed=2 * size, transcendentals=0),
        name="hold",
    )(*arrays, *after)


def first_reader(gate_up, down_weight, after, token):
    token[...] = (gate_up[0, 0, :16, :128] + down_weight[0, :16, :128]).astype(jnp.float32)


def first_reader_call(gate_up, down_weight, after):
    return pl.pallas_call(
        first_reader,
        out_shape=jax.ShapeDtypeStruct((16, 128), jnp.float32),
        in_specs=[WHOLE, WHOLE, ANYWHERE],
        out_specs=WHOLE,
        compiler_params=pltpu.CompilerParams(vmem_limit_bytes=VMEM_LIMIT),
        cost_estimate=EXPERT_COST,
        name="first_reader",
    )(gate_up, down_weight, after)


def attend_kernel(ep_count, held, tokens, row_blocks, all_open, lens, place, counts, owners, queries, *refs):
    blocks = refs[:ep_count]
    out_weight = refs[ep_count]
    kept_ref, sent_ref, pages_ref = refs[ep_count + 1 : ep_count + 4]
    scores, projected, ranks = refs[ep_count + 4 :]
    heads = queries.shape[1] // HD
    ep_index = place[0]
    block_index = place[1]
    suffix = ep_count * tokens

    page_count = owners.shape[0]
    pages_here = page_count // ep_count
    page_size = tokens // pages_here

    def rank_of(page, earlier):
        ranks[page] = earlier
        return earlier + (owners[page] == ep_index).astype(jnp.int32)

    lax.fori_loop(0, page_count, rank_of, jnp.int32(0))
    pages_ref[...] = jnp.zeros_like(pages_ref)
    for step in range(ep_count):
        source = ep_index ^ step
        for k in range(pages_here):
            page = source * pages_here + k

            @pl.when(owners[page] == ep_index)
            def _(step=step, source=source, k=k, page=page):
                first = held + k * page_size
                entries = blocks[step][first : first + page_size, :]
                row = lax.broadcasted_iota(jnp.int32, entries.shape, 0) + k * page_size
                entries = jnp.where(row < lens[source], entries.astype(jnp.float32), 0.0)
                at = pl.multiple_of(ranks[page] * page_size, page_size)
                pages_ref[pl.ds(at, page_size), :] = entries.astype(jnp.bfloat16)

    own_start = jnp.int32(0)
    for j in range(ep_count):
        own_start = own_start + jnp.where(j < ep_index, lens[j], 0)
    column = lax.broadcasted_iota(jnp.int32, (tokens, suffix), 1)
    slot = column % tokens
    query_position = own_start + lax.broadcasted_iota(jnp.int32, (tokens, suffix), 0)
    seen = jnp.zeros((tokens, suffix), jnp.int32)
    for step in range(ep_count):
        source = ep_index ^ step
        start = jnp.int32(0)
        for j in range(ep_count):
            start = start + jnp.where(j < source, lens[j], 0)
        last = jnp.minimum(query_position - start, lens[source] - 1)
        here = (column // tokens == step) & (slot <= last)
        seen = seen + here.astype(jnp.int32)
    bias = jnp.where(seen > 0, 0.0, MASKED)

    suffix_keys = jnp.concatenate([block[held : held + tokens, :HD] for block in blocks], axis=0)
    suffix_values = jnp.concatenate([block[held : held + tokens, HD:] for block in blocks], axis=0)
    scale = math.log2(math.e) / math.sqrt(HD)
    rows = min(ROWS, heads * tokens)
    together = rows // tokens
    attended = []
    for first in range(0, heads, together):
        grouped = jnp.concatenate(
            [queries[:, h * HD : (h + 1) * HD] for h in range(first, first + together)], axis=0
        )
        highest = None
        for step in range(ep_count):
            part = scale * lax.dot_general(
                grouped, blocks[step][:held, :HD], TRANSPOSED, preferred_element_type=jnp.float32
            )
            if not all_open:
                entry = lax.broadcasted_iota(jnp.int32, part.shape, 1)
                part = jnp.where(entry < counts[step], part, MASKED)
            scores[:, step * held : (step + 1) * held] = part
            top = jnp.max(part, axis=1, keepdims=True)
            highest = top if highest is None else jnp.maximum(highest, top)
        part = scale * lax.dot_general(
            grouped, suffix_keys, TRANSPOSED, preferred_element_type=jnp.float32
        )
        part = part + jnp.concatenate([bias] * together, axis=0)
        highest = jnp.maximum(highest, jnp.max(part, axis=1, keepdims=True))
        part = jnp.exp2(part - highest)
        total = jnp.sum(part, axis=1, keepdims=True)
        mixed = jnp.dot(
            part.astype(jnp.bfloat16), suffix_values, preferred_element_type=jnp.float32
        )
        for step in range(ep_count):
            part = jnp.exp2(scores[:, step * held : (step + 1) * held] - highest)
            total += jnp.sum(part, axis=1, keepdims=True)
            mixed += jnp.dot(
                part.astype(jnp.bfloat16),
                blocks[step][:held, HD:],
                preferred_element_type=jnp.float32,
            )
        mixed = (mixed / total).astype(jnp.bfloat16)
        attended += [mixed[h * tokens : (h + 1) * tokens] for h in range(together)]
    attended = jnp.concatenate(attended, axis=1)
    for at in range(0, out_weight.shape[1], COLUMNS):
        projected[:, at : at + COLUMNS] = jnp.dot(
            attended, out_weight[:, at : at + COLUMNS], preferred_element_type=jnp.float32
        )
    count = tokens // row_blocks
    for spot, piece in enumerate(piece_order(row_blocks)):
        rows = projected[pl.ds(pl.multiple_of((block_index ^ piece) * count, count), count), :]
        ref, spot = (kept_ref, spot) if 2 * spot < row_blocks else (sent_ref, spot - row_blocks // 2)
        ref[spot * count : (spot + 1) * count, :] = rows.astype(ref.dtype)


def attend_call(
    lens, place, counts, owners, queries, arrived, out_weight, held, blocks, own_most, all_open
):
    tokens = queries.shape[0]
    ep_count = len(arrived)
    model_width = out_weight.shape[1]
    heads = queries.shape[1] // HD
    keys = ep_count * (held + tokens)
    page_size = tokens * ep_count // owners.shape[0]
    return pl.pallas_call(
        lambda *refs: attend_kernel(ep_count, held, tokens, blocks, all_open, *refs),
        out_shape=[
            jax.ShapeDtypeStruct((tokens // 2, model_width), jnp.float32),
            jax.ShapeDtypeStruct((tokens // 2, model_width), jnp.bfloat16),
            jax.ShapeDtypeStruct((own_most * page_size, 2 * HD), jnp.bfloat16),
        ],
        in_specs=[SCALARS] * 4 + [WHOLE] * (ep_count + 2),
        out_specs=[WHOLE] * 3,
        scratch_shapes=[
            pltpu.VMEM((min(ROWS, heads * tokens), ep_count * held), jnp.float32),
            pltpu.VMEM((tokens, model_width), jnp.float32),
            pltpu.SMEM((owners.shape[0],), jnp.int32),
        ],
        compiler_params=pltpu.CompilerParams(vmem_limit_bytes=VMEM_LIMIT),
        cost_estimate=pl.CostEstimate(
            flops=4 * heads * tokens * keys * HD + 2 * tokens * heads * HD * model_width,
            bytes_accessed=2 * heads * HD * model_width,
            transcendentals=heads * tokens * keys,
        ),
        name="attend",
    )(lens, place, counts, owners, queries, *arrived, out_weight)


def expert_kernel(count, ep_count, blocks, weight_at, place, payload, *refs):
    row_refs = refs[:count]
    gate_up, down_weight = refs[count : count + 2]
    kept_ref, sent_ref = refs[-2:]
    tokens = 2 * kept_ref.shape[0]
    row_count = tokens // blocks

    parts = payload[weight_at:, :].astype(jnp.float32)
    part_row = lax.broadcasted_iota(jnp.int32, parts.shape, 0)
    chosen = (part_row % ep_count == place[0]) & (part_row < 3 * ep_count)
    by_token = jnp.sum(jnp.where(chosen, parts, 0.0), axis=0, keepdims=True)
    row = lax.broadcasted_iota(jnp.int32, (tokens, parts.shape[1]), 0)
    token = row % row_count
    for spot, piece in enumerate(piece_order(blocks)):
        token = token + jnp.where(row // row_count == spot, (place[1] ^ piece) * row_count, 0)
    here = lax.broadcasted_iota(jnp.int32, (tokens, parts.shape[1]), 1) == token
    row_weight = jnp.sum(jnp.where(here, by_token, 0.0), axis=1, keepdims=True)

    gate_part = up_part = 0.0
    for at in range(0, kept_ref.shape[1], COLUMNS):
        rows = jnp.concatenate([ref[:, at : at + COLUMNS] for ref in row_refs], axis=0)
        gate_part += lax.dot_general(
            rows, gate_up[0, 0, :, at : at + COLUMNS], TRANSPOSED, preferred_element_type=jnp.float32
        )
        up_part += lax.dot_general(
            rows, gate_up[0, 1, :, at : at + COLUMNS], TRANSPOSED, preferred_element_type=jnp.float32
        )
    hidden = gate_part / (1.0 + jnp.exp(-gate_part)) * up_part
    hidden = (hidden * row_weight).astype(jnp.bfloat16)
    half = kept_ref.shape[0]
    for at in range(0, kept_ref.shape[1], COLUMNS):
        out = jnp.dot(
            hidden, down_weight[0, :, at : at + COLUMNS], preferred_element_type=jnp.float32
        ).astype(jnp.bfloat16)
        kept_ref[:, at : at + COLUMNS] = out[:half]
        sent_ref[:, at : at + COLUMNS] = out[half:]


def expert_call(place, payload, have, gate_up, down_weight, after, ep_count, blocks, weight_at):
    if have[0].shape[0] % 16:
        have = [jnp.concatenate(have, axis=0)]
    tokens = sum(piece.shape[0] for piece in have)
    model_width = have[0].shape[1]
    hidden_units = down_weight.shape[1]
    half = jax.ShapeDtypeStruct((tokens // 2, model_width), jnp.bfloat16)
    return pl.pallas_call(
        lambda *refs: expert_kernel(len(have), ep_count, blocks, weight_at, *refs),
        out_shape=(half, half),
        in_specs=[SCALARS] + [WHOLE] * (len(have) + 3) + [ANYWHERE] * len(after),
        out_specs=(WHOLE, WHOLE),
        compiler_params=pltpu.CompilerParams(vmem_limit_bytes=VMEM_LIMIT),
        cost_estimate=EXPERT_COST,
        name="experts",
    )(place, payload, *have, gate_up, down_weight, *after)


def local(
    queries,
    new_kv,
    cache_pool,
    hit_pages,
    span_lengths,
    out_weight,
    hidden_in,
    norm_gain,
    expert_ids,
    gate_weights,
    gate_up,
    down_weight,
    new_owner,
):
    tokens = queries.shape[0]
    model_width = hidden_in.shape[1]
    ep_count = lax.axis_size("ep")
    tp_count = lax.axis_size("tp")
    blocks = lax.axis_size("kv") * tp_count
    ep_index = lax.axis_index("ep")
    kv_index = lax.axis_index("kv")
    tp_index = lax.axis_index("tp")
    block_index = kv_index * tp_count + tp_index
    keyval_local = new_kv.shape[1]
    heads_local = queries.shape[1] // HD
    keyval_pick = block_index * heads_local // (HQ // KVH) - kv_index * keyval_local
    row_count = tokens // blocks
    pool_pages = cache_pool.shape[0]
    page_size = cache_pool.shape[1]
    held = HOLD_MOST * page_size

    hits = hit_pages.shape[0]
    owned_hits = hit_pages // pool_pages == ep_index
    earlier = jnp.arange(hits)[None, :] < jnp.arange(hits)[:, None]
    hit_rank = jnp.sum((earlier & owned_hits[None, :]).astype(jnp.int32), axis=1)
    hit_pick = owned_hits[None, :] & (
        hit_rank[None, :] == jnp.arange(HOLD_MOST, dtype=jnp.int32)[:, None]
    )
    local_page = jnp.sum(jnp.where(hit_pick, hit_pages[None, :] - ep_index * pool_pages, 0), axis=1)
    chosen = cache_pool.at[local_page].get(mode="promise_in_bounds")
    own_pages = lax.dynamic_index_in_dim(chosen, keyval_pick, 2, keepdims=False).reshape(held, 2 * HD)
    own_suffix = lax.dynamic_index_in_dim(new_kv, keyval_pick, 1, keepdims=False)

    by_expert = jnp.sum(
        jnp.where(
            expert_ids[:, :, None] == jnp.arange(ep_count, dtype=jnp.int32)[None, None, :],
            gate_weights[:, :, None],
            0.0,
        ),
        axis=1,
    )
    weight_part = jnp.concatenate(three_parts(by_expert.T), axis=0)
    weight_rows = weight_part.shape[0]
    weight_part = jnp.pad(
        weight_part, ((0, -weight_rows % WEIGHT_ROWS), (0, 2 * HD - weight_part.shape[1]))
    )
    payload = jnp.concatenate([own_pages, own_suffix, weight_part], axis=0)
    arrived = [payload]
    for step in range(1, ep_count):
        arrived.append(
            lax.ppermute(payload, "ep", [(i, i ^ step) for i in range(ep_count)])
        )
    sources = [ep_index ^ step for step in range(ep_count)]

    all_open = hits == HOLD_MOST * ep_count
    holder = hit_pages // pool_pages
    counts = jnp.sum(
        (holder[None, :] == jnp.stack(sources)[:, None]).astype(jnp.int32) * page_size, axis=1
    )
    if all_open:
        counts = jnp.zeros((1,), jnp.int32)
    place = jnp.stack([ep_index, block_index]).astype(jnp.int32)
    exchange = lambda value, bit: lax.ppermute(
        value, ("kv", "tp"), [(i, i ^ bit) for i in range(blocks)]
    )
    across = lambda value, step: lax.ppermute(
        value, "ep", [(i, i ^ step) for i in range(ep_count)]
    )
    bits = [1 << place for place in range(1, blocks.bit_length() - 1)]

    def scatter(kept, sent):
        got = exchange(sent, 1)
        gives = []
        for bit in reversed(bits):
            half = kept.shape[0] // 2
            give = kept[half:].astype(jnp.float32) + got[half:].astype(jnp.float32)
            gives.append(give.astype(jnp.bfloat16))
            kept = kept[:half].astype(jnp.float32) + got[:half].astype(jnp.float32)
            got = exchange(gives[-1], bit)
        return kept.astype(jnp.float32) + got.astype(jnp.float32), gives

    own_most = 2 * (tokens // page_size)
    own_slots = block_index * row_count + jnp.arange(row_count, dtype=jnp.int32)
    rows_filled = own_slots < span_lengths[ep_index]
    core = jnp.broadcast_to(tp_index.astype(jnp.int32), (1, 1, 2 * HD))
    core, row_mask = lax.optimization_barrier((core, rows_filled.astype(jnp.int32)))
    held_out, _ = hold_call([out_weight], payload, place, row_mask, core)
    kept, sent, head_pages = attend_call(
        span_lengths,
        place,
        counts,
        new_owner,
        queries,
        arrived,
        held_out,
        held,
        blocks,
        own_most,
        all_open,
    )
    head_pages = head_pages.reshape(own_most, page_size, 2 * HD)
    heads_out, _ = scatter(kept, sent)
    own_hidden = lax.dynamic_slice_in_dim(hidden_in, block_index * row_count, row_count, 0)
    residual = (own_hidden.astype(jnp.float32) + heads_out).astype(jnp.bfloat16)
    resid_wide = residual.astype(jnp.float32)
    normed = (
        resid_wide
        * lax.rsqrt(jnp.mean(resid_wide * resid_wide, axis=1, keepdims=True) + EPSILON)
        * norm_gain
    ).astype(jnp.bfloat16)

    order = [0] + list(range(ep_count - 1, 0, -1))

    def group_rows(piece):
        have = [piece]
        for bit in bits + [1]:
            have += [exchange(part, bit) for part in have]
        return have

    def experts_of(step, have, after):
        return expert_call(
            place,
            arrived[step],
            have,
            gate_up,
            down_weight,
            after,
            ep_count,
            blocks,
            held + tokens,
        )

    token = first_reader_call(gate_up, down_weight, normed)
    early = [exchange(normed, bit) for bit in bits + [1]]
    token, *crossed = lax.optimization_barrier(
        [token] + early + [across(normed, step) for step in order[1:]]
    )
    own_have = [normed]
    for bit, piece in zip(bits + [1], crossed):
        own_have += [piece] + [exchange(part, bit) for part in own_have[1:]]
    haves = [own_have] + [group_rows(piece) for piece in crossed[len(early) :]]
    given = []
    finished = []
    mixture = resid_wide
    for turn, step in enumerate(order):
        after = [sent] if turn >= 1 else [token]
        after = after + (given[turn - 2 : turn - 1] if turn >= 2 else [])
        after = after + (finished[turn - 3 : turn - 2] if turn >= 3 else [])
        after = after + [have[1] for have in haves[turn + 1 : turn + 2] if turn >= 1]
        kept, sent = experts_of(step, haves[turn], after)
        own, gives = scatter(kept, sent)
        own = own.astype(jnp.bfloat16)
        given.append(gives[0] if gives else own)
        finished.append(own)
        if step > 0:
            own = across(own, step)
        mixture = mixture + own.astype(jnp.float32)
    layer_out = jnp.where(row_mask[:, None] > 0, mixture, 0.0).astype(jnp.bfloat16)

    if keyval_local == 1:
        decode_pages = head_pages[:, :, None, :]
    else:
        other = lax.ppermute(head_pages, "tp", [(i, i ^ 1) for i in range(tp_count)])
        first = core == 0
        decode_pages = jnp.stack(
            [jnp.where(first, head_pages, other), jnp.where(first, other, head_pages)], axis=2
        )
    return (layer_out, decode_pages)


def solution(mesh):
    placed = (
        P(("groups", "ep"), ("kv", "tp")),
        P(("groups", "ep"), "kv", None),
        P(("groups", "ep"), None, "kv", None),
        P("groups"),
        P("groups"),
        P(("kv", "tp"), None),
        P(("groups", "ep"), None),
        P(),
        P(("groups", "ep"), None),
        P(("groups", "ep"), None),
        P("ep", None, ("kv", "tp"), None),
        P("ep", ("kv", "tp"), None),
        P("groups"),
    )
    return jax.shard_map(
        local,
        mesh=mesh,
        in_specs=placed,
        out_specs=(P(("groups", "ep", "kv", "tp"), None), P(("groups", "ep"), None, "kv", None)),
        check_vma=False,
    )
```

```python
import math

import jax
import jax.numpy as jnp
from jax import lax
from jax.experimental import pallas as pl
from jax.experimental.pallas import tpu as pltpu
from jax.sharding import PartitionSpec as P

HD = 128
HQ = 32
KVH = 4
HOLD_MOST = 16
WEIGHT_ROWS = 16

MASKED = -1e30
EPSILON = 1e-06


def three_parts(wide):
    high = lax.reduce_precision(wide, 8, 7)
    rest = wide - high
    middle = lax.reduce_precision(rest, 8, 7)
    low = rest - middle
    return [part.astype(jnp.bfloat16) for part in (high, middle, low)]


def piece_order(blocks):
    order = [0]
    bit = 2
    while bit < blocks:
        order += [piece ^ bit for piece in order]
        bit *= 2
    return order + [piece ^ 1 for piece in order]


TRANSPOSED = (((1,), (1,)), ((), ()))
WHOLE = pl.BlockSpec(memory_space=pltpu.VMEM)
ANYWHERE = pl.BlockSpec(memory_space=pl.ANY)
SCALARS = pl.BlockSpec(memory_space=pltpu.SMEM)
COLUMNS = 1024
ROWS = 256
VMEM_LIMIT = 16 * 2**20
EXPERT_COST = pl.CostEstimate(flops=1024, bytes_accessed=1024, transcendentals=0)


def hold_kernel(count, *refs):
    sources, held, token, sem = refs[:count], refs[-2 - count : -2], refs[-2], refs[-1]
    token[...] = jnp.zeros_like(token)
    copies = [
        pltpu.make_async_copy(source, target, sem.at[i])
        for i, (source, target) in enumerate(zip(sources, held))
    ]
    for copy in copies:
        copy.start()
    for copy in copies:
        copy.wait()


def hold_call(arrays, *after):
    size = sum(math.prod(array.shape) * 2 for array in arrays)
    return pl.pallas_call(
        lambda *refs: hold_kernel(len(arrays), *refs),
        out_shape=[jax.ShapeDtypeStruct(array.shape, array.dtype) for array in arrays]
        + [jax.ShapeDtypeStruct((8, 128), jnp.float32)],
        in_specs=[ANYWHERE] * (len(arrays) + len(after)),
        out_specs=[WHOLE] * (len(arrays) + 1),
        scratch_shapes=[pltpu.SemaphoreType.DMA((len(arrays),))],
        compiler_params=pltpu.CompilerParams(vmem_limit_bytes=VMEM_LIMIT),
        cost_estimate=pl.CostEstimate(flops=0, bytes_accessed=2 * size, transcendentals=0),
        name="hold",
    )(*arrays, *after)


def prepare_kernel(ep_count, blocks, weight_at, place, *refs):
    payloads = refs[:ep_count]
    gate_up_from, down_from, _, gate_up, down_weight, row_weights, sem = refs[ep_count:]
    copies = [
        pltpu.make_async_copy(gate_up_from, gate_up, sem.at[0]),
        pltpu.make_async_copy(down_from, down_weight, sem.at[1]),
    ]
    for copy in copies:
        copy.start()

    tokens = row_weights.shape[0] // ep_count
    row_count = tokens // blocks
    wide = (tokens, payloads[0].shape[1])
    row = lax.broadcasted_iota(jnp.int32, wide, 0)
    token = row % row_count
    for spot, piece in enumerate(piece_order(blocks)):
        token = token + jnp.where(row // row_count == spot, (place[1] ^ piece) * row_count, 0)
    here = lax.broadcasted_iota(jnp.int32, wide, 1) == token
    for step, payload in enumerate(payloads):
        parts = payload[weight_at:, :].astype(jnp.float32)
        part_row = lax.broadcasted_iota(jnp.int32, parts.shape, 0)
        chosen = (part_row % ep_count == place[0]) & (part_row < 3 * ep_count)
        by_token = jnp.sum(jnp.where(chosen, parts, 0.0), axis=0, keepdims=True)
        column = jnp.sum(jnp.where(here, by_token, 0.0), axis=1, keepdims=True)
        row_weights[step * tokens : (step + 1) * tokens, :] = jnp.broadcast_to(column, (tokens, HD))
    for copy in copies:
        copy.wait()


def prepare_call(place, arrived, gate_up, down_weight, after, blocks, tokens, weight_at):
    ep_count = len(arrived)
    return pl.pallas_call(
        lambda *refs: prepare_kernel(ep_count, blocks, weight_at, *refs),
        out_shape=[
            jax.ShapeDtypeStruct(gate_up.shape, gate_up.dtype),
            jax.ShapeDtypeStruct(down_weight.shape, down_weight.dtype),
            jax.ShapeDtypeStruct((ep_count * tokens, HD), jnp.float32),
        ],
        in_specs=[SCALARS] + [WHOLE] * ep_count + [ANYWHERE] * 3,
        out_specs=[WHOLE] * 3,
        scratch_shapes=[pltpu.SemaphoreType.DMA((2,))],
        compiler_params=pltpu.CompilerParams(vmem_limit_bytes=VMEM_LIMIT),
        cost_estimate=EXPERT_COST,
        name="prepare",
    )(place, *arrived, gate_up, down_weight, after)


def attend_kernel(ep_count, held, tokens, row_blocks, all_open, lens, place, counts, owners, queries, *refs):
    blocks = refs[:ep_count]
    out_weight = refs[ep_count]
    kept_ref, sent_ref, pages_ref = refs[ep_count + 1 : ep_count + 4]
    scores, projected, ranks = refs[ep_count + 4 :]
    heads = queries.shape[1] // HD
    ep_index = place[0]
    block_index = place[1]
    suffix = ep_count * tokens

    page_count = owners.shape[0]
    pages_here = page_count // ep_count
    page_size = tokens // pages_here

    def rank_of(page, earlier):
        ranks[page] = earlier
        return earlier + (owners[page] == ep_index).astype(jnp.int32)

    lax.fori_loop(0, page_count, rank_of, jnp.int32(0))
    pages_ref[...] = jnp.zeros_like(pages_ref)
    for step in range(ep_count):
        source = ep_index ^ step
        for k in range(pages_here):
            page = source * pages_here + k

            @pl.when(owners[page] == ep_index)
            def _(step=step, source=source, k=k, page=page):
                first = held + k * page_size
                entries = blocks[step][first : first + page_size, :]
                row = lax.broadcasted_iota(jnp.int32, entries.shape, 0) + k * page_size
                entries = jnp.where(row < lens[source], entries.astype(jnp.float32), 0.0)
                at = pl.multiple_of(ranks[page] * page_size, page_size)
                pages_ref[pl.ds(at, page_size), :] = entries.astype(jnp.bfloat16)

    own_start = jnp.int32(0)
    for j in range(ep_count):
        own_start = own_start + jnp.where(j < ep_index, lens[j], 0)
    column = lax.broadcasted_iota(jnp.int32, (tokens, suffix), 1)
    slot = column % tokens
    query_position = own_start + lax.broadcasted_iota(jnp.int32, (tokens, suffix), 0)
    seen = jnp.zeros((tokens, suffix), jnp.int32)
    for step in range(ep_count):
        source = ep_index ^ step
        start = jnp.int32(0)
        for j in range(ep_count):
            start = start + jnp.where(j < source, lens[j], 0)
        last = jnp.minimum(query_position - start, lens[source] - 1)
        here = (column // tokens == step) & (slot <= last)
        seen = seen + here.astype(jnp.int32)
    bias = jnp.where(seen > 0, 0.0, MASKED)

    suffix_keys = jnp.concatenate([block[held : held + tokens, :HD] for block in blocks], axis=0)
    suffix_values = jnp.concatenate([block[held : held + tokens, HD:] for block in blocks], axis=0)
    scale = math.log2(math.e) / math.sqrt(HD)
    rows = min(ROWS, heads * tokens)
    together = rows // tokens
    attended = []
    for first in range(0, heads, together):
        grouped = jnp.concatenate(
            [queries[:, h * HD : (h + 1) * HD] for h in range(first, first + together)], axis=0
        )
        highest = None
        for step in range(ep_count):
            part = scale * lax.dot_general(
                grouped, blocks[step][:held, :HD], TRANSPOSED, preferred_element_type=jnp.float32
            )
            if not all_open:
                entry = lax.broadcasted_iota(jnp.int32, part.shape, 1)
                part = jnp.where(entry < counts[step], part, MASKED)
            scores[:, step * held : (step + 1) * held] = part
            top = jnp.max(part, axis=1, keepdims=True)
            highest = top if highest is None else jnp.maximum(highest, top)
        part = scale * lax.dot_general(
            grouped, suffix_keys, TRANSPOSED, preferred_element_type=jnp.float32
        )
        part = part + jnp.concatenate([bias] * together, axis=0)
        highest = jnp.maximum(highest, jnp.max(part, axis=1, keepdims=True))
        part = jnp.exp2(part - highest)
        total = jnp.sum(part, axis=1, keepdims=True)
        mixed = jnp.dot(
            part.astype(jnp.bfloat16), suffix_values, preferred_element_type=jnp.float32
        )
        for step in range(ep_count):
            part = jnp.exp2(scores[:, step * held : (step + 1) * held] - highest)
            total += jnp.sum(part, axis=1, keepdims=True)
            mixed += jnp.dot(
                part.astype(jnp.bfloat16),
                blocks[step][:held, HD:],
                preferred_element_type=jnp.float32,
            )
        mixed = (mixed / total).astype(jnp.bfloat16)
        attended += [mixed[h * tokens : (h + 1) * tokens] for h in range(together)]
    attended = jnp.concatenate(attended, axis=1)
    for at in range(0, out_weight.shape[1], COLUMNS):
        projected[:, at : at + COLUMNS] = jnp.dot(
            attended, out_weight[:, at : at + COLUMNS], preferred_element_type=jnp.float32
        )
    count = tokens // row_blocks
    for spot, piece in enumerate(piece_order(row_blocks)):
        rows = projected[pl.ds(pl.multiple_of((block_index ^ piece) * count, count), count), :]
        ref, spot = (kept_ref, spot) if 2 * spot < row_blocks else (sent_ref, spot - row_blocks // 2)
        ref[spot * count : (spot + 1) * count, :] = rows.astype(ref.dtype)


def attend_call(
    lens, place, counts, owners, queries, arrived, out_weight, held, blocks, own_most, all_open
):
    tokens = queries.shape[0]
    ep_count = len(arrived)
    model_width = out_weight.shape[1]
    heads = queries.shape[1] // HD
    keys = ep_count * (held + tokens)
    page_size = tokens * ep_count // owners.shape[0]
    return pl.pallas_call(
        lambda *refs: attend_kernel(ep_count, held, tokens, blocks, all_open, *refs),
        out_shape=[
            jax.ShapeDtypeStruct((tokens // 2, model_width), jnp.float32),
            jax.ShapeDtypeStruct((tokens // 2, model_width), jnp.bfloat16),
            jax.ShapeDtypeStruct((own_most * page_size, 2 * HD), jnp.bfloat16),
        ],
        in_specs=[SCALARS] * 4 + [WHOLE] * (ep_count + 2),
        out_specs=[WHOLE] * 3,
        scratch_shapes=[
            pltpu.VMEM((min(ROWS, heads * tokens), ep_count * held), jnp.float32),
            pltpu.VMEM((tokens, model_width), jnp.float32),
            pltpu.SMEM((owners.shape[0],), jnp.int32),
        ],
        compiler_params=pltpu.CompilerParams(vmem_limit_bytes=VMEM_LIMIT),
        cost_estimate=pl.CostEstimate(
            flops=4 * heads * tokens * keys * HD + 2 * tokens * heads * HD * model_width,
            bytes_accessed=2 * heads * HD * model_width,
            transcendentals=heads * tokens * keys,
        ),
        name="attend",
    )(lens, place, counts, owners, queries, *arrived, out_weight)


def expert_kernel(count, step, row_weights, *refs):
    row_refs = refs[:count]
    gate_up, down_weight = refs[count : count + 2]
    kept_ref, sent_ref = refs[-2:]
    tokens = 2 * kept_ref.shape[0]
    row_weight = row_weights[step * tokens : (step + 1) * tokens, :1]
    gate_part = up_part = 0.0
    for at in range(0, kept_ref.shape[1], COLUMNS):
        rows = jnp.concatenate([ref[:, at : at + COLUMNS] for ref in row_refs], axis=0)
        gate_part += lax.dot_general(
            rows, gate_up[0, 0, :, at : at + COLUMNS], TRANSPOSED, preferred_element_type=jnp.float32
        )
        up_part += lax.dot_general(
            rows, gate_up[0, 1, :, at : at + COLUMNS], TRANSPOSED, preferred_element_type=jnp.float32
        )
    hidden = gate_part / (1.0 + jnp.exp(-gate_part)) * up_part
    hidden = (hidden * row_weight).astype(jnp.bfloat16)
    half = kept_ref.shape[0]
    for at in range(0, kept_ref.shape[1], COLUMNS):
        out = jnp.dot(
            hidden, down_weight[0, :, at : at + COLUMNS], preferred_element_type=jnp.float32
        ).astype(jnp.bfloat16)
        kept_ref[:, at : at + COLUMNS] = out[:half]
        sent_ref[:, at : at + COLUMNS] = out[half:]


def expert_call(step, row_weights, have, gate_up, down_weight, after):
    if have[0].shape[0] % 16:
        have = [jnp.concatenate(have, axis=0)]
    tokens = sum(piece.shape[0] for piece in have)
    model_width = have[0].shape[1]
    hidden_units = down_weight.shape[1]
    half = jax.ShapeDtypeStruct((tokens // 2, model_width), jnp.bfloat16)
    return pl.pallas_call(
        lambda *refs: expert_kernel(len(have), step, *refs),
        out_shape=(half, half),
        in_specs=[WHOLE] * (len(have) + 3) + [ANYWHERE] * len(after),
        out_specs=(WHOLE, WHOLE),
        compiler_params=pltpu.CompilerParams(vmem_limit_bytes=VMEM_LIMIT),
        cost_estimate=EXPERT_COST,
        name="experts",
    )(row_weights, *have, gate_up, down_weight, *after)


def local(
    queries,
    new_kv,
    cache_pool,
    hit_pages,
    span_lengths,
    out_weight,
    hidden_in,
    norm_gain,
    expert_ids,
    gate_weights,
    gate_up,
    down_weight,
    new_owner,
):
    tokens = queries.shape[0]
    model_width = hidden_in.shape[1]
    ep_count = lax.axis_size("ep")
    tp_count = lax.axis_size("tp")
    blocks = lax.axis_size("kv") * tp_count
    ep_index = lax.axis_index("ep")
    kv_index = lax.axis_index("kv")
    tp_index = lax.axis_index("tp")
    block_index = kv_index * tp_count + tp_index
    keyval_local = new_kv.shape[1]
    heads_local = queries.shape[1] // HD
    keyval_pick = block_index * heads_local // (HQ // KVH) - kv_index * keyval_local
    row_count = tokens // blocks
    pool_pages = cache_pool.shape[0]
    page_size = cache_pool.shape[1]
    held = HOLD_MOST * page_size

    hits = hit_pages.shape[0]
    owned_hits = hit_pages // pool_pages == ep_index
    earlier = jnp.arange(hits)[None, :] < jnp.arange(hits)[:, None]
    hit_rank = jnp.sum((earlier & owned_hits[None, :]).astype(jnp.int32), axis=1)
    hit_pick = owned_hits[None, :] & (
        hit_rank[None, :] == jnp.arange(HOLD_MOST, dtype=jnp.int32)[:, None]
    )
    local_page = jnp.sum(jnp.where(hit_pick, hit_pages[None, :] - ep_index * pool_pages, 0), axis=1)
    chosen = cache_pool.at[local_page].get(mode="promise_in_bounds")
    own_pages = lax.dynamic_index_in_dim(chosen, keyval_pick, 2, keepdims=False).reshape(held, 2 * HD)
    own_suffix = lax.dynamic_index_in_dim(new_kv, keyval_pick, 1, keepdims=False)

    by_expert = jnp.sum(
        jnp.where(
            expert_ids[:, :, None] == jnp.arange(ep_count, dtype=jnp.int32)[None, None, :],
            gate_weights[:, :, None],
            0.0,
        ),
        axis=1,
    )
    weight_part = jnp.concatenate(three_parts(by_expert.T), axis=0)
    weight_rows = weight_part.shape[0]
    weight_part = jnp.pad(
        weight_part, ((0, -weight_rows % WEIGHT_ROWS), (0, 2 * HD - weight_part.shape[1]))
    )
    payload = jnp.concatenate([own_pages, own_suffix, weight_part], axis=0)
    arrived = [payload]
    for step in range(1, ep_count):
        arrived.append(
            lax.ppermute(payload, "ep", [(i, i ^ step) for i in range(ep_count)])
        )
    sources = [ep_index ^ step for step in range(ep_count)]

    all_open = hits == HOLD_MOST * ep_count
    holder = hit_pages // pool_pages
    counts = jnp.sum(
        (holder[None, :] == jnp.stack(sources)[:, None]).astype(jnp.int32) * page_size, axis=1
    )
    if all_open:
        counts = jnp.zeros((1,), jnp.int32)
    place = jnp.stack([ep_index, block_index]).astype(jnp.int32)
    exchange = lambda value, bit: lax.ppermute(
        value, ("kv", "tp"), [(i, i ^ bit) for i in range(blocks)]
    )
    across = lambda value, step: lax.ppermute(
        value, "ep", [(i, i ^ step) for i in range(ep_count)]
    )
    bits = [1 << place for place in range(1, blocks.bit_length() - 1)]

    def scatter(kept, sent):
        got = exchange(sent, 1)
        gives = []
        for bit in reversed(bits):
            half = kept.shape[0] // 2
            give = kept[half:].astype(jnp.float32) + got[half:].astype(jnp.float32)
            gives.append(give.astype(jnp.bfloat16))
            kept = kept[:half].astype(jnp.float32) + got[:half].astype(jnp.float32)
            got = exchange(gives[-1], bit)
        return kept.astype(jnp.float32) + got.astype(jnp.float32), gives

    own_most = 2 * (tokens // page_size)
    own_slots = block_index * row_count + jnp.arange(row_count, dtype=jnp.int32)
    rows_filled = own_slots < span_lengths[ep_index]
    core = jnp.broadcast_to(tp_index.astype(jnp.int32), (1, 1, 2 * HD))
    core, row_mask = lax.optimization_barrier((core, rows_filled.astype(jnp.int32)))
    held_out, _ = hold_call([out_weight], payload, place, row_mask, core)
    kept, sent, head_pages = attend_call(
        span_lengths,
        place,
        counts,
        new_owner,
        queries,
        arrived,
        held_out,
        held,
        blocks,
        own_most,
        all_open,
    )
    head_pages = head_pages.reshape(own_most, page_size, 2 * HD)
    heads_out, _ = scatter(kept, sent)
    own_hidden = lax.dynamic_slice_in_dim(hidden_in, block_index * row_count, row_count, 0)
    residual = (own_hidden.astype(jnp.float32) + heads_out).astype(jnp.bfloat16)
    resid_wide = residual.astype(jnp.float32)
    normed = (
        resid_wide
        * lax.rsqrt(jnp.mean(resid_wide * resid_wide, axis=1, keepdims=True) + EPSILON)
        * norm_gain
    ).astype(jnp.bfloat16)

    order = list(range(ep_count - 1, -1, -1))

    def group_rows(piece):
        have = [piece]
        for bit in bits + [1]:
            have += [exchange(part, bit) for part in have]
        return have

    held_gate_up, held_down, row_weights = prepare_call(
        place, arrived, gate_up, down_weight, normed, blocks, tokens, held + tokens
    )
    crossed = [across(normed, step) for step in order[:-1]]
    early = [exchange(normed, bit) for bit in bits + [1]]
    row_weights, *crossed = lax.optimization_barrier([row_weights] + crossed + early)
    early = crossed[len(order) - 1 :]
    own_have = [normed]
    for bit, piece in zip(bits + [1], early):
        own_have += [piece] + [exchange(part, bit) for part in own_have[1:]]
    haves = [group_rows(piece) for piece in crossed[: len(order) - 1]] + [own_have]
    given = []
    finished = []
    mixture = resid_wide
    for turn, step in enumerate(order):
        after = [sent] if turn >= 1 else []
        after += given[turn - 2 : turn - 1] if turn >= 2 else []
        after += [have[1] for have in haves[turn + 1 : turn + 2]]
        if step == 0:
            after += given[turn - 1 : turn] + finished[max(turn - 3, 0) : turn - 1]
        kept, sent = expert_call(
            step, row_weights, haves[turn], held_gate_up, held_down, after
        )
        own, gives = scatter(kept, sent)
        own = own.astype(jnp.bfloat16)
        given.append(gives[0] if gives else own)
        finished.append(own)
        if step > 0:
            own = across(own, step)
        mixture = mixture + own.astype(jnp.float32)
    layer_out = jnp.where(row_mask[:, None] > 0, mixture, 0.0).astype(jnp.bfloat16)

    if keyval_local == 1:
        decode_pages = head_pages[:, :, None, :]
    else:
        other = lax.ppermute(head_pages, "tp", [(i, i ^ 1) for i in range(tp_count)])
        first = core == 0
        decode_pages = jnp.stack(
            [jnp.where(first, head_pages, other), jnp.where(first, other, head_pages)], axis=2
        )
    return (layer_out, decode_pages)


def solution(mesh):
    placed = (
        P(("groups", "ep"), ("kv", "tp")),
        P(("groups", "ep"), "kv", None),
        P(("groups", "ep"), None, "kv", None),
        P("groups"),
        P("groups"),
        P(("kv", "tp"), None),
        P(("groups", "ep"), None),
        P(),
        P(("groups", "ep"), None),
        P(("groups", "ep"), None),
        P("ep", None, ("kv", "tp"), None),
        P("ep", ("kv", "tp"), None),
        P("groups"),
    )
    return jax.shard_map(
        local,
        mesh=mesh,
        in_specs=placed,
        out_specs=(P(("groups", "ep", "kv", "tp"), None), P(("groups", "ep"), None, "kv", None)),
        check_vma=False,
    )
```

```python
import math

import jax
import jax.numpy as jnp
from jax import lax
from jax.experimental import pallas as pl
from jax.experimental.pallas import tpu as pltpu
from jax.sharding import PartitionSpec as P

HD = 128
HQ = 32
KVH = 4
HOLD_MOST = 16
WEIGHT_ROWS = 16

MASKED = -1e30
EPSILON = 1e-06


def three_parts(wide):
    high = lax.reduce_precision(wide, 8, 7)
    rest = wide - high
    middle = lax.reduce_precision(rest, 8, 7)
    low = rest - middle
    return [part.astype(jnp.bfloat16) for part in (high, middle, low)]


def piece_order(blocks):
    order = [0]
    bit = 2
    while bit < blocks:
        order += [piece ^ bit for piece in order]
        bit *= 2
    return order + [piece ^ 1 for piece in order]


TRANSPOSED = (((1,), (1,)), ((), ()))
WHOLE = pl.BlockSpec(memory_space=pltpu.VMEM)
ANYWHERE = pl.BlockSpec(memory_space=pl.ANY)
SCALARS = pl.BlockSpec(memory_space=pltpu.SMEM)
COLUMNS = 1024
ROWS = 256
VMEM_LIMIT = 16 * 2**20
EXPERT_COST = pl.CostEstimate(flops=1024, bytes_accessed=1024, transcendentals=0)


def hold_kernel(count, *refs):
    sources, held, token, sem = refs[:count], refs[-2 - count : -2], refs[-2], refs[-1]
    token[...] = jnp.zeros_like(token)
    copies = [
        pltpu.make_async_copy(source, target, sem.at[i])
        for i, (source, target) in enumerate(zip(sources, held))
    ]
    for copy in copies:
        copy.start()
    for copy in copies:
        copy.wait()


def hold_call(arrays, *after):
    size = sum(math.prod(array.shape) * 2 for array in arrays)
    return pl.pallas_call(
        lambda *refs: hold_kernel(len(arrays), *refs),
        out_shape=[jax.ShapeDtypeStruct(array.shape, array.dtype) for array in arrays]
        + [jax.ShapeDtypeStruct((8, 128), jnp.float32)],
        in_specs=[ANYWHERE] * (len(arrays) + len(after)),
        out_specs=[WHOLE] * (len(arrays) + 1),
        scratch_shapes=[pltpu.SemaphoreType.DMA((len(arrays),))],
        compiler_params=pltpu.CompilerParams(vmem_limit_bytes=VMEM_LIMIT),
        cost_estimate=pl.CostEstimate(flops=0, bytes_accessed=2 * size, transcendentals=0),
        name="hold",
    )(*arrays, *after)


def prepare_kernel(ep_count, blocks, weight_at, place, *refs):
    payloads = refs[:ep_count]
    row_weights = refs[-1]
    tokens = row_weights.shape[0] // ep_count
    row_count = tokens // blocks
    wide = (tokens, payloads[0].shape[1])
    row = lax.broadcasted_iota(jnp.int32, wide, 0)
    token = row % row_count
    for spot, piece in enumerate(piece_order(blocks)):
        token = token + jnp.where(row // row_count == spot, (place[1] ^ piece) * row_count, 0)
    here = lax.broadcasted_iota(jnp.int32, wide, 1) == token
    for step, payload in enumerate(payloads):
        parts = payload[weight_at:, :].astype(jnp.float32)
        part_row = lax.broadcasted_iota(jnp.int32, parts.shape, 0)
        chosen = (part_row % ep_count == place[0]) & (part_row < 3 * ep_count)
        by_token = jnp.sum(jnp.where(chosen, parts, 0.0), axis=0, keepdims=True)
        column = jnp.sum(jnp.where(here, by_token, 0.0), axis=1, keepdims=True)
        row_weights[step * tokens : (step + 1) * tokens, :] = jnp.broadcast_to(column, (tokens, HD))


def prepare_call(place, arrived, after, blocks, tokens, weight_at):
    ep_count = len(arrived)
    return pl.pallas_call(
        lambda *refs: prepare_kernel(ep_count, blocks, weight_at, *refs),
        out_shape=jax.ShapeDtypeStruct((ep_count * tokens, HD), jnp.float32),
        in_specs=[SCALARS] + [WHOLE] * ep_count + [ANYWHERE],
        out_specs=WHOLE,
        compiler_params=pltpu.CompilerParams(vmem_limit_bytes=VMEM_LIMIT),
        cost_estimate=EXPERT_COST,
        name="prepare",
    )(place, *arrived, after)


def attend_kernel(ep_count, held, tokens, row_blocks, all_open, lens, place, counts, owners, queries, *refs):
    blocks = refs[:ep_count]
    out_weight = refs[ep_count]
    kept_ref, sent_ref, pages_ref = refs[ep_count + 1 : ep_count + 4]
    scores, projected, ranks = refs[ep_count + 4 :]
    heads = queries.shape[1] // HD
    ep_index = place[0]
    block_index = place[1]
    suffix = ep_count * tokens

    page_count = owners.shape[0]
    pages_here = page_count // ep_count
    page_size = tokens // pages_here

    def rank_of(page, earlier):
        ranks[page] = earlier
        return earlier + (owners[page] == ep_index).astype(jnp.int32)

    lax.fori_loop(0, page_count, rank_of, jnp.int32(0))
    pages_ref[...] = jnp.zeros_like(pages_ref)
    for step in range(ep_count):
        source = ep_index ^ step
        for k in range(pages_here):
            page = source * pages_here + k

            @pl.when(owners[page] == ep_index)
            def _(step=step, source=source, k=k, page=page):
                first = held + k * page_size
                entries = blocks[step][first : first + page_size, :]
                row = lax.broadcasted_iota(jnp.int32, entries.shape, 0) + k * page_size
                entries = jnp.where(row < lens[source], entries.astype(jnp.float32), 0.0)
                at = pl.multiple_of(ranks[page] * page_size, page_size)
                pages_ref[pl.ds(at, page_size), :] = entries.astype(jnp.bfloat16)

    own_start = jnp.int32(0)
    for j in range(ep_count):
        own_start = own_start + jnp.where(j < ep_index, lens[j], 0)
    column = lax.broadcasted_iota(jnp.int32, (tokens, suffix), 1)
    slot = column % tokens
    query_position = own_start + lax.broadcasted_iota(jnp.int32, (tokens, suffix), 0)
    seen = jnp.zeros((tokens, suffix), jnp.int32)
    for step in range(ep_count):
        source = ep_index ^ step
        start = jnp.int32(0)
        for j in range(ep_count):
            start = start + jnp.where(j < source, lens[j], 0)
        last = jnp.minimum(query_position - start, lens[source] - 1)
        here = (column // tokens == step) & (slot <= last)
        seen = seen + here.astype(jnp.int32)
    bias = jnp.where(seen > 0, 0.0, MASKED)

    suffix_keys = jnp.concatenate([block[held : held + tokens, :HD] for block in blocks], axis=0)
    suffix_values = jnp.concatenate([block[held : held + tokens, HD:] for block in blocks], axis=0)
    scale = math.log2(math.e) / math.sqrt(HD)
    rows = min(ROWS, heads * tokens)
    together = rows // tokens
    attended = []
    for first in range(0, heads, together):
        grouped = jnp.concatenate(
            [queries[:, h * HD : (h + 1) * HD] for h in range(first, first + together)], axis=0
        )
        highest = None
        for step in range(ep_count):
            part = scale * lax.dot_general(
                grouped, blocks[step][:held, :HD], TRANSPOSED, preferred_element_type=jnp.float32
            )
            if not all_open:
                entry = lax.broadcasted_iota(jnp.int32, part.shape, 1)
                part = jnp.where(entry < counts[step], part, MASKED)
            scores[:, step * held : (step + 1) * held] = part
            top = jnp.max(part, axis=1, keepdims=True)
            highest = top if highest is None else jnp.maximum(highest, top)
        part = scale * lax.dot_general(
            grouped, suffix_keys, TRANSPOSED, preferred_element_type=jnp.float32
        )
        part = part + jnp.concatenate([bias] * together, axis=0)
        highest = jnp.maximum(highest, jnp.max(part, axis=1, keepdims=True))
        part = jnp.exp2(part - highest)
        total = jnp.sum(part, axis=1, keepdims=True)
        mixed = jnp.dot(
            part.astype(jnp.bfloat16), suffix_values, preferred_element_type=jnp.float32
        )
        for step in range(ep_count):
            part = jnp.exp2(scores[:, step * held : (step + 1) * held] - highest)
            total += jnp.sum(part, axis=1, keepdims=True)
            mixed += jnp.dot(
                part.astype(jnp.bfloat16),
                blocks[step][:held, HD:],
                preferred_element_type=jnp.float32,
            )
        mixed = (mixed / total).astype(jnp.bfloat16)
        attended += [mixed[h * tokens : (h + 1) * tokens] for h in range(together)]
    attended = jnp.concatenate(attended, axis=1)
    for at in range(0, out_weight.shape[1], COLUMNS):
        projected[:, at : at + COLUMNS] = jnp.dot(
            attended, out_weight[:, at : at + COLUMNS], preferred_element_type=jnp.float32
        )
    count = tokens // row_blocks
    for spot, piece in enumerate(piece_order(row_blocks)):
        rows = projected[pl.ds(pl.multiple_of((block_index ^ piece) * count, count), count), :]
        ref, spot = (kept_ref, spot) if 2 * spot < row_blocks else (sent_ref, spot - row_blocks // 2)
        ref[spot * count : (spot + 1) * count, :] = rows.astype(ref.dtype)


def attend_call(
    lens, place, counts, owners, queries, arrived, out_weight, held, blocks, own_most, all_open
):
    tokens = queries.shape[0]
    ep_count = len(arrived)
    model_width = out_weight.shape[1]
    heads = queries.shape[1] // HD
    keys = ep_count * (held + tokens)
    page_size = tokens * ep_count // owners.shape[0]
    return pl.pallas_call(
        lambda *refs: attend_kernel(ep_count, held, tokens, blocks, all_open, *refs),
        out_shape=[
            jax.ShapeDtypeStruct((tokens // 2, model_width), jnp.float32),
            jax.ShapeDtypeStruct((tokens // 2, model_width), jnp.bfloat16),
            jax.ShapeDtypeStruct((own_most * page_size, 2 * HD), jnp.bfloat16),
        ],
        in_specs=[SCALARS] * 4 + [WHOLE] * (ep_count + 2),
        out_specs=[WHOLE] * 3,
        scratch_shapes=[
            pltpu.VMEM((min(ROWS, heads * tokens), ep_count * held), jnp.float32),
            pltpu.VMEM((tokens, model_width), jnp.float32),
            pltpu.SMEM((owners.shape[0],), jnp.int32),
        ],
        compiler_params=pltpu.CompilerParams(vmem_limit_bytes=VMEM_LIMIT),
        cost_estimate=pl.CostEstimate(
            flops=4 * heads * tokens * keys * HD + 2 * tokens * heads * HD * model_width,
            bytes_accessed=2 * heads * HD * model_width,
            transcendentals=heads * tokens * keys,
        ),
        name="attend",
    )(lens, place, counts, owners, queries, *arrived, out_weight)


def expert_kernel(count, steps, blocks, row_weights, *refs):
    row_refs = refs[:count]
    gate_up, down_weight = refs[count : count + 2]
    kept_ref, sent_ref = refs[-2:]
    tokens = 2 * kept_ref.shape[0] // len(steps)
    row_count = tokens // blocks
    row_weight = jnp.concatenate(
        [
            row_weights[step * tokens + spot * row_count : step * tokens + (spot + 1) * row_count, :1]
            for spot in range(blocks)
            for step in steps
        ],
        axis=0,
    )
    gate_part = up_part = 0.0
    for at in range(0, kept_ref.shape[1], COLUMNS):
        rows = jnp.concatenate([ref[:, at : at + COLUMNS] for ref in row_refs], axis=0)
        gate_part += lax.dot_general(
            rows, gate_up[0, 0, :, at : at + COLUMNS], TRANSPOSED, preferred_element_type=jnp.float32
        )
        up_part += lax.dot_general(
            rows, gate_up[0, 1, :, at : at + COLUMNS], TRANSPOSED, preferred_element_type=jnp.float32
        )
    hidden = gate_part / (1.0 + jnp.exp(-gate_part)) * up_part
    hidden = (hidden * row_weight).astype(jnp.bfloat16)
    half = kept_ref.shape[0]
    for at in range(0, kept_ref.shape[1], COLUMNS):
        out = jnp.dot(
            hidden, down_weight[0, :, at : at + COLUMNS], preferred_element_type=jnp.float32
        ).astype(jnp.bfloat16)
        kept_ref[:, at : at + COLUMNS] = out[:half]
        sent_ref[:, at : at + COLUMNS] = out[half:]


def expert_call(steps, blocks, row_weights, have, gate_up, down_weight, after):
    if have[0].shape[0] % 16:
        have = [jnp.concatenate(have, axis=0)]
    tokens = sum(piece.shape[0] for piece in have)
    model_width = have[0].shape[1]
    hidden_units = down_weight.shape[1]
    half = jax.ShapeDtypeStruct((tokens // 2, model_width), jnp.bfloat16)
    return pl.pallas_call(
        lambda *refs: expert_kernel(len(have), steps, blocks, *refs),
        out_shape=(half, half),
        in_specs=[WHOLE] * (len(have) + 3) + [ANYWHERE] * len(after),
        out_specs=(WHOLE, WHOLE),
        compiler_params=pltpu.CompilerParams(vmem_limit_bytes=VMEM_LIMIT),
        cost_estimate=EXPERT_COST,
        name="experts",
    )(row_weights, *have, gate_up, down_weight, *after)


def local(
    queries,
    new_kv,
    cache_pool,
    hit_pages,
    span_lengths,
    out_weight,
    hidden_in,
    norm_gain,
    expert_ids,
    gate_weights,
    gate_up,
    down_weight,
    new_owner,
):
    tokens = queries.shape[0]
    model_width = hidden_in.shape[1]
    ep_count = lax.axis_size("ep")
    tp_count = lax.axis_size("tp")
    blocks = lax.axis_size("kv") * tp_count
    ep_index = lax.axis_index("ep")
    kv_index = lax.axis_index("kv")
    tp_index = lax.axis_index("tp")
    block_index = kv_index * tp_count + tp_index
    keyval_local = new_kv.shape[1]
    heads_local = queries.shape[1] // HD
    keyval_pick = block_index * heads_local // (HQ // KVH) - kv_index * keyval_local
    row_count = tokens // blocks
    pool_pages = cache_pool.shape[0]
    page_size = cache_pool.shape[1]
    held = HOLD_MOST * page_size

    hits = hit_pages.shape[0]
    owned_hits = hit_pages // pool_pages == ep_index
    earlier = jnp.arange(hits)[None, :] < jnp.arange(hits)[:, None]
    hit_rank = jnp.sum((earlier & owned_hits[None, :]).astype(jnp.int32), axis=1)
    hit_pick = owned_hits[None, :] & (
        hit_rank[None, :] == jnp.arange(HOLD_MOST, dtype=jnp.int32)[:, None]
    )
    local_page = jnp.sum(jnp.where(hit_pick, hit_pages[None, :] - ep_index * pool_pages, 0), axis=1)
    chosen = cache_pool.at[local_page].get(mode="promise_in_bounds")
    own_pages = lax.dynamic_index_in_dim(chosen, keyval_pick, 2, keepdims=False).reshape(held, 2 * HD)
    own_suffix = lax.dynamic_index_in_dim(new_kv, keyval_pick, 1, keepdims=False)

    by_expert = jnp.sum(
        jnp.where(
            expert_ids[:, :, None] == jnp.arange(ep_count, dtype=jnp.int32)[None, None, :],
            gate_weights[:, :, None],
            0.0,
        ),
        axis=1,
    )
    weight_part = jnp.concatenate(three_parts(by_expert.T), axis=0)
    weight_rows = weight_part.shape[0]
    weight_part = jnp.pad(
        weight_part, ((0, -weight_rows % WEIGHT_ROWS), (0, 2 * HD - weight_part.shape[1]))
    )
    payload = jnp.concatenate([own_pages, own_suffix, weight_part], axis=0)
    arrived = [payload]
    for step in range(1, ep_count):
        arrived.append(
            lax.ppermute(payload, "ep", [(i, i ^ step) for i in range(ep_count)])
        )
    sources = [ep_index ^ step for step in range(ep_count)]

    all_open = hits == HOLD_MOST * ep_count
    holder = hit_pages // pool_pages
    counts = jnp.sum(
        (holder[None, :] == jnp.stack(sources)[:, None]).astype(jnp.int32) * page_size, axis=1
    )
    if all_open:
        counts = jnp.zeros((1,), jnp.int32)
    place = jnp.stack([ep_index, block_index]).astype(jnp.int32)
    exchange = lambda value, bit: lax.ppermute(
        value, ("kv", "tp"), [(i, i ^ bit) for i in range(blocks)]
    )
    across = lambda value, step: lax.ppermute(
        value, "ep", [(i, i ^ step) for i in range(ep_count)]
    )
    bits = [1 << place for place in range(1, blocks.bit_length() - 1)]

    def scatter(kept, sent):
        got = exchange(sent, 1)
        gives = []
        for bit in reversed(bits):
            half = kept.shape[0] // 2
            give = kept[half:].astype(jnp.float32) + got[half:].astype(jnp.float32)
            gives.append(give.astype(jnp.bfloat16))
            kept = kept[:half].astype(jnp.float32) + got[:half].astype(jnp.float32)
            got = exchange(gives[-1], bit)
        return kept.astype(jnp.float32) + got.astype(jnp.float32), gives

    own_most = 2 * (tokens // page_size)
    own_slots = block_index * row_count + jnp.arange(row_count, dtype=jnp.int32)
    rows_filled = own_slots < span_lengths[ep_index]
    core = jnp.broadcast_to(tp_index.astype(jnp.int32), (1, 1, 2 * HD))
    core, row_mask = lax.optimization_barrier((core, rows_filled.astype(jnp.int32)))
    own_hidden = lax.dynamic_slice_in_dim(hidden_in, block_index * row_count, row_count, 0)
    held_out, held_gate_up, held_down, _ = hold_call(
        [out_weight, gate_up, down_weight], payload, place, row_mask, core, own_hidden
    )
    kept, sent, head_pages = attend_call(
        span_lengths,
        place,
        counts,
        new_owner,
        queries,
        arrived,
        held_out,
        held,
        blocks,
        own_most,
        all_open,
    )
    head_pages = head_pages.reshape(own_most, page_size, 2 * HD)
    heads_out, _ = scatter(kept, sent)
    residual = (own_hidden.astype(jnp.float32) + heads_out).astype(jnp.bfloat16)
    resid_wide = residual.astype(jnp.float32)
    normed = (
        resid_wide
        * lax.rsqrt(jnp.mean(resid_wide * resid_wide, axis=1, keepdims=True) + EPSILON)
        * norm_gain
    ).astype(jnp.bfloat16)

    def group_rows(piece, before=None):
        have = [piece]
        for bit in bits + [1]:
            have += [exchange(part, bit) for part in have]
            if before is not None and len(have) == 2:
                have[1], before = lax.optimization_barrier([have[1], before])
        return have

    row_weights = prepare_call(place, arrived, normed, blocks, tokens, held + tokens)
    ep_bits = [1 << place for place in reversed(range(ep_count.bit_length() - 1))]
    early = [exchange(normed, bit) for bit in bits + [1]]
    direct = [across(normed, bit) for bit in ep_bits]
    row_weights, *tied = lax.optimization_barrier([row_weights] + early + direct)
    early, direct = tied[: len(early)], dict(zip(ep_bits, tied[len(early) :]))
    crossed = {0: normed}
    for bit in ep_bits:
        for step in list(crossed):
            crossed[step ^ bit] = across(crossed[step], bit) if step else direct[bit]
    own_have = [normed]
    for bit, piece in zip(bits + [1], early):
        own_have += [piece] + [exchange(part, bit) for part in own_have[1:]]

    groups = [[step] for step in [ep_count // 2] + [step for step in reversed(range(1, ep_count)) if step != ep_count // 2] + [0]]
    sums = {}
    sent, given, finished = None, [], []
    for turn, group in enumerate(groups):
        after = [sent] if turn >= 1 else []
        after += given[turn - 2 : turn - 1] if turn >= 2 else []
        if turn == len(groups) - 1:
            after += given[turn - 1 :] + finished[: turn - 1]
        haves = {
            step: group_rows(crossed[step], sent if turn == 1 else None) if step else own_have
            for step in group
        }
        have = [haves[step][spot] for spot in range(blocks) for step in group]
        kept, sent = expert_call(
            tuple(group), blocks, row_weights, have, held_gate_up, held_down, after
        )
        own, gives = scatter(kept, sent)
        given.append(gives[0] if gives else own.astype(jnp.bfloat16))
        finished.append(own.astype(jnp.bfloat16))
        for spot, step in enumerate(group):
            sums[step] = own[spot * row_count : (spot + 1) * row_count]
    for bit in reversed(ep_bits):
        for step in [step for step in sums if step & bit]:
            sums[step ^ bit] = sums[step ^ bit] + across(
                sums.pop(step).astype(jnp.bfloat16), bit
            ).astype(jnp.float32)
    mixture = resid_wide + sums[0]
    layer_out = jnp.where(row_mask[:, None] > 0, mixture, 0.0).astype(jnp.bfloat16)

    if keyval_local == 1:
        decode_pages = head_pages[:, :, None, :]
    else:
        other = lax.ppermute(head_pages, "tp", [(i, i ^ 1) for i in range(tp_count)])
        first = core == 0
        decode_pages = jnp.stack(
            [jnp.where(first, head_pages, other), jnp.where(first, other, head_pages)], axis=2
        )
    return (layer_out, decode_pages)


def solution(mesh):
    placed = (
        P(("groups", "ep"), ("kv", "tp")),
        P(("groups", "ep"), "kv", None),
        P(("groups", "ep"), None, "kv", None),
        P("groups"),
        P("groups"),
        P(("kv", "tp"), None),
        P(("groups", "ep"), None),
        P(),
        P(("groups", "ep"), None),
        P(("groups", "ep"), None),
        P("ep", None, ("kv", "tp"), None),
        P("ep", ("kv", "tp"), None),
        P("groups"),
    )
    return jax.shard_map(
        local,
        mesh=mesh,
        in_specs=placed,
        out_specs=(P(("groups", "ep", "kv", "tp"), None), P(("groups", "ep"), None, "kv", None)),
        check_vma=False,
    )
```

```python
import math

import jax
import jax.numpy as jnp
from jax import lax
from jax.experimental import pallas as pl
from jax.experimental.pallas import tpu as pltpu
from jax.sharding import PartitionSpec as P

HD = 128
HQ = 32
KVH = 4
HOLD_MOST = 16
WEIGHT_ROWS = 16

MASKED = -1e30
EPSILON = 1e-06


def three_parts(wide):
    high = lax.reduce_precision(wide, 8, 7)
    rest = wide - high
    middle = lax.reduce_precision(rest, 8, 7)
    low = rest - middle
    return [part.astype(jnp.bfloat16) for part in (high, middle, low)]


def piece_order(blocks):
    order = [0]
    bit = 2
    while bit < blocks:
        order += [piece ^ bit for piece in order]
        bit *= 2
    return order + [piece ^ 1 for piece in order]


TRANSPOSED = (((1,), (1,)), ((), ()))
WHOLE = pl.BlockSpec(memory_space=pltpu.VMEM)
ANYWHERE = pl.BlockSpec(memory_space=pl.ANY)
SCALARS = pl.BlockSpec(memory_space=pltpu.SMEM)
COLUMNS = 1024
ROWS = 256
VMEM_LIMIT = 16 * 2**20
EXPERT_COST = pl.CostEstimate(flops=1024, bytes_accessed=1024, transcendentals=0)


def hold_kernel(count, *refs):
    sources, held, token, sem = refs[:count], refs[-2 - count : -2], refs[-2], refs[-1]
    token[...] = jnp.zeros_like(token)
    copies = [
        pltpu.make_async_copy(source, target, sem.at[i])
        for i, (source, target) in enumerate(zip(sources, held))
    ]
    for copy in copies:
        copy.start()
    for copy in copies:
        copy.wait()


def hold_call(arrays, *after):
    size = sum(math.prod(array.shape) * 2 for array in arrays)
    return pl.pallas_call(
        lambda *refs: hold_kernel(len(arrays), *refs),
        out_shape=[jax.ShapeDtypeStruct(array.shape, array.dtype) for array in arrays]
        + [jax.ShapeDtypeStruct((8, 128), jnp.float32)],
        in_specs=[ANYWHERE] * (len(arrays) + len(after)),
        out_specs=[WHOLE] * (len(arrays) + 1),
        scratch_shapes=[pltpu.SemaphoreType.DMA((len(arrays),))],
        compiler_params=pltpu.CompilerParams(vmem_limit_bytes=VMEM_LIMIT),
        cost_estimate=pl.CostEstimate(flops=0, bytes_accessed=2 * size, transcendentals=0),
        name="hold",
    )(*arrays, *after)


def prepare_kernel(ep_count, blocks, weight_at, place, *refs):
    payloads = refs[:ep_count]
    row_weights = refs[-1]
    tokens = row_weights.shape[0] // ep_count
    row_count = tokens // blocks
    wide = (tokens, payloads[0].shape[1])
    row = lax.broadcasted_iota(jnp.int32, wide, 0)
    token = row % row_count
    for spot, piece in enumerate(piece_order(blocks)):
        token = token + jnp.where(row // row_count == spot, (place[1] ^ piece) * row_count, 0)
    here = lax.broadcasted_iota(jnp.int32, wide, 1) == token
    for step, payload in enumerate(payloads):
        parts = payload[weight_at:, :].astype(jnp.float32)
        part_row = lax.broadcasted_iota(jnp.int32, parts.shape, 0)
        chosen = (part_row % ep_count == place[0]) & (part_row < 3 * ep_count)
        by_token = jnp.sum(jnp.where(chosen, parts, 0.0), axis=0, keepdims=True)
        column = jnp.sum(jnp.where(here, by_token, 0.0), axis=1, keepdims=True)
        row_weights[step * tokens : (step + 1) * tokens, :] = jnp.broadcast_to(column, (tokens, HD))


def prepare_call(place, arrived, after, blocks, tokens, weight_at):
    ep_count = len(arrived)
    return pl.pallas_call(
        lambda *refs: prepare_kernel(ep_count, blocks, weight_at, *refs),
        out_shape=jax.ShapeDtypeStruct((ep_count * tokens, HD), jnp.float32),
        in_specs=[SCALARS] + [WHOLE] * ep_count + [ANYWHERE],
        out_specs=WHOLE,
        compiler_params=pltpu.CompilerParams(vmem_limit_bytes=VMEM_LIMIT),
        cost_estimate=EXPERT_COST,
        name="prepare",
    )(place, *arrived, after)


def attend_kernel(ep_count, held, tokens, row_blocks, all_open, lens, place, counts, owners, queries, *refs):
    blocks = refs[:ep_count]
    out_weight = refs[ep_count]
    kept_ref, sent_ref, pages_ref = refs[ep_count + 1 : ep_count + 4]
    scores, projected, ranks = refs[ep_count + 4 :]
    heads = queries.shape[1] // HD
    ep_index = place[0]
    block_index = place[1]
    suffix = ep_count * tokens

    page_count = owners.shape[0]
    pages_here = page_count // ep_count
    page_size = tokens // pages_here

    def rank_of(page, earlier):
        ranks[page] = earlier
        return earlier + (owners[page] == ep_index).astype(jnp.int32)

    lax.fori_loop(0, page_count, rank_of, jnp.int32(0))
    pages_ref[...] = jnp.zeros_like(pages_ref)
    for step in range(ep_count):
        source = ep_index ^ step
        for k in range(pages_here):
            page = source * pages_here + k

            @pl.when(owners[page] == ep_index)
            def _(step=step, source=source, k=k, page=page):
                first = held + k * page_size
                entries = blocks[step][first : first + page_size, :]
                row = lax.broadcasted_iota(jnp.int32, entries.shape, 0) + k * page_size
                entries = jnp.where(row < lens[source], entries.astype(jnp.float32), 0.0)
                at = pl.multiple_of(ranks[page] * page_size, page_size)
                pages_ref[pl.ds(at, page_size), :] = entries.astype(jnp.bfloat16)

    own_start = jnp.int32(0)
    for j in range(ep_count):
        own_start = own_start + jnp.where(j < ep_index, lens[j], 0)
    column = lax.broadcasted_iota(jnp.int32, (tokens, suffix), 1)
    slot = column % tokens
    query_position = own_start + lax.broadcasted_iota(jnp.int32, (tokens, suffix), 0)
    seen = jnp.zeros((tokens, suffix), jnp.int32)
    for step in range(ep_count):
        source = ep_index ^ step
        start = jnp.int32(0)
        for j in range(ep_count):
            start = start + jnp.where(j < source, lens[j], 0)
        last = jnp.minimum(query_position - start, lens[source] - 1)
        here = (column // tokens == step) & (slot <= last)
        seen = seen + here.astype(jnp.int32)
    bias = jnp.where(seen > 0, 0.0, MASKED)

    suffix_keys = jnp.concatenate([block[held : held + tokens, :HD] for block in blocks], axis=0)
    suffix_values = jnp.concatenate([block[held : held + tokens, HD:] for block in blocks], axis=0)
    scale = math.log2(math.e) / math.sqrt(HD)
    rows = min(ROWS, heads * tokens)
    together = rows // tokens
    attended = []
    for first in range(0, heads, together):
        grouped = jnp.concatenate(
            [queries[:, h * HD : (h + 1) * HD] for h in range(first, first + together)], axis=0
        )
        highest = None
        for step in range(ep_count):
            part = scale * lax.dot_general(
                grouped, blocks[step][:held, :HD], TRANSPOSED, preferred_element_type=jnp.float32
            )
            if not all_open:
                entry = lax.broadcasted_iota(jnp.int32, part.shape, 1)
                part = jnp.where(entry < counts[step], part, MASKED)
            scores[:, step * held : (step + 1) * held] = part
            top = jnp.max(part, axis=1, keepdims=True)
            highest = top if highest is None else jnp.maximum(highest, top)
        part = scale * lax.dot_general(
            grouped, suffix_keys, TRANSPOSED, preferred_element_type=jnp.float32
        )
        part = part + jnp.concatenate([bias] * together, axis=0)
        highest = jnp.maximum(highest, jnp.max(part, axis=1, keepdims=True))
        part = jnp.exp2(part - highest)
        total = jnp.sum(part, axis=1, keepdims=True)
        mixed = jnp.dot(
            part.astype(jnp.bfloat16), suffix_values, preferred_element_type=jnp.float32
        )
        for step in range(ep_count):
            part = jnp.exp2(scores[:, step * held : (step + 1) * held] - highest)
            total += jnp.sum(part, axis=1, keepdims=True)
            mixed += jnp.dot(
                part.astype(jnp.bfloat16),
                blocks[step][:held, HD:],
                preferred_element_type=jnp.float32,
            )
        mixed = (mixed / total).astype(jnp.bfloat16)
        attended += [mixed[h * tokens : (h + 1) * tokens] for h in range(together)]
    attended = jnp.concatenate(attended, axis=1)
    for at in range(0, out_weight.shape[1], COLUMNS):
        projected[:, at : at + COLUMNS] = jnp.dot(
            attended, out_weight[:, at : at + COLUMNS], preferred_element_type=jnp.float32
        )
    count = tokens // row_blocks
    for spot, piece in enumerate(piece_order(row_blocks)):
        rows = projected[pl.ds(pl.multiple_of((block_index ^ piece) * count, count), count), :]
        ref, spot = (kept_ref, spot) if 2 * spot < row_blocks else (sent_ref, spot - row_blocks // 2)
        ref[spot * count : (spot + 1) * count, :] = rows.astype(ref.dtype)


def attend_call(
    lens, place, counts, owners, queries, arrived, out_weight, held, blocks, own_most, all_open
):
    tokens = queries.shape[0]
    ep_count = len(arrived)
    model_width = out_weight.shape[1]
    heads = queries.shape[1] // HD
    keys = ep_count * (held + tokens)
    page_size = tokens * ep_count // owners.shape[0]
    return pl.pallas_call(
        lambda *refs: attend_kernel(ep_count, held, tokens, blocks, all_open, *refs),
        out_shape=[
            jax.ShapeDtypeStruct((tokens // 2, model_width), jnp.float32),
            jax.ShapeDtypeStruct((tokens // 2, model_width), jnp.bfloat16),
            jax.ShapeDtypeStruct((own_most * page_size, 2 * HD), jnp.bfloat16),
        ],
        in_specs=[SCALARS] * 4 + [WHOLE] * (ep_count + 2),
        out_specs=[WHOLE] * 3,
        scratch_shapes=[
            pltpu.VMEM((min(ROWS, heads * tokens), ep_count * held), jnp.float32),
            pltpu.VMEM((tokens, model_width), jnp.float32),
            pltpu.SMEM((owners.shape[0],), jnp.int32),
        ],
        compiler_params=pltpu.CompilerParams(vmem_limit_bytes=VMEM_LIMIT),
        cost_estimate=pl.CostEstimate(
            flops=4 * heads * tokens * keys * HD + 2 * tokens * heads * HD * model_width,
            bytes_accessed=2 * heads * HD * model_width,
            transcendentals=heads * tokens * keys,
        ),
        name="attend",
    )(lens, place, counts, owners, queries, *arrived, out_weight)


def expert_kernel(count, steps, blocks, row_weights, *refs):
    row_refs = refs[:count]
    gate_up, down_weight = refs[count : count + 2]
    kept_ref, sent_ref = refs[-2:]
    tokens = 2 * kept_ref.shape[0] // len(steps)
    row_count = tokens // blocks
    row_weight = jnp.concatenate(
        [
            row_weights[step * tokens + spot * row_count : step * tokens + (spot + 1) * row_count, :1]
            for spot in range(blocks)
            for step in steps
        ],
        axis=0,
    )
    gate_part = up_part = 0.0
    for at in range(0, kept_ref.shape[1], COLUMNS):
        rows = jnp.concatenate([ref[:, at : at + COLUMNS] for ref in row_refs], axis=0)
        gate_part += lax.dot_general(
            rows, gate_up[0, 0, :, at : at + COLUMNS], TRANSPOSED, preferred_element_type=jnp.float32
        )
        up_part += lax.dot_general(
            rows, gate_up[0, 1, :, at : at + COLUMNS], TRANSPOSED, preferred_element_type=jnp.float32
        )
    hidden = gate_part / (1.0 + jnp.exp(-gate_part)) * up_part
    hidden = (hidden * row_weight).astype(jnp.bfloat16)
    half = kept_ref.shape[0]
    for at in range(0, kept_ref.shape[1], COLUMNS):
        out = jnp.dot(
            hidden, down_weight[0, :, at : at + COLUMNS], preferred_element_type=jnp.float32
        ).astype(jnp.bfloat16)
        kept_ref[:, at : at + COLUMNS] = out[:half]
        sent_ref[:, at : at + COLUMNS] = out[half:]


def expert_call(steps, blocks, row_weights, have, gate_up, down_weight, after):
    if have[0].shape[0] % 16:
        have = [jnp.concatenate(have, axis=0)]
    tokens = sum(piece.shape[0] for piece in have)
    model_width = have[0].shape[1]
    hidden_units = down_weight.shape[1]
    half = jax.ShapeDtypeStruct((tokens // 2, model_width), jnp.bfloat16)
    return pl.pallas_call(
        lambda *refs: expert_kernel(len(have), steps, blocks, *refs),
        out_shape=(half, half),
        in_specs=[WHOLE] * (len(have) + 3) + [ANYWHERE] * len(after),
        out_specs=(WHOLE, WHOLE),
        compiler_params=pltpu.CompilerParams(vmem_limit_bytes=VMEM_LIMIT),
        cost_estimate=EXPERT_COST,
        name="experts",
    )(row_weights, *have, gate_up, down_weight, *after)


def local(
    queries,
    new_kv,
    cache_pool,
    hit_pages,
    span_lengths,
    out_weight,
    hidden_in,
    norm_gain,
    expert_ids,
    gate_weights,
    gate_up,
    down_weight,
    new_owner,
):
    tokens = queries.shape[0]
    model_width = hidden_in.shape[1]
    ep_count = lax.axis_size("ep")
    tp_count = lax.axis_size("tp")
    blocks = lax.axis_size("kv") * tp_count
    ep_index = lax.axis_index("ep")
    kv_index = lax.axis_index("kv")
    tp_index = lax.axis_index("tp")
    block_index = kv_index * tp_count + tp_index
    keyval_local = new_kv.shape[1]
    heads_local = queries.shape[1] // HD
    keyval_pick = block_index * heads_local // (HQ // KVH) - kv_index * keyval_local
    row_count = tokens // blocks
    pool_pages = cache_pool.shape[0]
    page_size = cache_pool.shape[1]
    held = HOLD_MOST * page_size

    hits = hit_pages.shape[0]
    owned_hits = hit_pages // pool_pages == ep_index
    earlier = jnp.arange(hits)[None, :] < jnp.arange(hits)[:, None]
    hit_rank = jnp.sum((earlier & owned_hits[None, :]).astype(jnp.int32), axis=1)
    hit_pick = owned_hits[None, :] & (
        hit_rank[None, :] == jnp.arange(HOLD_MOST, dtype=jnp.int32)[:, None]
    )
    local_page = jnp.sum(jnp.where(hit_pick, hit_pages[None, :] - ep_index * pool_pages, 0), axis=1)
    chosen = cache_pool.at[local_page].get(mode="promise_in_bounds")
    own_pages = lax.dynamic_index_in_dim(chosen, keyval_pick, 2, keepdims=False).reshape(held, 2 * HD)
    own_suffix = lax.dynamic_index_in_dim(new_kv, keyval_pick, 1, keepdims=False)

    by_expert = jnp.sum(
        jnp.where(
            expert_ids[:, :, None] == jnp.arange(ep_count, dtype=jnp.int32)[None, None, :],
            gate_weights[:, :, None],
            0.0,
        ),
        axis=1,
    )
    weight_part = jnp.concatenate(three_parts(by_expert.T), axis=0)
    weight_rows = weight_part.shape[0]
    weight_part = jnp.pad(
        weight_part, ((0, -weight_rows % WEIGHT_ROWS), (0, 2 * HD - weight_part.shape[1]))
    )
    payload = jnp.concatenate([own_pages, own_suffix, weight_part], axis=0)
    arrived = [payload]
    for step in range(1, ep_count):
        arrived.append(
            lax.ppermute(payload, "ep", [(i, i ^ step) for i in range(ep_count)])
        )
    sources = [ep_index ^ step for step in range(ep_count)]

    all_open = hits == HOLD_MOST * ep_count
    holder = hit_pages // pool_pages
    counts = jnp.sum(
        (holder[None, :] == jnp.stack(sources)[:, None]).astype(jnp.int32) * page_size, axis=1
    )
    if all_open:
        counts = jnp.zeros((1,), jnp.int32)
    place = jnp.stack([ep_index, block_index]).astype(jnp.int32)
    exchange = lambda value, bit: lax.ppermute(
        value, ("kv", "tp"), [(i, i ^ bit) for i in range(blocks)]
    )
    across = lambda value, step: lax.ppermute(
        value, "ep", [(i, i ^ step) for i in range(ep_count)]
    )
    bits = [1 << place for place in range(1, blocks.bit_length() - 1)]

    def scatter(kept, sent, before=None):
        got = exchange(sent, 1)
        gives = []
        for bit in reversed(bits):
            half = kept.shape[0] // 2
            give = kept[half:].astype(jnp.float32) + got[half:].astype(jnp.float32)
            give = give.astype(jnp.bfloat16)
            if before is not None and not gives:
                give, before = lax.optimization_barrier((give, before))
            gives.append(give)
            kept = kept[:half].astype(jnp.float32) + got[:half].astype(jnp.float32)
            got = exchange(give, bit)
        return kept.astype(jnp.float32) + got.astype(jnp.float32), gives, got

    own_most = 2 * (tokens // page_size)
    own_slots = block_index * row_count + jnp.arange(row_count, dtype=jnp.int32)
    rows_filled = own_slots < span_lengths[ep_index]
    core = jnp.broadcast_to(tp_index.astype(jnp.int32), (1, 1, 2 * HD))
    core, row_mask = lax.optimization_barrier((core, rows_filled.astype(jnp.int32)))
    own_hidden = lax.dynamic_slice_in_dim(hidden_in, block_index * row_count, row_count, 0)
    held_out, held_gate_up, held_down, _ = hold_call(
        [out_weight, gate_up, down_weight], payload, place, row_mask, core, own_hidden
    )
    kept, sent, head_pages = attend_call(
        span_lengths,
        place,
        counts,
        new_owner,
        queries,
        arrived,
        held_out,
        held,
        blocks,
        own_most,
        all_open,
    )
    head_pages = head_pages.reshape(own_most, page_size, 2 * HD)
    heads_out, _, _ = scatter(kept, sent)
    residual = (own_hidden.astype(jnp.float32) + heads_out).astype(jnp.bfloat16)
    resid_wide = residual.astype(jnp.float32)
    normed = (
        resid_wide
        * lax.rsqrt(jnp.mean(resid_wide * resid_wide, axis=1, keepdims=True) + EPSILON)
        * norm_gain
    ).astype(jnp.bfloat16)

    def group_rows(have, bits):
        for bit in bits:
            have = have + [exchange(part, bit) for part in have]
        return have

    def experts(group, haves, after):
        have = [haves[step][spot] for spot in range(blocks) for step in group]
        return expert_call(
            tuple(group), blocks, row_weights, have, held_gate_up, held_down, after
        )

    row_weights = prepare_call(place, arrived, normed, blocks, tokens, held + tokens)
    ep_bits = [1 << place for place in reversed(range(ep_count.bit_length() - 1))]
    early = [exchange(normed, bit) for bit in bits + [1]]
    direct = [across(normed, bit) for bit in ep_bits]
    row_weights, *tied = lax.optimization_barrier([row_weights] + early + direct)
    early, direct = tied[: len(early)], dict(zip(ep_bits, tied[len(early) :]))

    own_have = [normed]
    for bit, piece in zip(bits + [1], early):
        own_have += [piece] + [exchange(part, bit) for part in own_have[1:]]
    kept, sent = experts([0], {0: own_have}, [])
    crossed = {0: normed}
    for bit in ep_bits:
        for step in list(crossed):
            crossed[step ^ bit] = across(crossed[step], bit) if step else direct[bit]
    forwarded = [step for step in crossed if step & (step - 1)]
    leading = ep_bits[0]
    halves = [group_rows([direct[bit]], bits[:1]) for bit in ep_bits]
    sent, halves, ahead = lax.optimization_barrier(
        (sent, halves, [crossed[step] for step in forwarded])
    )
    haves = {bit: group_rows(half, bits[1:] + [1]) for bit, half in zip(ep_bits, halves)}
    haves.update({step: group_rows([piece], bits + [1]) for step, piece in zip(forwarded, ahead)})

    order = [0, leading] + [step for step in reversed(range(1, ep_count)) if step != leading]
    sums = {}
    given, finished = [], []
    for turn, step in enumerate(order):
        if turn >= 1:
            after = [sent]
            after += given[:2] if turn == 2 else []
            kept, sent = experts([step], haves, after)
        last = turn >= 3 and turn == len(order) - 1
        sums[step], gives, received = scatter(kept, sent, received if last else None)
        finished.append(sums[step].astype(jnp.bfloat16))
        given.append(gives[0] if gives else finished[-1])
    for bit in reversed(ep_bits):
        for step in [step for step in sums if step & bit]:
            sums[step ^ bit] = sums[step ^ bit] + across(
                sums.pop(step).astype(jnp.bfloat16), bit
            ).astype(jnp.float32)
    mixture = resid_wide + sums[0]
    layer_out = jnp.where(row_mask[:, None] > 0, mixture, 0.0).astype(jnp.bfloat16)

    if keyval_local == 1:
        decode_pages = head_pages[:, :, None, :]
    else:
        other = lax.ppermute(head_pages, "tp", [(i, i ^ 1) for i in range(tp_count)])
        first = core == 0
        decode_pages = jnp.stack(
            [jnp.where(first, head_pages, other), jnp.where(first, other, head_pages)], axis=2
        )
    return (layer_out, decode_pages)


def solution(mesh):
    placed = (
        P(("groups", "ep"), ("kv", "tp")),
        P(("groups", "ep"), "kv", None),
        P(("groups", "ep"), None, "kv", None),
        P("groups"),
        P("groups"),
        P(("kv", "tp"), None),
        P(("groups", "ep"), None),
        P(),
        P(("groups", "ep"), None),
        P(("groups", "ep"), None),
        P("ep", None, ("kv", "tp"), None),
        P("ep", ("kv", "tp"), None),
        P("groups"),
    )
    return jax.shard_map(
        local,
        mesh=mesh,
        in_specs=placed,
        out_specs=(P(("groups", "ep", "kv", "tp"), None), P(("groups", "ep"), None, "kv", None)),
        check_vma=False,
    )
```

```python
import math

import jax
import jax.numpy as jnp
from jax import lax
from jax.experimental import pallas as pl
from jax.experimental.pallas import tpu as pltpu
from jax.sharding import PartitionSpec as P

HD = 128
HQ = 32
KVH = 4
HOLD_MOST = 16
WEIGHT_ROWS = 16

MASKED = -1e30
EPSILON = 1e-06


def three_parts(wide):
    high = lax.reduce_precision(wide, 8, 7)
    rest = wide - high
    middle = lax.reduce_precision(rest, 8, 7)
    low = rest - middle
    return [part.astype(jnp.bfloat16) for part in (high, middle, low)]


def piece_order(blocks):
    order = [0]
    bit = 2
    while bit < blocks:
        order += [piece ^ bit for piece in order]
        bit *= 2
    return order + [piece ^ 1 for piece in order]


TRANSPOSED = (((1,), (1,)), ((), ()))
WHOLE = pl.BlockSpec(memory_space=pltpu.VMEM)
ANYWHERE = pl.BlockSpec(memory_space=pl.ANY)
SCALARS = pl.BlockSpec(memory_space=pltpu.SMEM)
COLUMNS = 1024
ROWS = 256
VMEM_LIMIT = 16 * 2**20
EXPERT_COST = pl.CostEstimate(flops=1024, bytes_accessed=1024, transcendentals=0)


def hold_kernel(count, *refs):
    sources, held, token, sem = refs[:count], refs[-2 - count : -2], refs[-2], refs[-1]
    token[...] = jnp.zeros_like(token)
    copies = [
        pltpu.make_async_copy(source, target, sem.at[i])
        for i, (source, target) in enumerate(zip(sources, held))
    ]
    for copy in copies:
        copy.start()
    for copy in copies:
        copy.wait()


def hold_call(arrays, *after):
    size = sum(math.prod(array.shape) * 2 for array in arrays)
    return pl.pallas_call(
        lambda *refs: hold_kernel(len(arrays), *refs),
        out_shape=[jax.ShapeDtypeStruct(array.shape, array.dtype) for array in arrays]
        + [jax.ShapeDtypeStruct((8, 128), jnp.float32)],
        in_specs=[ANYWHERE] * (len(arrays) + len(after)),
        out_specs=[WHOLE] * (len(arrays) + 1),
        scratch_shapes=[pltpu.SemaphoreType.DMA((len(arrays),))],
        compiler_params=pltpu.CompilerParams(vmem_limit_bytes=VMEM_LIMIT),
        cost_estimate=pl.CostEstimate(flops=0, bytes_accessed=2 * size, transcendentals=0),
        name="hold",
    )(*arrays, *after)


def prepare_kernel(ep_count, blocks, weight_at, place, *refs):
    payloads = refs[:ep_count]
    row_weights = refs[-1]
    tokens = row_weights.shape[0] // ep_count
    row_count = tokens // blocks
    wide = (tokens, payloads[0].shape[1])
    row = lax.broadcasted_iota(jnp.int32, wide, 0)
    token = row % row_count
    for spot, piece in enumerate(piece_order(blocks)):
        token = token + jnp.where(row // row_count == spot, (place[1] ^ piece) * row_count, 0)
    here = lax.broadcasted_iota(jnp.int32, wide, 1) == token
    for step, payload in enumerate(payloads):
        parts = payload[weight_at:, :].astype(jnp.float32)
        part_row = lax.broadcasted_iota(jnp.int32, parts.shape, 0)
        chosen = (part_row % ep_count == place[0]) & (part_row < 3 * ep_count)
        by_token = jnp.sum(jnp.where(chosen, parts, 0.0), axis=0, keepdims=True)
        column = jnp.sum(jnp.where(here, by_token, 0.0), axis=1, keepdims=True)
        row_weights[step * tokens : (step + 1) * tokens, :] = jnp.broadcast_to(column, (tokens, HD))


def prepare_call(place, arrived, after, blocks, tokens, weight_at):
    ep_count = len(arrived)
    return pl.pallas_call(
        lambda *refs: prepare_kernel(ep_count, blocks, weight_at, *refs),
        out_shape=jax.ShapeDtypeStruct((ep_count * tokens, HD), jnp.float32),
        in_specs=[SCALARS] + [WHOLE] * ep_count + [ANYWHERE],
        out_specs=WHOLE,
        compiler_params=pltpu.CompilerParams(vmem_limit_bytes=VMEM_LIMIT),
        cost_estimate=EXPERT_COST,
        name="prepare",
    )(place, *arrived, after)


def attend_kernel(ep_count, held, tokens, row_blocks, all_open, lens, place, counts, owners, queries, *refs):
    blocks = refs[:ep_count]
    out_weight = refs[ep_count]
    kept_ref, sent_ref, pages_ref = refs[ep_count + 1 : ep_count + 4]
    scores, projected, ranks = refs[ep_count + 4 :]
    heads = queries.shape[1] // HD
    ep_index = place[0]
    block_index = place[1]
    suffix = ep_count * tokens

    page_count = owners.shape[0]
    pages_here = page_count // ep_count
    page_size = tokens // pages_here

    def rank_of(page, earlier):
        ranks[page] = earlier
        return earlier + (owners[page] == ep_index).astype(jnp.int32)

    lax.fori_loop(0, page_count, rank_of, jnp.int32(0))
    pages_ref[...] = jnp.zeros_like(pages_ref)
    for step in range(ep_count):
        source = ep_index ^ step
        for k in range(pages_here):
            page = source * pages_here + k

            @pl.when(owners[page] == ep_index)
            def _(step=step, source=source, k=k, page=page):
                first = held + k * page_size
                entries = blocks[step][first : first + page_size, :]
                row = lax.broadcasted_iota(jnp.int32, entries.shape, 0) + k * page_size
                entries = jnp.where(row < lens[source], entries.astype(jnp.float32), 0.0)
                at = pl.multiple_of(ranks[page] * page_size, page_size)
                pages_ref[pl.ds(at, page_size), :] = entries.astype(jnp.bfloat16)

    own_start = jnp.int32(0)
    for j in range(ep_count):
        own_start = own_start + jnp.where(j < ep_index, lens[j], 0)
    column = lax.broadcasted_iota(jnp.int32, (tokens, suffix), 1)
    slot = column % tokens
    query_position = own_start + lax.broadcasted_iota(jnp.int32, (tokens, suffix), 0)
    seen = jnp.zeros((tokens, suffix), jnp.int32)
    for step in range(ep_count):
        source = ep_index ^ step
        start = jnp.int32(0)
        for j in range(ep_count):
            start = start + jnp.where(j < source, lens[j], 0)
        last = jnp.minimum(query_position - start, lens[source] - 1)
        here = (column // tokens == step) & (slot <= last)
        seen = seen + here.astype(jnp.int32)
    bias = jnp.where(seen > 0, 0.0, MASKED)

    suffix_keys = jnp.concatenate([block[held : held + tokens, :HD] for block in blocks], axis=0)
    suffix_values = jnp.concatenate([block[held : held + tokens, HD:] for block in blocks], axis=0)
    scale = math.log2(math.e) / math.sqrt(HD)
    rows = min(ROWS, heads * tokens)
    together = rows // tokens
    attended = []
    for first in range(0, heads, together):
        grouped = jnp.concatenate(
            [queries[:, h * HD : (h + 1) * HD] for h in range(first, first + together)], axis=0
        )
        highest = None
        for step in range(ep_count):
            part = scale * lax.dot_general(
                grouped, blocks[step][:held, :HD], TRANSPOSED, preferred_element_type=jnp.float32
            )
            if not all_open:
                entry = lax.broadcasted_iota(jnp.int32, part.shape, 1)
                part = jnp.where(entry < counts[step], part, MASKED)
            scores[:, step * held : (step + 1) * held] = part
            top = jnp.max(part, axis=1, keepdims=True)
            highest = top if highest is None else jnp.maximum(highest, top)
        part = scale * lax.dot_general(
            grouped, suffix_keys, TRANSPOSED, preferred_element_type=jnp.float32
        )
        part = part + jnp.concatenate([bias] * together, axis=0)
        highest = jnp.maximum(highest, jnp.max(part, axis=1, keepdims=True))
        part = jnp.exp2(part - highest)
        total = jnp.sum(part, axis=1, keepdims=True)
        mixed = jnp.dot(
            part.astype(jnp.bfloat16), suffix_values, preferred_element_type=jnp.float32
        )
        for step in range(ep_count):
            part = jnp.exp2(scores[:, step * held : (step + 1) * held] - highest)
            total += jnp.sum(part, axis=1, keepdims=True)
            mixed += jnp.dot(
                part.astype(jnp.bfloat16),
                blocks[step][:held, HD:],
                preferred_element_type=jnp.float32,
            )
        mixed = (mixed / total).astype(jnp.bfloat16)
        attended += [mixed[h * tokens : (h + 1) * tokens] for h in range(together)]
    attended = jnp.concatenate(attended, axis=1)
    for at in range(0, out_weight.shape[1], COLUMNS):
        projected[:, at : at + COLUMNS] = jnp.dot(
            attended, out_weight[:, at : at + COLUMNS], preferred_element_type=jnp.float32
        )
    count = tokens // row_blocks
    for spot, piece in enumerate(piece_order(row_blocks)):
        rows = projected[pl.ds(pl.multiple_of((block_index ^ piece) * count, count), count), :]
        ref, spot = (kept_ref, spot) if 2 * spot < row_blocks else (sent_ref, spot - row_blocks // 2)
        ref[spot * count : (spot + 1) * count, :] = rows.astype(ref.dtype)


def attend_call(
    lens, place, counts, owners, queries, arrived, out_weight, held, blocks, own_most, all_open
):
    tokens = queries.shape[0]
    ep_count = len(arrived)
    model_width = out_weight.shape[1]
    heads = queries.shape[1] // HD
    keys = ep_count * (held + tokens)
    page_size = tokens * ep_count // owners.shape[0]
    return pl.pallas_call(
        lambda *refs: attend_kernel(ep_count, held, tokens, blocks, all_open, *refs),
        out_shape=[
            jax.ShapeDtypeStruct((tokens // 2, model_width), jnp.float32),
            jax.ShapeDtypeStruct((tokens // 2, model_width), jnp.bfloat16),
            jax.ShapeDtypeStruct((own_most * page_size, 2 * HD), jnp.bfloat16),
        ],
        in_specs=[SCALARS] * 4 + [WHOLE] * (ep_count + 2),
        out_specs=[WHOLE] * 3,
        scratch_shapes=[
            pltpu.VMEM((min(ROWS, heads * tokens), ep_count * held), jnp.float32),
            pltpu.VMEM((tokens, model_width), jnp.float32),
            pltpu.SMEM((owners.shape[0],), jnp.int32),
        ],
        compiler_params=pltpu.CompilerParams(vmem_limit_bytes=VMEM_LIMIT),
        cost_estimate=pl.CostEstimate(
            flops=4 * heads * tokens * keys * HD + 2 * tokens * heads * HD * model_width,
            bytes_accessed=2 * heads * HD * model_width,
            transcendentals=heads * tokens * keys,
        ),
        name="attend",
    )(lens, place, counts, owners, queries, *arrived, out_weight)


def expert_kernel(count, steps, blocks, row_weights, *refs):
    row_refs = refs[:count]
    gate_up, down_weight = refs[count : count + 2]
    kept_ref, sent_ref = refs[-2:]
    tokens = 2 * kept_ref.shape[0] // len(steps)
    row_count = tokens // blocks
    row_weight = jnp.concatenate(
        [
            row_weights[step * tokens + spot * row_count : step * tokens + (spot + 1) * row_count, :1]
            for spot in range(blocks)
            for step in steps
        ],
        axis=0,
    )
    gate_part = up_part = 0.0
    for at in range(0, kept_ref.shape[1], COLUMNS):
        rows = jnp.concatenate([ref[:, at : at + COLUMNS] for ref in row_refs], axis=0)
        gate_part += lax.dot_general(
            rows, gate_up[0, 0, :, at : at + COLUMNS], TRANSPOSED, preferred_element_type=jnp.float32
        )
        up_part += lax.dot_general(
            rows, gate_up[0, 1, :, at : at + COLUMNS], TRANSPOSED, preferred_element_type=jnp.float32
        )
    hidden = gate_part / (1.0 + jnp.exp(-gate_part)) * up_part
    hidden = (hidden * row_weight).astype(jnp.bfloat16)
    half = kept_ref.shape[0]
    for at in range(0, kept_ref.shape[1], COLUMNS):
        out = jnp.dot(
            hidden, down_weight[0, :, at : at + COLUMNS], preferred_element_type=jnp.float32
        ).astype(jnp.bfloat16)
        kept_ref[:, at : at + COLUMNS] = out[:half]
        sent_ref[:, at : at + COLUMNS] = out[half:]


def expert_call(steps, blocks, row_weights, have, gate_up, down_weight, after):
    if have[0].shape[0] % 16:
        have = [jnp.concatenate(have, axis=0)]
    tokens = sum(piece.shape[0] for piece in have)
    model_width = have[0].shape[1]
    hidden_units = down_weight.shape[1]
    half = jax.ShapeDtypeStruct((tokens // 2, model_width), jnp.bfloat16)
    return pl.pallas_call(
        lambda *refs: expert_kernel(len(have), steps, blocks, *refs),
        out_shape=(half, half),
        in_specs=[WHOLE] * (len(have) + 3) + [ANYWHERE] * len(after),
        out_specs=(WHOLE, WHOLE),
        compiler_params=pltpu.CompilerParams(vmem_limit_bytes=VMEM_LIMIT),
        cost_estimate=EXPERT_COST,
        name="experts",
    )(row_weights, *have, gate_up, down_weight, *after)


def local(
    queries,
    new_kv,
    cache_pool,
    hit_pages,
    span_lengths,
    out_weight,
    hidden_in,
    norm_gain,
    expert_ids,
    gate_weights,
    gate_up,
    down_weight,
    new_owner,
):
    tokens = queries.shape[0]
    model_width = hidden_in.shape[1]
    ep_count = lax.axis_size("ep")
    tp_count = lax.axis_size("tp")
    blocks = lax.axis_size("kv") * tp_count
    ep_index = lax.axis_index("ep")
    kv_index = lax.axis_index("kv")
    tp_index = lax.axis_index("tp")
    block_index = kv_index * tp_count + tp_index
    keyval_local = new_kv.shape[1]
    heads_local = queries.shape[1] // HD
    keyval_pick = block_index * heads_local // (HQ // KVH) - kv_index * keyval_local
    row_count = tokens // blocks
    pool_pages = cache_pool.shape[0]
    page_size = cache_pool.shape[1]
    held = HOLD_MOST * page_size

    hits = hit_pages.shape[0]
    owned_hits = hit_pages // pool_pages == ep_index
    earlier = jnp.arange(hits)[None, :] < jnp.arange(hits)[:, None]
    hit_rank = jnp.sum((earlier & owned_hits[None, :]).astype(jnp.int32), axis=1)
    hit_pick = owned_hits[None, :] & (
        hit_rank[None, :] == jnp.arange(HOLD_MOST, dtype=jnp.int32)[:, None]
    )
    local_page = jnp.sum(jnp.where(hit_pick, hit_pages[None, :] - ep_index * pool_pages, 0), axis=1)
    chosen = cache_pool.at[local_page].get(mode="promise_in_bounds")
    own_pages = lax.dynamic_index_in_dim(chosen, keyval_pick, 2, keepdims=False).reshape(held, 2 * HD)
    own_suffix = lax.dynamic_index_in_dim(new_kv, keyval_pick, 1, keepdims=False)

    by_expert = jnp.sum(
        jnp.where(
            expert_ids[:, :, None] == jnp.arange(ep_count, dtype=jnp.int32)[None, None, :],
            gate_weights[:, :, None],
            0.0,
        ),
        axis=1,
    )
    weight_part = jnp.concatenate(three_parts(by_expert.T), axis=0)
    weight_rows = weight_part.shape[0]
    weight_part = jnp.pad(
        weight_part, ((0, -weight_rows % WEIGHT_ROWS), (0, 2 * HD - weight_part.shape[1]))
    )
    payload = jnp.concatenate([own_pages, own_suffix, weight_part], axis=0)
    arrived = [payload]
    for step in range(1, ep_count):
        arrived.append(
            lax.ppermute(payload, "ep", [(i, i ^ step) for i in range(ep_count)])
        )
    sources = [ep_index ^ step for step in range(ep_count)]

    all_open = hits == HOLD_MOST * ep_count
    holder = hit_pages // pool_pages
    counts = jnp.sum(
        (holder[None, :] == jnp.stack(sources)[:, None]).astype(jnp.int32) * page_size, axis=1
    )
    if all_open:
        counts = jnp.zeros((1,), jnp.int32)
    place = jnp.stack([ep_index, block_index]).astype(jnp.int32)
    exchange = lambda value, bit: lax.ppermute(
        value, ("kv", "tp"), [(i, i ^ bit) for i in range(blocks)]
    )
    across = lambda value, step: lax.ppermute(
        value, "ep", [(i, i ^ step) for i in range(ep_count)]
    )
    bits = [1 << place for place in range(1, blocks.bit_length() - 1)]

    def scatter(kept, sent):
        got = exchange(sent, 1)
        gives = []
        for bit in reversed(bits):
            half = kept.shape[0] // 2
            give = kept[half:].astype(jnp.float32) + got[half:].astype(jnp.float32)
            gives.append(give.astype(jnp.bfloat16))
            kept = kept[:half].astype(jnp.float32) + got[:half].astype(jnp.float32)
            got = exchange(gives[-1], bit)
        return kept.astype(jnp.float32) + got.astype(jnp.float32), gives

    own_most = 2 * (tokens // page_size)
    own_slots = block_index * row_count + jnp.arange(row_count, dtype=jnp.int32)
    rows_filled = own_slots < span_lengths[ep_index]
    core = jnp.broadcast_to(tp_index.astype(jnp.int32), (1, 1, 2 * HD))
    core, row_mask = lax.optimization_barrier((core, rows_filled.astype(jnp.int32)))
    own_hidden = lax.dynamic_slice_in_dim(hidden_in, block_index * row_count, row_count, 0)
    held_out, held_gate_up, held_down, _ = hold_call(
        [out_weight, gate_up, down_weight], payload, place, row_mask, core, own_hidden
    )
    kept, sent, head_pages = attend_call(
        span_lengths,
        place,
        counts,
        new_owner,
        queries,
        arrived,
        held_out,
        held,
        blocks,
        own_most,
        all_open,
    )
    head_pages = head_pages.reshape(own_most, page_size, 2 * HD)
    heads_out, _ = scatter(kept, sent)
    residual = (own_hidden.astype(jnp.float32) + heads_out).astype(jnp.bfloat16)
    resid_wide = residual.astype(jnp.float32)
    normed = (
        resid_wide
        * lax.rsqrt(jnp.mean(resid_wide * resid_wide, axis=1, keepdims=True) + EPSILON)
        * norm_gain
    ).astype(jnp.bfloat16)

    def group_rows(have, bits, before=None):
        for bit in bits:
            have = have + [exchange(part, bit) for part in have]
            if before is not None and len(have) == 2:
                have[1], before = lax.optimization_barrier([have[1], before])
        return have

    row_weights = prepare_call(place, arrived, normed, blocks, tokens, held + tokens)
    ep_bits = [1 << place for place in reversed(range(ep_count.bit_length() - 1))]
    early = [exchange(normed, bit) for bit in bits + [1]]
    direct = [across(normed, bit) for bit in ep_bits]
    row_weights, *tied = lax.optimization_barrier([row_weights] + early + direct)
    early, direct = tied[: len(early)], dict(zip(ep_bits, tied[len(early) :]))
    crossed = {0: normed}
    for bit in ep_bits:
        for step in list(crossed):
            crossed[step ^ bit] = across(crossed[step], bit) if step else direct[bit]
    leading = ep_bits[0]
    forwarded = [step for step in crossed if step & (step - 1)]
    lead_have = group_rows([crossed[leading]], bits[:1])
    lead_have[1:], ahead = lax.optimization_barrier(
        (lead_have[1:], [crossed[step] for step in forwarded])
    )
    crossed.update(zip(forwarded, ahead))
    lead_have = group_rows(lead_have, bits[1:] + [1])
    own_have = [normed]
    for bit, piece in zip(bits + [1], early):
        own_have += [piece] + [exchange(part, bit) for part in own_have[1:]]

    groups = [[step] for step in [ep_count // 2] + [step for step in reversed(range(1, ep_count)) if step != ep_count // 2] + [0]]
    sums = {}
    sent, given, finished = None, [], []
    for turn, group in enumerate(groups):
        after = [sent] if turn >= 1 else []
        after += given[turn - 2 : turn] if turn >= 2 else []
        if turn == len(groups) - 1:
            after += finished[: turn - 1]
        haves = {0: own_have, leading: lead_have}
        for step in group:
            if step not in haves:
                piece = crossed[step]
                if turn > 1 and bits:
                    piece, reached = lax.optimization_barrier((piece, reached))
                haves[step] = group_rows([piece], bits + [1], sent if turn == 1 else None)
                reached = haves[step][1]
        have = [haves[step][spot] for spot in range(blocks) for step in group]
        kept, sent = expert_call(
            tuple(group), blocks, row_weights, have, held_gate_up, held_down, after
        )
        own, gives = scatter(kept, sent)
        given.append(gives[0] if gives else own.astype(jnp.bfloat16))
        finished.append(own.astype(jnp.bfloat16))
        for spot, step in enumerate(group):
            sums[step] = own[spot * row_count : (spot + 1) * row_count]
    mixture = resid_wide
    for step, own in sums.items():
        if step:
            own = across(own.astype(jnp.bfloat16), step).astype(jnp.float32)
        mixture = mixture + own
    layer_out = jnp.where(row_mask[:, None] > 0, mixture, 0.0).astype(jnp.bfloat16)

    if keyval_local == 1:
        decode_pages = head_pages[:, :, None, :]
    else:
        other = lax.ppermute(head_pages, "tp", [(i, i ^ 1) for i in range(tp_count)])
        first = core == 0
        decode_pages = jnp.stack(
            [jnp.where(first, head_pages, other), jnp.where(first, other, head_pages)], axis=2
        )
    return (layer_out, decode_pages)


def solution(mesh):
    placed = (
        P(("groups", "ep"), ("kv", "tp")),
        P(("groups", "ep"), "kv", None),
        P(("groups", "ep"), None, "kv", None),
        P("groups"),
        P("groups"),
        P(("kv", "tp"), None),
        P(("groups", "ep"), None),
        P(),
        P(("groups", "ep"), None),
        P(("groups", "ep"), None),
        P("ep", None, ("kv", "tp"), None),
        P("ep", ("kv", "tp"), None),
        P("groups"),
    )
    return jax.shard_map(
        local,
        mesh=mesh,
        in_specs=placed,
        out_specs=(P(("groups", "ep", "kv", "tp"), None), P(("groups", "ep"), None, "kv", None)),
        check_vma=False,
    )
```

```python
import math

import jax
import jax.numpy as jnp
from jax import lax
from jax.experimental import pallas as pl
from jax.experimental.pallas import tpu as pltpu
from jax.sharding import PartitionSpec as P

HD = 128
HQ = 32
KVH = 4
HOLD_MOST = 16
WEIGHT_ROWS = 16

MASKED = -1e30
EPSILON = 1e-06


def three_parts(wide):
    high = lax.reduce_precision(wide, 8, 7)
    rest = wide - high
    middle = lax.reduce_precision(rest, 8, 7)
    low = rest - middle
    return [part.astype(jnp.bfloat16) for part in (high, middle, low)]


def piece_order(blocks):
    order = [0]
    bit = 2
    while bit < blocks:
        order += [piece ^ bit for piece in order]
        bit *= 2
    return order + [piece ^ 1 for piece in order]


TRANSPOSED = (((1,), (1,)), ((), ()))
WHOLE = pl.BlockSpec(memory_space=pltpu.VMEM)
ANYWHERE = pl.BlockSpec(memory_space=pl.ANY)
SCALARS = pl.BlockSpec(memory_space=pltpu.SMEM)
COLUMNS = 1024
ROWS = 256
VMEM_LIMIT = 16 * 2**20
EXPERT_COST = pl.CostEstimate(flops=1024, bytes_accessed=1024, transcendentals=0)


def hold_kernel(count, *refs):
    sources, held, token, sem = refs[:count], refs[-2 - count : -2], refs[-2], refs[-1]
    token[...] = jnp.zeros_like(token)
    copies = [
        pltpu.make_async_copy(source, target, sem.at[i])
        for i, (source, target) in enumerate(zip(sources, held))
    ]
    for copy in copies:
        copy.start()
    for copy in copies:
        copy.wait()


def hold_call(arrays, *after):
    size = sum(math.prod(array.shape) * 2 for array in arrays)
    return pl.pallas_call(
        lambda *refs: hold_kernel(len(arrays), *refs),
        out_shape=[jax.ShapeDtypeStruct(array.shape, array.dtype) for array in arrays]
        + [jax.ShapeDtypeStruct((8, 128), jnp.float32)],
        in_specs=[ANYWHERE] * (len(arrays) + len(after)),
        out_specs=[WHOLE] * (len(arrays) + 1),
        scratch_shapes=[pltpu.SemaphoreType.DMA((len(arrays),))],
        compiler_params=pltpu.CompilerParams(vmem_limit_bytes=VMEM_LIMIT),
        cost_estimate=pl.CostEstimate(flops=0, bytes_accessed=2 * size, transcendentals=0),
        name="hold",
    )(*arrays, *after)


def prepare_kernel(ep_count, blocks, weight_at, place, *refs):
    payloads = refs[:ep_count]
    row_weights = refs[-1]
    tokens = row_weights.shape[0] // ep_count
    row_count = tokens // blocks
    wide = (tokens, payloads[0].shape[1])
    row = lax.broadcasted_iota(jnp.int32, wide, 0)
    token = row % row_count
    for spot, piece in enumerate(piece_order(blocks)):
        token = token + jnp.where(row // row_count == spot, (place[1] ^ piece) * row_count, 0)
    here = lax.broadcasted_iota(jnp.int32, wide, 1) == token
    for step, payload in enumerate(payloads):
        parts = payload[weight_at:, :].astype(jnp.float32)
        part_row = lax.broadcasted_iota(jnp.int32, parts.shape, 0)
        chosen = (part_row % ep_count == place[0]) & (part_row < 3 * ep_count)
        by_token = jnp.sum(jnp.where(chosen, parts, 0.0), axis=0, keepdims=True)
        column = jnp.sum(jnp.where(here, by_token, 0.0), axis=1, keepdims=True)
        row_weights[step * tokens : (step + 1) * tokens, :] = jnp.broadcast_to(column, (tokens, HD))


def prepare_call(place, arrived, after, blocks, tokens, weight_at):
    ep_count = len(arrived)
    return pl.pallas_call(
        lambda *refs: prepare_kernel(ep_count, blocks, weight_at, *refs),
        out_shape=jax.ShapeDtypeStruct((ep_count * tokens, HD), jnp.float32),
        in_specs=[SCALARS] + [WHOLE] * ep_count + [ANYWHERE],
        out_specs=WHOLE,
        compiler_params=pltpu.CompilerParams(vmem_limit_bytes=VMEM_LIMIT),
        cost_estimate=EXPERT_COST,
        name="prepare",
    )(place, *arrived, after)


def attend_kernel(ep_count, held, tokens, row_blocks, all_open, lens, place, counts, owners, queries, *refs):
    blocks = refs[:ep_count]
    out_weight = refs[ep_count]
    kept_ref, sent_ref, pages_ref = refs[ep_count + 1 : ep_count + 4]
    scores, projected, ranks = refs[ep_count + 4 :]
    heads = queries.shape[1] // HD
    ep_index = place[0]
    block_index = place[1]
    suffix = ep_count * tokens

    page_count = owners.shape[0]
    pages_here = page_count // ep_count
    page_size = tokens // pages_here

    def rank_of(page, earlier):
        ranks[page] = earlier
        return earlier + (owners[page] == ep_index).astype(jnp.int32)

    lax.fori_loop(0, page_count, rank_of, jnp.int32(0))
    pages_ref[...] = jnp.zeros_like(pages_ref)
    for step in range(ep_count):
        source = ep_index ^ step
        for k in range(pages_here):
            page = source * pages_here + k

            @pl.when(owners[page] == ep_index)
            def _(step=step, source=source, k=k, page=page):
                first = held + k * page_size
                entries = blocks[step][first : first + page_size, :]
                row = lax.broadcasted_iota(jnp.int32, entries.shape, 0) + k * page_size
                entries = jnp.where(row < lens[source], entries.astype(jnp.float32), 0.0)
                at = pl.multiple_of(ranks[page] * page_size, page_size)
                pages_ref[pl.ds(at, page_size), :] = entries.astype(jnp.bfloat16)

    own_start = jnp.int32(0)
    for j in range(ep_count):
        own_start = own_start + jnp.where(j < ep_index, lens[j], 0)
    column = lax.broadcasted_iota(jnp.int32, (tokens, suffix), 1)
    slot = column % tokens
    query_position = own_start + lax.broadcasted_iota(jnp.int32, (tokens, suffix), 0)
    seen = jnp.zeros((tokens, suffix), jnp.int32)
    for step in range(ep_count):
        source = ep_index ^ step
        start = jnp.int32(0)
        for j in range(ep_count):
            start = start + jnp.where(j < source, lens[j], 0)
        last = jnp.minimum(query_position - start, lens[source] - 1)
        here = (column // tokens == step) & (slot <= last)
        seen = seen + here.astype(jnp.int32)
    bias = jnp.where(seen > 0, 0.0, MASKED)

    suffix_keys = jnp.concatenate([block[held : held + tokens, :HD] for block in blocks], axis=0)
    suffix_values = jnp.concatenate([block[held : held + tokens, HD:] for block in blocks], axis=0)
    scale = math.log2(math.e) / math.sqrt(HD)
    rows = min(ROWS, heads * tokens)
    together = rows // tokens
    attended = []
    for first in range(0, heads, together):
        grouped = jnp.concatenate(
            [queries[:, h * HD : (h + 1) * HD] for h in range(first, first + together)], axis=0
        )
        highest = None
        for step in range(ep_count):
            part = scale * lax.dot_general(
                grouped, blocks[step][:held, :HD], TRANSPOSED, preferred_element_type=jnp.float32
            )
            if not all_open:
                entry = lax.broadcasted_iota(jnp.int32, part.shape, 1)
                part = jnp.where(entry < counts[step], part, MASKED)
            scores[:, step * held : (step + 1) * held] = part
            top = jnp.max(part, axis=1, keepdims=True)
            highest = top if highest is None else jnp.maximum(highest, top)
        part = scale * lax.dot_general(
            grouped, suffix_keys, TRANSPOSED, preferred_element_type=jnp.float32
        )
        part = part + jnp.concatenate([bias] * together, axis=0)
        highest = jnp.maximum(highest, jnp.max(part, axis=1, keepdims=True))
        part = jnp.exp2(part - highest)
        total = jnp.sum(part, axis=1, keepdims=True)
        mixed = jnp.dot(
            part.astype(jnp.bfloat16), suffix_values, preferred_element_type=jnp.float32
        )
        for step in range(ep_count):
            part = jnp.exp2(scores[:, step * held : (step + 1) * held] - highest)
            total += jnp.sum(part, axis=1, keepdims=True)
            mixed += jnp.dot(
                part.astype(jnp.bfloat16),
                blocks[step][:held, HD:],
                preferred_element_type=jnp.float32,
            )
        mixed = (mixed / total).astype(jnp.bfloat16)
        attended += [mixed[h * tokens : (h + 1) * tokens] for h in range(together)]
    attended = jnp.concatenate(attended, axis=1)
    for at in range(0, out_weight.shape[1], COLUMNS):
        projected[:, at : at + COLUMNS] = jnp.dot(
            attended, out_weight[:, at : at + COLUMNS], preferred_element_type=jnp.float32
        )
    count = tokens // row_blocks
    for spot, piece in enumerate(piece_order(row_blocks)):
        rows = projected[pl.ds(pl.multiple_of((block_index ^ piece) * count, count), count), :]
        ref, spot = (kept_ref, spot) if 2 * spot < row_blocks else (sent_ref, spot - row_blocks // 2)
        ref[spot * count : (spot + 1) * count, :] = rows.astype(ref.dtype)


def attend_call(
    lens, place, counts, owners, queries, arrived, out_weight, held, blocks, own_most, all_open
):
    tokens = queries.shape[0]
    ep_count = len(arrived)
    model_width = out_weight.shape[1]
    heads = queries.shape[1] // HD
    keys = ep_count * (held + tokens)
    page_size = tokens * ep_count // owners.shape[0]
    return pl.pallas_call(
        lambda *refs: attend_kernel(ep_count, held, tokens, blocks, all_open, *refs),
        out_shape=[
            jax.ShapeDtypeStruct((tokens // 2, model_width), jnp.float32),
            jax.ShapeDtypeStruct((tokens // 2, model_width), jnp.bfloat16),
            jax.ShapeDtypeStruct((own_most * page_size, 2 * HD), jnp.bfloat16),
        ],
        in_specs=[SCALARS] * 4 + [WHOLE] * (ep_count + 2),
        out_specs=[WHOLE] * 3,
        scratch_shapes=[
            pltpu.VMEM((min(ROWS, heads * tokens), ep_count * held), jnp.float32),
            pltpu.VMEM((tokens, model_width), jnp.float32),
            pltpu.SMEM((owners.shape[0],), jnp.int32),
        ],
        compiler_params=pltpu.CompilerParams(vmem_limit_bytes=VMEM_LIMIT),
        cost_estimate=pl.CostEstimate(
            flops=4 * heads * tokens * keys * HD + 2 * tokens * heads * HD * model_width,
            bytes_accessed=2 * heads * HD * model_width,
            transcendentals=heads * tokens * keys,
        ),
        name="attend",
    )(lens, place, counts, owners, queries, *arrived, out_weight)


def expert_kernel(count, steps, blocks, row_weights, *refs):
    row_refs = refs[:count]
    gate_up, down_weight = refs[count : count + 2]
    kept_ref, sent_ref = refs[-2:]
    tokens = 2 * kept_ref.shape[0] // len(steps)
    row_count = tokens // blocks
    row_weight = jnp.concatenate(
        [
            row_weights[step * tokens + spot * row_count : step * tokens + (spot + 1) * row_count, :1]
            for spot in range(blocks)
            for step in steps
        ],
        axis=0,
    )
    gate_part = up_part = 0.0
    for at in range(0, kept_ref.shape[1], COLUMNS):
        rows = jnp.concatenate([ref[:, at : at + COLUMNS] for ref in row_refs], axis=0)
        gate_part += lax.dot_general(
            rows, gate_up[0, 0, :, at : at + COLUMNS], TRANSPOSED, preferred_element_type=jnp.float32
        )
        up_part += lax.dot_general(
            rows, gate_up[0, 1, :, at : at + COLUMNS], TRANSPOSED, preferred_element_type=jnp.float32
        )
    hidden = gate_part / (1.0 + jnp.exp(-gate_part)) * up_part
    hidden = (hidden * row_weight).astype(jnp.bfloat16)
    half = kept_ref.shape[0]
    for at in range(0, kept_ref.shape[1], COLUMNS):
        out = jnp.dot(
            hidden, down_weight[0, :, at : at + COLUMNS], preferred_element_type=jnp.float32
        ).astype(jnp.bfloat16)
        kept_ref[:, at : at + COLUMNS] = out[:half]
        sent_ref[:, at : at + COLUMNS] = out[half:]


def expert_call(steps, blocks, row_weights, have, gate_up, down_weight, after):
    if have[0].shape[0] % 16:
        have = [jnp.concatenate(have, axis=0)]
    tokens = sum(piece.shape[0] for piece in have)
    model_width = have[0].shape[1]
    hidden_units = down_weight.shape[1]
    half = jax.ShapeDtypeStruct((tokens // 2, model_width), jnp.bfloat16)
    return pl.pallas_call(
        lambda *refs: expert_kernel(len(have), steps, blocks, *refs),
        out_shape=(half, half),
        in_specs=[WHOLE] * (len(have) + 3) + [ANYWHERE] * len(after),
        out_specs=(WHOLE, WHOLE),
        compiler_params=pltpu.CompilerParams(vmem_limit_bytes=VMEM_LIMIT),
        cost_estimate=EXPERT_COST,
        name="experts",
    )(row_weights, *have, gate_up, down_weight, *after)


def local(
    queries,
    new_kv,
    cache_pool,
    hit_pages,
    span_lengths,
    out_weight,
    hidden_in,
    norm_gain,
    expert_ids,
    gate_weights,
    gate_up,
    down_weight,
    new_owner,
):
    tokens = queries.shape[0]
    model_width = hidden_in.shape[1]
    ep_count = lax.axis_size("ep")
    tp_count = lax.axis_size("tp")
    blocks = lax.axis_size("kv") * tp_count
    ep_index = lax.axis_index("ep")
    kv_index = lax.axis_index("kv")
    tp_index = lax.axis_index("tp")
    block_index = kv_index * tp_count + tp_index
    keyval_local = new_kv.shape[1]
    heads_local = queries.shape[1] // HD
    keyval_pick = block_index * heads_local // (HQ // KVH) - kv_index * keyval_local
    row_count = tokens // blocks
    pool_pages = cache_pool.shape[0]
    page_size = cache_pool.shape[1]
    held = HOLD_MOST * page_size

    hits = hit_pages.shape[0]
    here_page = lax.optimization_barrier(hit_pages - ep_index * pool_pages)
    owned_hits = (here_page >= 0) & (here_page < pool_pages)
    earlier = jnp.arange(hits)[None, :] < jnp.arange(hits)[:, None]
    hit_rank = jnp.sum((earlier & owned_hits[None, :]).astype(jnp.int32), axis=1)
    hit_pick = owned_hits[None, :] & (
        hit_rank[None, :] == jnp.arange(HOLD_MOST, dtype=jnp.int32)[:, None]
    )
    local_page = jnp.sum(jnp.where(hit_pick, here_page[None, :], 0), axis=1)
    chosen = cache_pool.at[local_page].get(mode="promise_in_bounds")
    own_pages = lax.dynamic_index_in_dim(chosen, keyval_pick, 2, keepdims=False).reshape(held, 2 * HD)
    own_suffix = lax.dynamic_index_in_dim(new_kv, keyval_pick, 1, keepdims=False)

    by_expert = jnp.sum(
        jnp.where(
            expert_ids[:, :, None] == jnp.arange(ep_count, dtype=jnp.int32)[None, None, :],
            gate_weights[:, :, None],
            0.0,
        ),
        axis=1,
    )
    weight_part = jnp.concatenate(three_parts(by_expert.T), axis=0)
    weight_rows = weight_part.shape[0]
    weight_part = jnp.pad(
        weight_part, ((0, -weight_rows % WEIGHT_ROWS), (0, 2 * HD - weight_part.shape[1]))
    )
    payload = jnp.concatenate([own_pages, own_suffix, weight_part], axis=0)
    arrived = [payload]
    for step in range(1, ep_count):
        arrived.append(
            lax.ppermute(payload, "ep", [(i, i ^ step) for i in range(ep_count)])
        )
    sources = [ep_index ^ step for step in range(ep_count)]

    all_open = hits == HOLD_MOST * ep_count
    holder = hit_pages // pool_pages
    counts = jnp.sum(
        (holder[None, :] == jnp.stack(sources)[:, None]).astype(jnp.int32) * page_size, axis=1
    )
    if all_open:
        counts = jnp.zeros((1,), jnp.int32)
    place = jnp.stack([ep_index, block_index]).astype(jnp.int32)
    exchange = lambda value, bit: lax.ppermute(
        value, ("kv", "tp"), [(i, i ^ bit) for i in range(blocks)]
    )
    across = lambda value, step: lax.ppermute(
        value, "ep", [(i, i ^ step) for i in range(ep_count)]
    )
    bits = [1 << place for place in range(1, blocks.bit_length() - 1)]

    def scatter(kept, sent):
        got = received = exchange(sent, 1)
        gives = []
        for bit in reversed(bits):
            half = kept.shape[0] // 2
            give = kept[half:].astype(jnp.float32) + got[half:].astype(jnp.float32)
            gives.append(give.astype(jnp.bfloat16))
            kept = kept[:half].astype(jnp.float32) + got[:half].astype(jnp.float32)
            got = exchange(gives[-1], bit)
        return kept.astype(jnp.float32) + got.astype(jnp.float32), gives, received

    own_most = 2 * (tokens // page_size)
    own_slots = block_index * row_count + jnp.arange(row_count, dtype=jnp.int32)
    rows_filled = own_slots < span_lengths[ep_index]
    core = jnp.broadcast_to(tp_index.astype(jnp.int32), (1, 1, 2 * HD))
    core, row_mask = lax.optimization_barrier((core, rows_filled.astype(jnp.int32)))
    own_hidden = lax.dynamic_slice_in_dim(hidden_in, block_index * row_count, row_count, 0)
    held_out, held_gate_up, held_down, _ = hold_call(
        [out_weight, gate_up, down_weight], payload, place, row_mask, core, own_hidden
    )
    kept, sent, head_pages = attend_call(
        span_lengths,
        place,
        counts,
        new_owner,
        queries,
        arrived,
        held_out,
        held,
        blocks,
        own_most,
        all_open,
    )
    head_pages = head_pages.reshape(own_most, page_size, 2 * HD)
    heads_out, _, _ = scatter(kept, sent)
    residual = (own_hidden.astype(jnp.float32) + heads_out).astype(jnp.bfloat16)
    resid_wide = residual.astype(jnp.float32)
    normed = (
        resid_wide
        * lax.rsqrt(jnp.mean(resid_wide * resid_wide, axis=1, keepdims=True) + EPSILON)
        * norm_gain
    ).astype(jnp.bfloat16)

    def group_rows(have, bits, before=None):
        for bit in bits:
            have = have + [exchange(part, bit) for part in have]
            if before is not None and len(have) == 2:
                have[1], before = lax.optimization_barrier([have[1], before])
        return have

    row_weights = prepare_call(place, arrived, normed, blocks, tokens, held + tokens)
    ep_bits = [1 << place for place in reversed(range(ep_count.bit_length() - 1))]
    early = [exchange(normed, bit) for bit in bits + [1]]
    direct = [across(normed, bit) for bit in ep_bits]
    row_weights, *tied = lax.optimization_barrier([row_weights] + early + direct)
    early, direct = tied[: len(early)], dict(zip(ep_bits, tied[len(early) :]))
    crossed = {0: normed}
    for bit in ep_bits:
        for step in list(crossed):
            crossed[step ^ bit] = across(crossed[step], bit) if step else direct[bit]
    leading = ep_bits[0]
    forwarded = [step for step in crossed if step & (step - 1)]
    lead_have = group_rows([crossed[leading]], bits[:1])
    lead_have[1:], ahead = lax.optimization_barrier(
        (lead_have[1:], [crossed[step] for step in forwarded])
    )
    crossed.update(zip(forwarded, ahead))
    lead_have = group_rows(lead_have, bits[1:] + [1])
    own_have = [normed]
    for bit, piece in zip(bits + [1], early):
        own_have += [piece] + [exchange(part, bit) for part in own_have[1:]]

    groups = [[step] for step in [ep_count // 2] + [step for step in reversed(range(1, ep_count)) if step != ep_count // 2] + [0]]
    sums = {}
    sent, given, finished = None, [], []
    for turn, group in enumerate(groups):
        after = [sent] if turn >= 1 else []
        after += given[turn - 2 : turn] if turn >= 2 else []
        if turn == len(groups) - 1:
            after += finished[: turn - 1]
        haves = {0: own_have, leading: lead_have}
        for step in group:
            if step not in haves:
                piece = crossed[step]
                if turn > 1 and bits:
                    piece, reached = lax.optimization_barrier((piece, reached))
                haves[step] = group_rows([piece], bits + [1], sent if turn == 1 else received)
                reached = haves[step][1]
        have = [haves[step][spot] for spot in range(blocks) for step in group]
        kept, sent = expert_call(
            tuple(group), blocks, row_weights, have, held_gate_up, held_down, after
        )
        own, gives, received = scatter(kept, sent)
        given.append(gives[0] if gives else own.astype(jnp.bfloat16))
        finished.append(own.astype(jnp.bfloat16))
        for spot, step in enumerate(group):
            sums[step] = own[spot * row_count : (spot + 1) * row_count]
    mixture = resid_wide
    for step, own in sums.items():
        if step:
            own = across(own.astype(jnp.bfloat16), step).astype(jnp.float32)
        mixture = mixture + own
    layer_out = jnp.where(row_mask[:, None] > 0, mixture, 0.0).astype(jnp.bfloat16)

    if keyval_local == 1:
        decode_pages = head_pages[:, :, None, :]
    else:
        other = lax.ppermute(head_pages, "tp", [(i, i ^ 1) for i in range(tp_count)])
        first = core == 0
        decode_pages = jnp.stack(
            [jnp.where(first, head_pages, other), jnp.where(first, other, head_pages)], axis=2
        )
    return (layer_out, decode_pages)


def solution(mesh):
    placed = (
        P(("groups", "ep"), ("kv", "tp")),
        P(("groups", "ep"), "kv", None),
        P(("groups", "ep"), None, "kv", None),
        P("groups"),
        P("groups"),
        P(("kv", "tp"), None),
        P(("groups", "ep"), None),
        P(),
        P(("groups", "ep"), None),
        P(("groups", "ep"), None),
        P("ep", None, ("kv", "tp"), None),
        P("ep", ("kv", "tp"), None),
        P("groups"),
    )
    return jax.shard_map(
        local,
        mesh=mesh,
        in_specs=placed,
        out_specs=(P(("groups", "ep", "kv", "tp"), None), P(("groups", "ep"), None, "kv", None)),
        check_vma=False,
    )
```

```python
import math

import jax
import jax.numpy as jnp
from jax import lax
from jax.experimental import pallas as pl
from jax.experimental.pallas import tpu as pltpu
from jax.sharding import PartitionSpec as P

HD = 128
HQ = 32
KVH = 4
HOLD_MOST = 16
WEIGHT_ROWS = 16

MASKED = -1e30
EPSILON = 1e-06


def three_parts(wide):
    high = lax.reduce_precision(wide, 8, 7)
    rest = wide - high
    middle = lax.reduce_precision(rest, 8, 7)
    low = rest - middle
    return [part.astype(jnp.bfloat16) for part in (high, middle, low)]


def piece_order(blocks):
    order = [0]
    bit = 2
    while bit < blocks:
        order += [piece ^ bit for piece in order]
        bit *= 2
    return order + [piece ^ 1 for piece in order]


TRANSPOSED = (((1,), (1,)), ((), ()))
WHOLE = pl.BlockSpec(memory_space=pltpu.VMEM)
ANYWHERE = pl.BlockSpec(memory_space=pl.ANY)
SCALARS = pl.BlockSpec(memory_space=pltpu.SMEM)
COLUMNS = 1024
ROWS = 256
VMEM_LIMIT = 16 * 2**20
EXPERT_COST = pl.CostEstimate(flops=1024, bytes_accessed=1024, transcendentals=0)


def hold_kernel(count, *refs):
    sources, held, token, sem = refs[:count], refs[-2 - count : -2], refs[-2], refs[-1]
    token[...] = jnp.zeros_like(token)
    copies = [
        pltpu.make_async_copy(source, target, sem.at[i])
        for i, (source, target) in enumerate(zip(sources, held))
    ]
    for copy in copies:
        copy.start()
    for copy in copies:
        copy.wait()


def hold_call(arrays, *after):
    size = sum(math.prod(array.shape) * 2 for array in arrays)
    return pl.pallas_call(
        lambda *refs: hold_kernel(len(arrays), *refs),
        out_shape=[jax.ShapeDtypeStruct(array.shape, array.dtype) for array in arrays]
        + [jax.ShapeDtypeStruct((8, 128), jnp.float32)],
        in_specs=[ANYWHERE] * (len(arrays) + len(after)),
        out_specs=[WHOLE] * (len(arrays) + 1),
        scratch_shapes=[pltpu.SemaphoreType.DMA((len(arrays),))],
        compiler_params=pltpu.CompilerParams(vmem_limit_bytes=VMEM_LIMIT),
        cost_estimate=pl.CostEstimate(flops=0, bytes_accessed=2 * size, transcendentals=0),
        name="hold",
    )(*arrays, *after)


def normalize_kernel(kept, got, hidden, gain, residual, normed):
    wide = hidden[...].astype(jnp.float32) + (kept[...] + got[...].astype(jnp.float32))
    residual[...] = wide.astype(jnp.bfloat16)
    wide = residual[...].astype(jnp.float32)
    square = jnp.mean(wide * wide, axis=1, keepdims=True)
    normed[...] = (wide * lax.rsqrt(square + EPSILON) * gain[...]).astype(jnp.bfloat16)


def normalize_call(kept, got, hidden, gain):
    rows = jax.ShapeDtypeStruct(hidden.shape, jnp.bfloat16)
    return pl.pallas_call(
        normalize_kernel,
        out_shape=[rows, rows],
        in_specs=[WHOLE] * 4,
        out_specs=[WHOLE] * 2,
        compiler_params=pltpu.CompilerParams(vmem_limit_bytes=VMEM_LIMIT),
        cost_estimate=EXPERT_COST,
        name="normalize",
    )(kept, got, hidden, gain)


def prepare_kernel(ep_count, blocks, weight_at, lens, owners, place, *refs):
    payloads = refs[:ep_count]
    row_weights, pages_ref, ranks = refs[-3:]
    tokens = row_weights.shape[0] // ep_count
    row_count = tokens // blocks
    wide = (tokens, payloads[0].shape[1])
    row = lax.broadcasted_iota(jnp.int32, wide, 0)
    token = row % row_count
    for spot, piece in enumerate(piece_order(blocks)):
        token = token + jnp.where(row // row_count == spot, (place[1] ^ piece) * row_count, 0)
    here = lax.broadcasted_iota(jnp.int32, wide, 1) == token
    for step, payload in enumerate(payloads):
        parts = payload[weight_at:, :].astype(jnp.float32)
        part_row = lax.broadcasted_iota(jnp.int32, parts.shape, 0)
        chosen = (part_row % ep_count == place[0]) & (part_row < 3 * ep_count)
        by_token = jnp.sum(jnp.where(chosen, parts, 0.0), axis=0, keepdims=True)
        column = jnp.sum(jnp.where(here, by_token, 0.0), axis=1, keepdims=True)
        row_weights[step * tokens : (step + 1) * tokens, :] = jnp.broadcast_to(column, (tokens, HD))

    ep_index = place[0]
    page_count = owners.shape[0]
    pages_here = page_count // ep_count
    page_size = tokens // pages_here

    def rank_of(page, earlier):
        ranks[page] = earlier
        return earlier + (owners[page] == ep_index).astype(jnp.int32)

    lax.fori_loop(0, page_count, rank_of, jnp.int32(0))
    pages_ref[...] = jnp.zeros_like(pages_ref)
    for step in range(ep_count):
        source = ep_index ^ step
        for k in range(pages_here):
            page = source * pages_here + k

            @pl.when(owners[page] == ep_index)
            def _(step=step, source=source, k=k, page=page):
                first = weight_at - tokens + k * page_size
                entries = payloads[step][first : first + page_size, :]
                row = lax.broadcasted_iota(jnp.int32, entries.shape, 0) + k * page_size
                entries = jnp.where(row < lens[source], entries.astype(jnp.float32), 0.0)
                at = pl.multiple_of(ranks[page] * page_size, page_size)
                pages_ref[pl.ds(at, page_size), :] = entries.astype(jnp.bfloat16)


def prepare_call(lens, owners, place, arrived, after, blocks, tokens, weight_at, own_most):
    ep_count = len(arrived)
    page_size = tokens * ep_count // owners.shape[0]
    return pl.pallas_call(
        lambda *refs: prepare_kernel(ep_count, blocks, weight_at, *refs),
        out_shape=[
            jax.ShapeDtypeStruct((ep_count * tokens, HD), jnp.float32),
            jax.ShapeDtypeStruct((own_most * page_size, 2 * HD), jnp.bfloat16),
        ],
        in_specs=[SCALARS] * 3 + [WHOLE] * ep_count + [ANYWHERE],
        out_specs=[WHOLE] * 2,
        scratch_shapes=[pltpu.SMEM((owners.shape[0],), jnp.int32)],
        compiler_params=pltpu.CompilerParams(vmem_limit_bytes=VMEM_LIMIT),
        cost_estimate=EXPERT_COST,
        name="prepare",
    )(lens, owners, place, *arrived, after)


def attend_kernel(ep_count, held, tokens, row_blocks, all_open, lens, place, counts, queries, *refs):
    blocks = refs[:ep_count]
    out_weight = refs[ep_count]
    kept_ref, sent_ref = refs[ep_count + 1 : ep_count + 3]
    scores, projected = refs[ep_count + 3 :]
    heads = queries.shape[1] // HD
    ep_index = place[0]
    block_index = place[1]
    suffix = ep_count * tokens

    own_start = jnp.int32(0)
    for j in range(ep_count):
        own_start = own_start + jnp.where(j < ep_index, lens[j], 0)
    column = lax.broadcasted_iota(jnp.int32, (tokens, suffix), 1)
    slot = column % tokens
    query_position = own_start + lax.broadcasted_iota(jnp.int32, (tokens, suffix), 0)
    seen = jnp.zeros((tokens, suffix), jnp.int32)
    for step in range(ep_count):
        source = ep_index ^ step
        start = jnp.int32(0)
        for j in range(ep_count):
            start = start + jnp.where(j < source, lens[j], 0)
        last = jnp.minimum(query_position - start, lens[source] - 1)
        here = (column // tokens == step) & (slot <= last)
        seen = seen + here.astype(jnp.int32)
    bias = jnp.where(seen > 0, 0.0, MASKED)

    suffix_keys = jnp.concatenate([block[held : held + tokens, :HD] for block in blocks], axis=0)
    suffix_values = jnp.concatenate([block[held : held + tokens, HD:] for block in blocks], axis=0)
    scale = math.log2(math.e) / math.sqrt(HD)
    rows = min(ROWS, heads * tokens)
    together = rows // tokens
    attended = []
    for first in range(0, heads, together):
        grouped = jnp.concatenate(
            [queries[:, h * HD : (h + 1) * HD] for h in range(first, first + together)], axis=0
        )
        highest = None
        for step in range(ep_count):
            part = scale * lax.dot_general(
                grouped, blocks[step][:held, :HD], TRANSPOSED, preferred_element_type=jnp.float32
            )
            if not all_open:
                entry = lax.broadcasted_iota(jnp.int32, part.shape, 1)
                part = jnp.where(entry < counts[step], part, MASKED)
            scores[:, step * held : (step + 1) * held] = part
            top = jnp.max(part, axis=1, keepdims=True)
            highest = top if highest is None else jnp.maximum(highest, top)
        part = scale * lax.dot_general(
            grouped, suffix_keys, TRANSPOSED, preferred_element_type=jnp.float32
        )
        part = part + jnp.concatenate([bias] * together, axis=0)
        highest = jnp.maximum(highest, jnp.max(part, axis=1, keepdims=True))
        part = jnp.exp2(part - highest)
        total = jnp.sum(part, axis=1, keepdims=True)
        mixed = jnp.dot(
            part.astype(jnp.bfloat16), suffix_values, preferred_element_type=jnp.float32
        )
        for step in range(ep_count):
            part = jnp.exp2(scores[:, step * held : (step + 1) * held] - highest)
            total += jnp.sum(part, axis=1, keepdims=True)
            mixed += jnp.dot(
                part.astype(jnp.bfloat16),
                blocks[step][:held, HD:],
                preferred_element_type=jnp.float32,
            )
        mixed = (mixed / total).astype(jnp.bfloat16)
        attended += [mixed[h * tokens : (h + 1) * tokens] for h in range(together)]
    attended = jnp.concatenate(attended, axis=1)
    for at in range(0, out_weight.shape[1], COLUMNS):
        projected[:, at : at + COLUMNS] = jnp.dot(
            attended, out_weight[:, at : at + COLUMNS], preferred_element_type=jnp.float32
        )
    count = tokens // row_blocks
    for spot, piece in enumerate(piece_order(row_blocks)):
        rows = projected[pl.ds(pl.multiple_of((block_index ^ piece) * count, count), count), :]
        ref, spot = (kept_ref, spot) if 2 * spot < row_blocks else (sent_ref, spot - row_blocks // 2)
        ref[spot * count : (spot + 1) * count, :] = rows.astype(ref.dtype)


def attend_call(
    lens, place, counts, queries, arrived, out_weight, held, blocks, all_open
):
    tokens = queries.shape[0]
    ep_count = len(arrived)
    model_width = out_weight.shape[1]
    heads = queries.shape[1] // HD
    keys = ep_count * (held + tokens)
    return pl.pallas_call(
        lambda *refs: attend_kernel(ep_count, held, tokens, blocks, all_open, *refs),
        out_shape=[
            jax.ShapeDtypeStruct((tokens // 2, model_width), jnp.float32),
            jax.ShapeDtypeStruct((tokens // 2, model_width), jnp.bfloat16),
        ],
        in_specs=[SCALARS] * 3 + [WHOLE] * (ep_count + 2),
        out_specs=[WHOLE] * 2,
        scratch_shapes=[
            pltpu.VMEM((min(ROWS, heads * tokens), ep_count * held), jnp.float32),
            pltpu.VMEM((tokens, model_width), jnp.float32),
        ],
        compiler_params=pltpu.CompilerParams(vmem_limit_bytes=VMEM_LIMIT),
        cost_estimate=pl.CostEstimate(
            flops=4 * heads * tokens * keys * HD + 2 * tokens * heads * HD * model_width,
            bytes_accessed=2 * heads * HD * model_width,
            transcendentals=heads * tokens * keys,
        ),
        name="attend",
    )(lens, place, counts, queries, *arrived, out_weight)


def expert_kernel(count, steps, blocks, row_weights, *refs):
    row_refs = refs[:count]
    gate_up, down_weight = refs[count : count + 2]
    kept_ref, sent_ref = refs[-2:]
    tokens = 2 * kept_ref.shape[0] // len(steps)
    row_count = tokens // blocks
    row_weight = jnp.concatenate(
        [
            row_weights[step * tokens + spot * row_count : step * tokens + (spot + 1) * row_count, :1]
            for spot in range(blocks)
            for step in steps
        ],
        axis=0,
    )
    gate_part = up_part = 0.0
    for at in range(0, kept_ref.shape[1], COLUMNS):
        rows = jnp.concatenate([ref[:, at : at + COLUMNS] for ref in row_refs], axis=0)
        gate_part += lax.dot_general(
            rows, gate_up[0, 0, :, at : at + COLUMNS], TRANSPOSED, preferred_element_type=jnp.float32
        )
        up_part += lax.dot_general(
            rows, gate_up[0, 1, :, at : at + COLUMNS], TRANSPOSED, preferred_element_type=jnp.float32
        )
    hidden = gate_part / (1.0 + jnp.exp(-gate_part)) * up_part
    hidden = (hidden * row_weight).astype(jnp.bfloat16)
    half = kept_ref.shape[0]
    for at in range(0, kept_ref.shape[1], COLUMNS):
        out = jnp.dot(
            hidden, down_weight[0, :, at : at + COLUMNS], preferred_element_type=jnp.float32
        ).astype(jnp.bfloat16)
        kept_ref[:, at : at + COLUMNS] = out[:half]
        sent_ref[:, at : at + COLUMNS] = out[half:]


def expert_call(steps, blocks, row_weights, have, gate_up, down_weight, after):
    if have[0].shape[0] % 16:
        have = [jnp.concatenate(have, axis=0)]
    tokens = sum(piece.shape[0] for piece in have)
    model_width = have[0].shape[1]
    hidden_units = down_weight.shape[1]
    half = jax.ShapeDtypeStruct((tokens // 2, model_width), jnp.bfloat16)
    return pl.pallas_call(
        lambda *refs: expert_kernel(len(have), steps, blocks, *refs),
        out_shape=(half, half),
        in_specs=[WHOLE] * (len(have) + 3) + [ANYWHERE] * len(after),
        out_specs=(WHOLE, WHOLE),
        compiler_params=pltpu.CompilerParams(vmem_limit_bytes=VMEM_LIMIT),
        cost_estimate=EXPERT_COST,
        name="experts",
    )(row_weights, *have, gate_up, down_weight, *after)


def local(
    queries,
    new_kv,
    cache_pool,
    hit_pages,
    span_lengths,
    out_weight,
    hidden_in,
    norm_gain,
    expert_ids,
    gate_weights,
    gate_up,
    down_weight,
    new_owner,
):
    tokens = queries.shape[0]
    model_width = hidden_in.shape[1]
    ep_count = lax.axis_size("ep")
    tp_count = lax.axis_size("tp")
    blocks = lax.axis_size("kv") * tp_count
    ep_index = lax.axis_index("ep")
    kv_index = lax.axis_index("kv")
    tp_index = lax.axis_index("tp")
    block_index = kv_index * tp_count + tp_index
    keyval_local = new_kv.shape[1]
    heads_local = queries.shape[1] // HD
    keyval_pick = block_index * heads_local // (HQ // KVH) - kv_index * keyval_local
    row_count = tokens // blocks
    pool_pages = cache_pool.shape[0]
    page_size = cache_pool.shape[1]
    held = HOLD_MOST * page_size

    hits = hit_pages.shape[0]
    here_page = lax.optimization_barrier(hit_pages - ep_index * pool_pages)
    owned_hits = (here_page >= 0) & (here_page < pool_pages)
    earlier = jnp.arange(hits)[None, :] < jnp.arange(hits)[:, None]
    hit_rank = jnp.sum((earlier & owned_hits[None, :]).astype(jnp.int32), axis=1)
    hit_pick = owned_hits[None, :] & (
        hit_rank[None, :] == jnp.arange(HOLD_MOST, dtype=jnp.int32)[:, None]
    )
    local_page = jnp.sum(jnp.where(hit_pick, here_page[None, :], 0), axis=1)
    chosen = cache_pool.at[local_page].get(mode="promise_in_bounds")
    own_pages = lax.dynamic_index_in_dim(chosen, keyval_pick, 2, keepdims=False).reshape(held, 2 * HD)
    own_suffix = lax.dynamic_index_in_dim(new_kv, keyval_pick, 1, keepdims=False)

    by_expert = jnp.sum(
        jnp.where(
            expert_ids[:, :, None] == jnp.arange(ep_count, dtype=jnp.int32)[None, None, :],
            gate_weights[:, :, None],
            0.0,
        ),
        axis=1,
    )
    weight_part = jnp.concatenate(three_parts(by_expert.T), axis=0)
    weight_rows = weight_part.shape[0]
    weight_part = jnp.pad(
        weight_part, ((0, -weight_rows % WEIGHT_ROWS), (0, 2 * HD - weight_part.shape[1]))
    )
    payload = jnp.concatenate([own_pages, own_suffix, weight_part], axis=0)
    arrived = [payload]
    for step in range(1, ep_count):
        arrived.append(
            lax.ppermute(payload, "ep", [(i, i ^ step) for i in range(ep_count)])
        )
    sources = [ep_index ^ step for step in range(ep_count)]

    all_open = hits == HOLD_MOST * ep_count
    holder = hit_pages // pool_pages
    counts = jnp.sum(
        (holder[None, :] == jnp.stack(sources)[:, None]).astype(jnp.int32) * page_size, axis=1
    )
    if all_open:
        counts = jnp.zeros((1,), jnp.int32)
    place = jnp.stack([ep_index, block_index]).astype(jnp.int32)
    exchange = lambda value, bit: lax.ppermute(
        value, ("kv", "tp"), [(i, i ^ bit) for i in range(blocks)]
    )
    across = lambda value, step: lax.ppermute(
        value, "ep", [(i, i ^ step) for i in range(ep_count)]
    )
    bits = [1 << place for place in range(1, blocks.bit_length() - 1)]

    def scatter(kept, sent):
        got = received = exchange(sent, 1)
        gives = []
        for bit in reversed(bits):
            half = kept.shape[0] // 2
            give = kept[half:].astype(jnp.float32) + got[half:].astype(jnp.float32)
            gives.append(give.astype(jnp.bfloat16))
            kept = kept[:half].astype(jnp.float32) + got[:half].astype(jnp.float32)
            got = exchange(gives[-1], bit)
        return kept.astype(jnp.float32), got, gives, received

    own_most = 2 * (tokens // page_size)
    own_slots = block_index * row_count + jnp.arange(row_count, dtype=jnp.int32)
    rows_filled = own_slots < span_lengths[ep_index]
    core = jnp.broadcast_to(tp_index.astype(jnp.int32), (1, 1, 2 * HD))
    core, row_mask = lax.optimization_barrier((core, rows_filled.astype(jnp.int32)))
    wide_gain = norm_gain[None, :]
    own_hidden = lax.dynamic_slice_in_dim(hidden_in, block_index * row_count, row_count, 0)
    held_out, held_gate_up, held_down, _ = hold_call(
        [out_weight, gate_up, down_weight], payload, place, row_mask, core, own_hidden, wide_gain
    )
    kept, sent = attend_call(
        span_lengths,
        place,
        counts,
        queries,
        arrived,
        held_out,
        held,
        blocks,
        all_open,
    )
    residual, normed = normalize_call(*scatter(kept, sent)[:2], own_hidden, wide_gain)
    resid_wide = residual.astype(jnp.float32)

    def group_rows(have, bits, before=None):
        for bit in bits:
            have = have + [exchange(part, bit) for part in have]
            if before is not None and len(have) == 2:
                have[1], before = lax.optimization_barrier([have[1], before])
        return have

    row_weights, head_pages = prepare_call(
        span_lengths,
        new_owner,
        place,
        arrived,
        normed,
        blocks,
        tokens,
        held + tokens,
        own_most,
    )
    head_pages = head_pages.reshape(own_most, page_size, 2 * HD)
    ep_bits = [1 << place for place in reversed(range(ep_count.bit_length() - 1))]
    early = [exchange(normed, bit) for bit in bits + [1]]
    direct = [across(normed, bit) for bit in ep_bits]
    row_weights, *tied = lax.optimization_barrier([row_weights] + early + direct)
    early, direct = tied[: len(early)], dict(zip(ep_bits, tied[len(early) :]))
    crossed = {0: normed}
    for bit in ep_bits:
        for step in list(crossed):
            crossed[step ^ bit] = across(crossed[step], bit) if step else direct[bit]
    leading = ep_bits[0]
    forwarded = [step for step in crossed if step & (step - 1)]
    lead_have = group_rows([crossed[leading]], bits[:1])
    lead_have[1:], ahead = lax.optimization_barrier(
        (lead_have[1:], [crossed[step] for step in forwarded])
    )
    crossed.update(zip(forwarded, ahead))
    lead_have = group_rows(lead_have, bits[1:] + [1])
    own_have = [normed]
    for bit, piece in zip(bits + [1], early):
        own_have += [piece] + [exchange(part, bit) for part in own_have[1:]]

    groups = [[step] for step in [ep_count // 2] + [step for step in reversed(range(1, ep_count)) if step != ep_count // 2] + [0]]
    sums = {}
    sent, given, finished = None, [], []
    for turn, group in enumerate(groups):
        after = [sent] if turn >= 1 else []
        if turn == 1:
            after += []
        elif turn == len(groups) - 1:
            after += given[turn - 1 : turn]
        elif turn >= 2:
            after += given[turn - 2 : turn]
        haves = {0: own_have, leading: lead_have}
        for step in group:
            if step not in haves:
                piece = crossed[step]
                haves[step] = group_rows([piece], bits + [1], sent if turn == 1 else received)
                reached = haves[step][1]
        have = [haves[step][spot] for spot in range(blocks) for step in group]
        kept, sent = expert_call(
            tuple(group), blocks, row_weights, have, held_gate_up, held_down, after
        )
        own, got, gives, received = scatter(kept, sent)
        own = own + got.astype(jnp.float32)
        given.append(gives[0] if gives else own.astype(jnp.bfloat16))
        finished.append(own.astype(jnp.bfloat16))
        for spot, step in enumerate(group):
            sums[step] = own[spot * row_count : (spot + 1) * row_count]
    mixture = resid_wide
    for step, own in sums.items():
        if step:
            own = across(own.astype(jnp.bfloat16), step).astype(jnp.float32)
        mixture = mixture + own
    layer_out = jnp.where(row_mask[:, None] > 0, mixture, 0.0).astype(jnp.bfloat16)

    if keyval_local == 1:
        decode_pages = head_pages[:, :, None, :]
    else:
        other = lax.ppermute(head_pages, "tp", [(i, i ^ 1) for i in range(tp_count)])
        first = core == 0
        decode_pages = jnp.stack(
            [jnp.where(first, head_pages, other), jnp.where(first, other, head_pages)], axis=2
        )
    return (layer_out, decode_pages)


def solution(mesh):
    placed = (
        P(("groups", "ep"), ("kv", "tp")),
        P(("groups", "ep"), "kv", None),
        P(("groups", "ep"), None, "kv", None),
        P("groups"),
        P("groups"),
        P(("kv", "tp"), None),
        P(("groups", "ep"), None),
        P(),
        P(("groups", "ep"), None),
        P(("groups", "ep"), None),
        P("ep", None, ("kv", "tp"), None),
        P("ep", ("kv", "tp"), None),
        P("groups"),
    )
    return jax.shard_map(
        local,
        mesh=mesh,
        in_specs=placed,
        out_specs=(P(("groups", "ep", "kv", "tp"), None), P(("groups", "ep"), None, "kv", None)),
        check_vma=False,
    )
```

```python
import math

import jax
import jax.numpy as jnp
from jax import lax
from jax.experimental import pallas as pl
from jax.experimental.pallas import tpu as pltpu
from jax.sharding import PartitionSpec as P

HD = 128
HQ = 32
KVH = 4
HOLD_MOST = 16
WEIGHT_ROWS = 16

MASKED = -1e30
EPSILON = 1e-06


def three_parts(wide):
    high = lax.reduce_precision(wide, 8, 7)
    rest = wide - high
    middle = lax.reduce_precision(rest, 8, 7)
    low = rest - middle
    return [part.astype(jnp.bfloat16) for part in (high, middle, low)]


def piece_order(blocks):
    order = [0]
    bit = 2
    while bit < blocks:
        order += [piece ^ bit for piece in order]
        bit *= 2
    return order + [piece ^ 1 for piece in order]


TRANSPOSED = (((1,), (1,)), ((), ()))
WHOLE = pl.BlockSpec(memory_space=pltpu.VMEM)
ANYWHERE = pl.BlockSpec(memory_space=pl.ANY)
SCALARS = pl.BlockSpec(memory_space=pltpu.SMEM)
COLUMNS = 1024
ROWS = 256
VMEM_LIMIT = 16 * 2**20
EXPERT_COST = pl.CostEstimate(flops=1024, bytes_accessed=1024, transcendentals=0)


def hold_kernel(count, *refs):
    sources, held, token, sem = refs[:count], refs[-2 - count : -2], refs[-2], refs[-1]
    token[...] = jnp.zeros_like(token)
    copies = [
        pltpu.make_async_copy(source, target, sem.at[i])
        for i, (source, target) in enumerate(zip(sources, held))
    ]
    for copy in copies:
        copy.start()
    for copy in copies:
        copy.wait()


def hold_call(arrays, *after):
    size = sum(math.prod(array.shape) * 2 for array in arrays)
    return pl.pallas_call(
        lambda *refs: hold_kernel(len(arrays), *refs),
        out_shape=[jax.ShapeDtypeStruct(array.shape, array.dtype) for array in arrays]
        + [jax.ShapeDtypeStruct((8, 128), jnp.float32)],
        in_specs=[ANYWHERE] * (len(arrays) + len(after)),
        out_specs=[WHOLE] * (len(arrays) + 1),
        scratch_shapes=[pltpu.SemaphoreType.DMA((len(arrays),))],
        compiler_params=pltpu.CompilerParams(vmem_limit_bytes=VMEM_LIMIT),
        cost_estimate=pl.CostEstimate(flops=0, bytes_accessed=2 * size, transcendentals=0),
        name="hold",
    )(*arrays, *after)


def normalize_kernel(kept, got, hidden, gain, residual, normed):
    wide = hidden[...].astype(jnp.float32) + (kept[...] + got[...].astype(jnp.float32))
    residual[...] = wide.astype(jnp.bfloat16)
    wide = residual[...].astype(jnp.float32)
    square = jnp.mean(wide * wide, axis=1, keepdims=True)
    normed[...] = (wide * lax.rsqrt(square + EPSILON) * gain[...]).astype(jnp.bfloat16)


def normalize_call(kept, got, hidden, gain):
    rows = jax.ShapeDtypeStruct(hidden.shape, jnp.bfloat16)
    return pl.pallas_call(
        normalize_kernel,
        out_shape=[rows, rows],
        in_specs=[WHOLE] * 4,
        out_specs=[WHOLE] * 2,
        compiler_params=pltpu.CompilerParams(vmem_limit_bytes=VMEM_LIMIT),
        cost_estimate=EXPERT_COST,
        name="normalize",
    )(kept, got, hidden, gain)


def join_kernel(count, *refs):
    total = refs[0][...].astype(jnp.float32)
    for ref in refs[1:count]:
        total += ref[...].astype(jnp.float32)
    refs[-1][...] = total


def join_call(terms, after):
    return pl.pallas_call(
        lambda *refs: join_kernel(len(terms), *refs),
        out_shape=jax.ShapeDtypeStruct(terms[0].shape, jnp.float32),
        in_specs=[WHOLE] * len(terms) + [ANYWHERE] * len(after),
        out_specs=WHOLE,
        compiler_params=pltpu.CompilerParams(vmem_limit_bytes=VMEM_LIMIT),
        cost_estimate=EXPERT_COST,
        name="join",
    )(*terms, *after)


def prepare_kernel(ep_count, blocks, weight_at, lens, owners, place, *refs):
    payloads = refs[:ep_count]
    row_weights, pages_ref, ranks = refs[-3:]
    tokens = row_weights.shape[0] // ep_count
    row_count = tokens // blocks
    wide = (tokens, payloads[0].shape[1])
    row = lax.broadcasted_iota(jnp.int32, wide, 0)
    token = row % row_count
    for spot, piece in enumerate(piece_order(blocks)):
        token = token + jnp.where(row // row_count == spot, (place[1] ^ piece) * row_count, 0)
    here = lax.broadcasted_iota(jnp.int32, wide, 1) == token
    for step, payload in enumerate(payloads):
        parts = payload[weight_at:, :].astype(jnp.float32)
        part_row = lax.broadcasted_iota(jnp.int32, parts.shape, 0)
        chosen = (part_row % ep_count == place[0]) & (part_row < 3 * ep_count)
        by_token = jnp.sum(jnp.where(chosen, parts, 0.0), axis=0, keepdims=True)
        column = jnp.sum(jnp.where(here, by_token, 0.0), axis=1, keepdims=True)
        row_weights[step * tokens : (step + 1) * tokens, :] = jnp.broadcast_to(column, (tokens, HD))

    ep_index = place[0]
    page_count = owners.shape[0]
    pages_here = page_count // ep_count
    page_size = tokens // pages_here

    def rank_of(page, earlier):
        ranks[page] = earlier
        return earlier + (owners[page] == ep_index).astype(jnp.int32)

    lax.fori_loop(0, page_count, rank_of, jnp.int32(0))
    pages_ref[...] = jnp.zeros_like(pages_ref)
    for step in range(ep_count):
        source = ep_index ^ step
        for k in range(pages_here):
            page = source * pages_here + k

            @pl.when(owners[page] == ep_index)
            def _(step=step, source=source, k=k, page=page):
                first = weight_at - tokens + k * page_size
                entries = payloads[step][first : first + page_size, :]
                row = lax.broadcasted_iota(jnp.int32, entries.shape, 0) + k * page_size
                entries = jnp.where(row < lens[source], entries.astype(jnp.float32), 0.0)
                at = pl.multiple_of(ranks[page] * page_size, page_size)
                pages_ref[pl.ds(at, page_size), :] = entries.astype(jnp.bfloat16)


def prepare_call(lens, owners, place, arrived, after, blocks, tokens, weight_at, own_most):
    ep_count = len(arrived)
    page_size = tokens * ep_count // owners.shape[0]
    return pl.pallas_call(
        lambda *refs: prepare_kernel(ep_count, blocks, weight_at, *refs),
        out_shape=[
            jax.ShapeDtypeStruct((ep_count * tokens, HD), jnp.float32),
            jax.ShapeDtypeStruct((own_most * page_size, 2 * HD), jnp.bfloat16),
        ],
        in_specs=[SCALARS] * 3 + [WHOLE] * ep_count + [ANYWHERE],
        out_specs=[WHOLE] * 2,
        scratch_shapes=[pltpu.SMEM((owners.shape[0],), jnp.int32)],
        compiler_params=pltpu.CompilerParams(vmem_limit_bytes=VMEM_LIMIT),
        cost_estimate=EXPERT_COST,
        name="prepare",
    )(lens, owners, place, *arrived, after)


def attend_kernel(ep_count, held, tokens, row_blocks, all_open, lens, place, counts, queries, *refs):
    blocks = refs[:ep_count]
    out_weight = refs[ep_count]
    kept_ref, sent_ref = refs[ep_count + 1 : ep_count + 3]
    scores, projected = refs[ep_count + 3 :]
    heads = queries.shape[1] // HD
    ep_index = place[0]
    block_index = place[1]
    suffix = ep_count * tokens

    own_start = jnp.int32(0)
    for j in range(ep_count):
        own_start = own_start + jnp.where(j < ep_index, lens[j], 0)
    column = lax.broadcasted_iota(jnp.int32, (tokens, suffix), 1)
    slot = column % tokens
    query_position = own_start + lax.broadcasted_iota(jnp.int32, (tokens, suffix), 0)
    seen = jnp.zeros((tokens, suffix), jnp.int32)
    for step in range(ep_count):
        source = ep_index ^ step
        start = jnp.int32(0)
        for j in range(ep_count):
            start = start + jnp.where(j < source, lens[j], 0)
        last = jnp.minimum(query_position - start, lens[source] - 1)
        here = (column // tokens == step) & (slot <= last)
        seen = seen + here.astype(jnp.int32)
    bias = jnp.where(seen > 0, 0.0, MASKED)

    suffix_keys = jnp.concatenate([block[held : held + tokens, :HD] for block in blocks], axis=0)
    suffix_values = jnp.concatenate([block[held : held + tokens, HD:] for block in blocks], axis=0)
    scale = math.log2(math.e) / math.sqrt(HD)
    rows = min(ROWS, heads * tokens)
    together = rows // tokens
    attended = []
    for first in range(0, heads, together):
        grouped = jnp.concatenate(
            [queries[:, h * HD : (h + 1) * HD] for h in range(first, first + together)], axis=0
        )
        highest = None
        for step in range(ep_count):
            part = scale * lax.dot_general(
                grouped, blocks[step][:held, :HD], TRANSPOSED, preferred_element_type=jnp.float32
            )
            if not all_open:
                entry = lax.broadcasted_iota(jnp.int32, part.shape, 1)
                part = jnp.where(entry < counts[step], part, MASKED)
            scores[:, step * held : (step + 1) * held] = part
            top = jnp.max(part, axis=1, keepdims=True)
            highest = top if highest is None else jnp.maximum(highest, top)
        part = scale * lax.dot_general(
            grouped, suffix_keys, TRANSPOSED, preferred_element_type=jnp.float32
        )
        part = part + jnp.concatenate([bias] * together, axis=0)
        highest = jnp.maximum(highest, jnp.max(part, axis=1, keepdims=True))
        part = jnp.exp2(part - highest)
        total = jnp.sum(part, axis=1, keepdims=True)
        mixed = jnp.dot(
            part.astype(jnp.bfloat16), suffix_values, preferred_element_type=jnp.float32
        )
        for step in range(ep_count):
            part = jnp.exp2(scores[:, step * held : (step + 1) * held] - highest)
            total += jnp.sum(part, axis=1, keepdims=True)
            mixed += jnp.dot(
                part.astype(jnp.bfloat16),
                blocks[step][:held, HD:],
                preferred_element_type=jnp.float32,
            )
        mixed = (mixed / total).astype(jnp.bfloat16)
        attended += [mixed[h * tokens : (h + 1) * tokens] for h in range(together)]
    attended = jnp.concatenate(attended, axis=1)
    for at in range(0, out_weight.shape[1], COLUMNS):
        projected[:, at : at + COLUMNS] = jnp.dot(
            attended, out_weight[:, at : at + COLUMNS], preferred_element_type=jnp.float32
        )
    count = tokens // row_blocks
    for spot, piece in enumerate(piece_order(row_blocks)):
        rows = projected[pl.ds(pl.multiple_of((block_index ^ piece) * count, count), count), :]
        ref, spot = (kept_ref, spot) if 2 * spot < row_blocks else (sent_ref, spot - row_blocks // 2)
        ref[spot * count : (spot + 1) * count, :] = rows.astype(ref.dtype)


def attend_call(
    lens, place, counts, queries, arrived, out_weight, held, blocks, all_open
):
    tokens = queries.shape[0]
    ep_count = len(arrived)
    model_width = out_weight.shape[1]
    heads = queries.shape[1] // HD
    keys = ep_count * (held + tokens)
    return pl.pallas_call(
        lambda *refs: attend_kernel(ep_count, held, tokens, blocks, all_open, *refs),
        out_shape=[
            jax.ShapeDtypeStruct((tokens // 2, model_width), jnp.float32),
            jax.ShapeDtypeStruct((tokens // 2, model_width), jnp.bfloat16),
        ],
        in_specs=[SCALARS] * 3 + [WHOLE] * (ep_count + 2),
        out_specs=[WHOLE] * 2,
        scratch_shapes=[
            pltpu.VMEM((min(ROWS, heads * tokens), ep_count * held), jnp.float32),
            pltpu.VMEM((tokens, model_width), jnp.float32),
        ],
        compiler_params=pltpu.CompilerParams(vmem_limit_bytes=VMEM_LIMIT),
        cost_estimate=pl.CostEstimate(
            flops=4 * heads * tokens * keys * HD + 2 * tokens * heads * HD * model_width,
            bytes_accessed=2 * heads * HD * model_width,
            transcendentals=heads * tokens * keys,
        ),
        name="attend",
    )(lens, place, counts, queries, *arrived, out_weight)


def expert_kernel(count, steps, blocks, row_weights, *refs):
    row_refs = refs[:count]
    gate_up, down_weight = refs[count : count + 2]
    kept_ref, sent_ref = refs[-2:]
    tokens = 2 * kept_ref.shape[0] // len(steps)
    row_count = tokens // blocks
    row_weight = jnp.concatenate(
        [
            row_weights[step * tokens + spot * row_count : step * tokens + (spot + 1) * row_count, :1]
            for spot in range(blocks)
            for step in steps
        ],
        axis=0,
    )
    gate_part = up_part = 0.0
    for at in range(0, kept_ref.shape[1], COLUMNS):
        rows = jnp.concatenate([ref[:, at : at + COLUMNS] for ref in row_refs], axis=0)
        gate_part += lax.dot_general(
            rows, gate_up[0, 0, :, at : at + COLUMNS], TRANSPOSED, preferred_element_type=jnp.float32
        )
        up_part += lax.dot_general(
            rows, gate_up[0, 1, :, at : at + COLUMNS], TRANSPOSED, preferred_element_type=jnp.float32
        )
    hidden = gate_part / (1.0 + jnp.exp(-gate_part)) * up_part
    hidden = (hidden * row_weight).astype(jnp.bfloat16)
    half = kept_ref.shape[0]
    for at in range(0, kept_ref.shape[1], COLUMNS):
        out = jnp.dot(
            hidden, down_weight[0, :, at : at + COLUMNS], preferred_element_type=jnp.float32
        ).astype(jnp.bfloat16)
        kept_ref[:, at : at + COLUMNS] = out[:half]
        sent_ref[:, at : at + COLUMNS] = out[half:]


def expert_call(steps, blocks, row_weights, have, gate_up, down_weight, after):
    if have[0].shape[0] % 16:
        have = [jnp.concatenate(have, axis=0)]
    tokens = sum(piece.shape[0] for piece in have)
    model_width = have[0].shape[1]
    hidden_units = down_weight.shape[1]
    half = jax.ShapeDtypeStruct((tokens // 2, model_width), jnp.bfloat16)
    return pl.pallas_call(
        lambda *refs: expert_kernel(len(have), steps, blocks, *refs),
        out_shape=(half, half),
        in_specs=[WHOLE] * (len(have) + 3) + [ANYWHERE] * len(after),
        out_specs=(WHOLE, WHOLE),
        compiler_params=pltpu.CompilerParams(vmem_limit_bytes=VMEM_LIMIT),
        cost_estimate=EXPERT_COST,
        name="experts",
    )(row_weights, *have, gate_up, down_weight, *after)


def local(
    queries,
    new_kv,
    cache_pool,
    hit_pages,
    span_lengths,
    out_weight,
    hidden_in,
    norm_gain,
    expert_ids,
    gate_weights,
    gate_up,
    down_weight,
    new_owner,
):
    tokens = queries.shape[0]
    model_width = hidden_in.shape[1]
    ep_count = lax.axis_size("ep")
    tp_count = lax.axis_size("tp")
    blocks = lax.axis_size("kv") * tp_count
    ep_index = lax.axis_index("ep")
    kv_index = lax.axis_index("kv")
    tp_index = lax.axis_index("tp")
    block_index = kv_index * tp_count + tp_index
    keyval_local = new_kv.shape[1]
    heads_local = queries.shape[1] // HD
    keyval_pick = block_index * heads_local // (HQ // KVH) - kv_index * keyval_local
    row_count = tokens // blocks
    pool_pages = cache_pool.shape[0]
    page_size = cache_pool.shape[1]
    held = HOLD_MOST * page_size

    hits = hit_pages.shape[0]
    here_page = lax.optimization_barrier(hit_pages - ep_index * pool_pages)
    owned_hits = (here_page >= 0) & (here_page < pool_pages)
    earlier = jnp.arange(hits)[None, :] < jnp.arange(hits)[:, None]
    hit_rank = jnp.sum((earlier & owned_hits[None, :]).astype(jnp.int32), axis=1)
    hit_pick = owned_hits[None, :] & (
        hit_rank[None, :] == jnp.arange(HOLD_MOST, dtype=jnp.int32)[:, None]
    )
    local_page = jnp.sum(jnp.where(hit_pick, here_page[None, :], 0), axis=1)
    chosen = cache_pool.at[local_page].get(mode="promise_in_bounds")
    own_pages = lax.dynamic_index_in_dim(chosen, keyval_pick, 2, keepdims=False).reshape(held, 2 * HD)
    own_suffix = lax.dynamic_index_in_dim(new_kv, keyval_pick, 1, keepdims=False)

    by_expert = jnp.sum(
        jnp.where(
            expert_ids[:, :, None] == jnp.arange(ep_count, dtype=jnp.int32)[None, None, :],
            gate_weights[:, :, None],
            0.0,
        ),
        axis=1,
    )
    weight_part = jnp.concatenate(three_parts(by_expert.T), axis=0)
    weight_rows = weight_part.shape[0]
    weight_part = jnp.pad(
        weight_part, ((0, -weight_rows % WEIGHT_ROWS), (0, 2 * HD - weight_part.shape[1]))
    )
    payload = jnp.concatenate([own_pages, own_suffix, weight_part], axis=0)
    arrived = [payload]
    for step in range(1, ep_count):
        arrived.append(
            lax.ppermute(payload, "ep", [(i, i ^ step) for i in range(ep_count)])
        )
    sources = [ep_index ^ step for step in range(ep_count)]

    all_open = hits == HOLD_MOST * ep_count
    holder = hit_pages // pool_pages
    counts = jnp.sum(
        (holder[None, :] == jnp.stack(sources)[:, None]).astype(jnp.int32) * page_size, axis=1
    )
    if all_open:
        counts = jnp.zeros((1,), jnp.int32)
    place = jnp.stack([ep_index, block_index]).astype(jnp.int32)
    exchange = lambda value, bit: lax.ppermute(
        value, ("kv", "tp"), [(i, i ^ bit) for i in range(blocks)]
    )
    across = lambda value, step: lax.ppermute(
        value, "ep", [(i, i ^ step) for i in range(ep_count)]
    )
    bits = [1 << place for place in range(1, blocks.bit_length() - 1)]

    def scatter(kept, sent):
        got = received = exchange(sent, 1)
        gives = []
        for bit in reversed(bits):
            half = kept.shape[0] // 2
            give = kept[half:].astype(jnp.float32) + got[half:].astype(jnp.float32)
            gives.append(give.astype(jnp.bfloat16))
            kept = kept[:half].astype(jnp.float32) + got[:half].astype(jnp.float32)
            got = exchange(gives[-1], bit)
        return kept.astype(jnp.float32), got, gives, received

    own_most = 2 * (tokens // page_size)
    own_slots = block_index * row_count + jnp.arange(row_count, dtype=jnp.int32)
    rows_filled = own_slots < span_lengths[ep_index]
    core = jnp.broadcast_to(tp_index.astype(jnp.int32), (1, 1, 2 * HD))
    core, row_mask = lax.optimization_barrier((core, rows_filled.astype(jnp.int32)))
    wide_gain = norm_gain[None, :]
    own_hidden = lax.dynamic_slice_in_dim(hidden_in, block_index * row_count, row_count, 0)
    held_out, held_gate_up, held_down, _ = hold_call(
        [out_weight, gate_up, down_weight], payload, place, row_mask, core, own_hidden, wide_gain
    )
    kept, sent = attend_call(
        span_lengths,
        place,
        counts,
        queries,
        arrived,
        held_out,
        held,
        blocks,
        all_open,
    )
    residual, normed = normalize_call(*scatter(kept, sent)[:2], own_hidden, wide_gain)
    resid_wide = residual.astype(jnp.float32)

    def group_rows(have, bits, before=None):
        for bit in bits:
            have = have + [exchange(part, bit) for part in have]
            if before is not None and len(have) == 2:
                have[1], before = lax.optimization_barrier([have[1], before])
        return have

    row_weights, head_pages = prepare_call(
        span_lengths,
        new_owner,
        place,
        arrived,
        normed,
        blocks,
        tokens,
        held + tokens,
        own_most,
    )
    head_pages = head_pages.reshape(own_most, page_size, 2 * HD)
    ep_bits = [1 << place for place in reversed(range(ep_count.bit_length() - 1))]
    early = [exchange(normed, bit) for bit in bits + [1]]
    direct = [across(normed, bit) for bit in ep_bits]
    row_weights, *tied = lax.optimization_barrier([row_weights] + early + direct)
    early, direct = tied[: len(early)], dict(zip(ep_bits, tied[len(early) :]))
    crossed = {0: normed}
    for bit in ep_bits:
        for step in list(crossed):
            crossed[step ^ bit] = across(crossed[step], bit) if step else direct[bit]
    leading = ep_bits[0]
    forwarded = [step for step in crossed if step & (step - 1)]
    lead_have = group_rows([crossed[leading]], bits[:1])
    lead_have[1:], ahead = lax.optimization_barrier(
        (lead_have[1:], [crossed[step] for step in forwarded])
    )
    crossed.update(zip(forwarded, ahead))
    lead_have = group_rows(lead_have, bits[1:] + [1])
    own_have = [normed]
    for bit, piece in zip(bits + [1], early):
        own_have += [piece] + [exchange(part, bit) for part in own_have[1:]]
    own_kept, sent = expert_call(
        (0,), blocks, row_weights, own_have, held_gate_up, held_down, []
    )
    own_sum, own_got, own_given, _ = scatter(own_kept, sent)
    own_sum = own_sum + own_got.astype(jnp.float32)
    crossed = {0: normed}
    for bit in ep_bits:
        for step in list(crossed):
            crossed[step ^ bit] = across(crossed[step], bit) if step else direct[bit]
    leading = ep_bits[0]
    forwarded = [step for step in crossed if step & (step - 1)]
    lead_have = group_rows([crossed[leading]], bits[:1])
    lead_have[1:], ahead, sent = lax.optimization_barrier(
        (lead_have[1:], [crossed[step] for step in forwarded], sent)
    )
    crossed.update(zip(forwarded, ahead))
    lead_have = group_rows(lead_have, bits[1:] + [1])

    order = [leading] + [step for step in reversed(range(1, ep_count)) if step != leading]
    mixture = resid_wide
    given, finished = [], []
    crossing = []
    for turn, step in enumerate(order):
        after = [sent]
        if turn == 1:
            after += []
        elif turn >= 2:
            after += given[:1]
        if turn == 0:
            have = lead_have
        else:
            piece = crossed[step]
            if turn > 1 and bits:
                piece, reached = lax.optimization_barrier((piece, reached))
            have = group_rows([piece], bits + [1], sent if turn == 1 else received)
            reached = have[1] if bits else piece
        kept, sent = expert_call(
            (step,), blocks, row_weights, have, held_gate_up, held_down, after
        )
        own, got, gives, received = scatter(kept, sent)
        own = (own + got.astype(jnp.float32)).astype(jnp.bfloat16)
        given.append(gives[0] if gives else own)
        finished.append(own)
        crossing.append(across(own, step))
    mixture = mixture + own_sum
    for rows in crossing:
        mixture = mixture + rows.astype(jnp.float32)
    layer_out = jnp.where(row_mask[:, None] > 0, mixture, 0.0).astype(jnp.bfloat16)

    if keyval_local == 1:
        decode_pages = head_pages[:, :, None, :]
    else:
        other = lax.ppermute(head_pages, "tp", [(i, i ^ 1) for i in range(tp_count)])
        first = core == 0
        decode_pages = jnp.stack(
            [jnp.where(first, head_pages, other), jnp.where(first, other, head_pages)], axis=2
        )
    return (layer_out, decode_pages)


def solution(mesh):
    placed = (
        P(("groups", "ep"), ("kv", "tp")),
        P(("groups", "ep"), "kv", None),
        P(("groups", "ep"), None, "kv", None),
        P("groups"),
        P("groups"),
        P(("kv", "tp"), None),
        P(("groups", "ep"), None),
        P(),
        P(("groups", "ep"), None),
        P(("groups", "ep"), None),
        P("ep", None, ("kv", "tp"), None),
        P("ep", ("kv", "tp"), None),
        P("groups"),
    )
    return jax.shard_map(
        local,
        mesh=mesh,
        in_specs=placed,
        out_specs=(P(("groups", "ep", "kv", "tp"), None), P(("groups", "ep"), None, "kv", None)),
        check_vma=False,
    )
```

```python
import math

import jax
import jax.numpy as jnp
from jax import lax
from jax.experimental import pallas as pl
from jax.experimental.pallas import tpu as pltpu
from jax.sharding import PartitionSpec as P

HD = 128
HQ = 32
KVH = 4
HOLD_MOST = 16
WEIGHT_ROWS = 16

MASKED = -1e30
EPSILON = 1e-06


def three_parts(wide):
    high = lax.reduce_precision(wide, 8, 7)
    rest = wide - high
    middle = lax.reduce_precision(rest, 8, 7)
    low = rest - middle
    return [part.astype(jnp.bfloat16) for part in (high, middle, low)]


def piece_order(blocks):
    order = [0]
    bit = 2
    while bit < blocks:
        order += [piece ^ bit for piece in order]
        bit *= 2
    return order + [piece ^ 1 for piece in order]


TRANSPOSED = (((1,), (1,)), ((), ()))
WHOLE = pl.BlockSpec(memory_space=pltpu.VMEM)
ANYWHERE = pl.BlockSpec(memory_space=pl.ANY)
SCALARS = pl.BlockSpec(memory_space=pltpu.SMEM)
COLUMNS = 1024
ROWS = 256
VMEM_LIMIT = 16 * 2**20
EXPERT_COST = pl.CostEstimate(flops=1024, bytes_accessed=1024, transcendentals=0)


def hold_kernel(count, *refs):
    sources, held, token, sem = refs[:count], refs[-2 - count : -2], refs[-2], refs[-1]
    token[...] = jnp.zeros_like(token)
    copies = [
        pltpu.make_async_copy(source, target, sem.at[i])
        for i, (source, target) in enumerate(zip(sources, held))
    ]
    for copy in copies:
        copy.start()
    for copy in copies:
        copy.wait()


def hold_call(arrays, *after):
    size = sum(math.prod(array.shape) * 2 for array in arrays)
    return pl.pallas_call(
        lambda *refs: hold_kernel(len(arrays), *refs),
        out_shape=[jax.ShapeDtypeStruct(array.shape, array.dtype) for array in arrays]
        + [jax.ShapeDtypeStruct((8, 128), jnp.float32)],
        in_specs=[ANYWHERE] * (len(arrays) + len(after)),
        out_specs=[WHOLE] * (len(arrays) + 1),
        scratch_shapes=[pltpu.SemaphoreType.DMA((len(arrays),))],
        compiler_params=pltpu.CompilerParams(vmem_limit_bytes=VMEM_LIMIT),
        cost_estimate=pl.CostEstimate(flops=0, bytes_accessed=2 * size, transcendentals=0),
        name="hold",
    )(*arrays, *after)


def normalize_kernel(kept, got, hidden, gain, residual, normed):
    wide = hidden[...].astype(jnp.float32) + (kept[...] + got[...].astype(jnp.float32))
    residual[...] = wide.astype(jnp.bfloat16)
    wide = residual[...].astype(jnp.float32)
    square = jnp.mean(wide * wide, axis=1, keepdims=True)
    normed[...] = (wide * lax.rsqrt(square + EPSILON) * gain[...]).astype(jnp.bfloat16)


def normalize_call(kept, got, hidden, gain):
    rows = jax.ShapeDtypeStruct(hidden.shape, jnp.bfloat16)
    return pl.pallas_call(
        normalize_kernel,
        out_shape=[rows, rows],
        in_specs=[WHOLE] * 4,
        out_specs=[WHOLE] * 2,
        compiler_params=pltpu.CompilerParams(vmem_limit_bytes=VMEM_LIMIT),
        cost_estimate=EXPERT_COST,
        name="normalize",
    )(kept, got, hidden, gain)


def prepare_kernel(ep_count, blocks, weight_at, lens, owners, place, *refs):
    payloads = refs[:ep_count]
    row_weights, pages_ref, ranks = refs[-3:]
    tokens = row_weights.shape[0] // ep_count
    row_count = tokens // blocks
    wide = (tokens, payloads[0].shape[1])
    row = lax.broadcasted_iota(jnp.int32, wide, 0)
    token = row % row_count
    for spot, piece in enumerate(piece_order(blocks)):
        token = token + jnp.where(row // row_count == spot, (place[1] ^ piece) * row_count, 0)
    here = lax.broadcasted_iota(jnp.int32, wide, 1) == token
    for step, payload in enumerate(payloads):
        parts = payload[weight_at:, :].astype(jnp.float32)
        part_row = lax.broadcasted_iota(jnp.int32, parts.shape, 0)
        chosen = (part_row % ep_count == place[0]) & (part_row < 3 * ep_count)
        by_token = jnp.sum(jnp.where(chosen, parts, 0.0), axis=0, keepdims=True)
        column = jnp.sum(jnp.where(here, by_token, 0.0), axis=1, keepdims=True)
        row_weights[step * tokens : (step + 1) * tokens, :] = jnp.broadcast_to(column, (tokens, HD))

    ep_index = place[0]
    page_count = owners.shape[0]
    pages_here = page_count // ep_count
    page_size = tokens // pages_here

    def rank_of(page, earlier):
        ranks[page] = earlier
        return earlier + (owners[page] == ep_index).astype(jnp.int32)

    lax.fori_loop(0, page_count, rank_of, jnp.int32(0))
    pages_ref[...] = jnp.zeros_like(pages_ref)
    for step in range(ep_count):
        source = ep_index ^ step
        for k in range(pages_here):
            page = source * pages_here + k

            @pl.when(owners[page] == ep_index)
            def _(step=step, source=source, k=k, page=page):
                first = weight_at - tokens + k * page_size
                entries = payloads[step][first : first + page_size, :]
                row = lax.broadcasted_iota(jnp.int32, entries.shape, 0) + k * page_size
                entries = jnp.where(row < lens[source], entries.astype(jnp.float32), 0.0)
                at = pl.multiple_of(ranks[page] * page_size, page_size)
                pages_ref[pl.ds(at, page_size), :] = entries.astype(jnp.bfloat16)


def prepare_call(lens, owners, place, arrived, after, blocks, tokens, weight_at, own_most):
    ep_count = len(arrived)
    page_size = tokens * ep_count // owners.shape[0]
    return pl.pallas_call(
        lambda *refs: prepare_kernel(ep_count, blocks, weight_at, *refs),
        out_shape=[
            jax.ShapeDtypeStruct((ep_count * tokens, HD), jnp.float32),
            jax.ShapeDtypeStruct((own_most * page_size, 2 * HD), jnp.bfloat16),
        ],
        in_specs=[SCALARS] * 3 + [WHOLE] * ep_count + [ANYWHERE],
        out_specs=[WHOLE] * 2,
        scratch_shapes=[pltpu.SMEM((owners.shape[0],), jnp.int32)],
        compiler_params=pltpu.CompilerParams(vmem_limit_bytes=VMEM_LIMIT),
        cost_estimate=EXPERT_COST,
        name="prepare",
    )(lens, owners, place, *arrived, after)


def attend_kernel(ep_count, held, tokens, row_blocks, all_open, lens, place, counts, queries, *refs):
    blocks = refs[:ep_count]
    out_weight = refs[ep_count]
    kept_ref, sent_ref = refs[ep_count + 1 : ep_count + 3]
    scores, projected = refs[ep_count + 3 :]
    heads = queries.shape[1] // HD
    ep_index = place[0]
    block_index = place[1]
    suffix = ep_count * tokens

    own_start = jnp.int32(0)
    for j in range(ep_count):
        own_start = own_start + jnp.where(j < ep_index, lens[j], 0)
    column = lax.broadcasted_iota(jnp.int32, (tokens, suffix), 1)
    slot = column % tokens
    query_position = own_start + lax.broadcasted_iota(jnp.int32, (tokens, suffix), 0)
    seen = jnp.zeros((tokens, suffix), jnp.int32)
    for step in range(ep_count):
        source = ep_index ^ step
        start = jnp.int32(0)
        for j in range(ep_count):
            start = start + jnp.where(j < source, lens[j], 0)
        last = jnp.minimum(query_position - start, lens[source] - 1)
        here = (column // tokens == step) & (slot <= last)
        seen = seen + here.astype(jnp.int32)
    bias = jnp.where(seen > 0, 0.0, MASKED)

    suffix_keys = jnp.concatenate([block[held : held + tokens, :HD] for block in blocks], axis=0)
    suffix_values = jnp.concatenate([block[held : held + tokens, HD:] for block in blocks], axis=0)
    scale = math.log2(math.e) / math.sqrt(HD)
    rows = min(ROWS, heads * tokens)
    together = rows // tokens
    attended = []
    for first in range(0, heads, together):
        grouped = jnp.concatenate(
            [queries[:, h * HD : (h + 1) * HD] for h in range(first, first + together)], axis=0
        )
        highest = None
        for step in range(ep_count):
            part = scale * lax.dot_general(
                grouped, blocks[step][:held, :HD], TRANSPOSED, preferred_element_type=jnp.float32
            )
            if not all_open:
                entry = lax.broadcasted_iota(jnp.int32, part.shape, 1)
                part = jnp.where(entry < counts[step], part, MASKED)
            scores[:, step * held : (step + 1) * held] = part
            top = jnp.max(part, axis=1, keepdims=True)
            highest = top if highest is None else jnp.maximum(highest, top)
        part = scale * lax.dot_general(
            grouped, suffix_keys, TRANSPOSED, preferred_element_type=jnp.float32
        )
        part = part + jnp.concatenate([bias] * together, axis=0)
        highest = jnp.maximum(highest, jnp.max(part, axis=1, keepdims=True))
        part = jnp.exp2(part - highest)
        total = jnp.sum(part, axis=1, keepdims=True)
        mixed = jnp.dot(
            part.astype(jnp.bfloat16), suffix_values, preferred_element_type=jnp.float32
        )
        for step in range(ep_count):
            part = jnp.exp2(scores[:, step * held : (step + 1) * held] - highest)
            total += jnp.sum(part, axis=1, keepdims=True)
            mixed += jnp.dot(
                part.astype(jnp.bfloat16),
                blocks[step][:held, HD:],
                preferred_element_type=jnp.float32,
            )
        mixed = (mixed / total).astype(jnp.bfloat16)
        attended += [mixed[h * tokens : (h + 1) * tokens] for h in range(together)]
    attended = jnp.concatenate(attended, axis=1)
    for at in range(0, out_weight.shape[1], COLUMNS):
        projected[:, at : at + COLUMNS] = jnp.dot(
            attended, out_weight[:, at : at + COLUMNS], preferred_element_type=jnp.float32
        )
    count = tokens // row_blocks
    for spot, piece in enumerate(piece_order(row_blocks)):
        rows = projected[pl.ds(pl.multiple_of((block_index ^ piece) * count, count), count), :]
        ref, spot = (kept_ref, spot) if 2 * spot < row_blocks else (sent_ref, spot - row_blocks // 2)
        ref[spot * count : (spot + 1) * count, :] = rows.astype(ref.dtype)


def attend_call(
    lens, place, counts, queries, arrived, out_weight, held, blocks, all_open
):
    tokens = queries.shape[0]
    ep_count = len(arrived)
    model_width = out_weight.shape[1]
    heads = queries.shape[1] // HD
    keys = ep_count * (held + tokens)
    return pl.pallas_call(
        lambda *refs: attend_kernel(ep_count, held, tokens, blocks, all_open, *refs),
        out_shape=[
            jax.ShapeDtypeStruct((tokens // 2, model_width), jnp.float32),
            jax.ShapeDtypeStruct((tokens // 2, model_width), jnp.bfloat16),
        ],
        in_specs=[SCALARS] * 3 + [WHOLE] * (ep_count + 2),
        out_specs=[WHOLE] * 2,
        scratch_shapes=[
            pltpu.VMEM((min(ROWS, heads * tokens), ep_count * held), jnp.float32),
            pltpu.VMEM((tokens, model_width), jnp.float32),
        ],
        compiler_params=pltpu.CompilerParams(vmem_limit_bytes=VMEM_LIMIT),
        cost_estimate=pl.CostEstimate(
            flops=4 * heads * tokens * keys * HD + 2 * tokens * heads * HD * model_width,
            bytes_accessed=2 * heads * HD * model_width,
            transcendentals=heads * tokens * keys,
        ),
        name="attend",
    )(lens, place, counts, queries, *arrived, out_weight)


def expert_kernel(count, steps, blocks, row_weights, *refs):
    row_refs = refs[:count]
    gate_up, down_weight = refs[count : count + 2]
    kept_ref, sent_ref = refs[-2:]
    tokens = 2 * kept_ref.shape[0] // len(steps)
    row_count = tokens // blocks
    row_weight = jnp.concatenate(
        [
            row_weights[step * tokens + spot * row_count : step * tokens + (spot + 1) * row_count, :1]
            for spot in range(blocks)
            for step in steps
        ],
        axis=0,
    )
    gate_part = up_part = 0.0
    for at in range(0, kept_ref.shape[1], COLUMNS):
        rows = jnp.concatenate([ref[:, at : at + COLUMNS] for ref in row_refs], axis=0)
        gate_part += lax.dot_general(
            rows, gate_up[0, 0, :, at : at + COLUMNS], TRANSPOSED, preferred_element_type=jnp.float32
        )
        up_part += lax.dot_general(
            rows, gate_up[0, 1, :, at : at + COLUMNS], TRANSPOSED, preferred_element_type=jnp.float32
        )
    hidden = gate_part / (1.0 + jnp.exp(-gate_part)) * up_part
    hidden = (hidden * row_weight).astype(jnp.bfloat16)
    half = kept_ref.shape[0]
    for at in range(0, kept_ref.shape[1], COLUMNS):
        out = jnp.dot(
            hidden, down_weight[0, :, at : at + COLUMNS], preferred_element_type=jnp.float32
        ).astype(jnp.bfloat16)
        kept_ref[:, at : at + COLUMNS] = out[:half]
        sent_ref[:, at : at + COLUMNS] = out[half:]


def expert_call(steps, blocks, row_weights, have, gate_up, down_weight, after):
    if have[0].shape[0] % 16:
        have = [jnp.concatenate(have, axis=0)]
    tokens = sum(piece.shape[0] for piece in have)
    model_width = have[0].shape[1]
    hidden_units = down_weight.shape[1]
    half = jax.ShapeDtypeStruct((tokens // 2, model_width), jnp.bfloat16)
    return pl.pallas_call(
        lambda *refs: expert_kernel(len(have), steps, blocks, *refs),
        out_shape=(half, half),
        in_specs=[WHOLE] * (len(have) + 3) + [ANYWHERE] * len(after),
        out_specs=(WHOLE, WHOLE),
        compiler_params=pltpu.CompilerParams(vmem_limit_bytes=VMEM_LIMIT),
        cost_estimate=EXPERT_COST,
        name="experts",
    )(row_weights, *have, gate_up, down_weight, *after)


def local(
    queries,
    new_kv,
    cache_pool,
    hit_pages,
    span_lengths,
    out_weight,
    hidden_in,
    norm_gain,
    expert_ids,
    gate_weights,
    gate_up,
    down_weight,
    new_owner,
):
    tokens = queries.shape[0]
    model_width = hidden_in.shape[1]
    ep_count = lax.axis_size("ep")
    tp_count = lax.axis_size("tp")
    blocks = lax.axis_size("kv") * tp_count
    ep_index = lax.axis_index("ep")
    kv_index = lax.axis_index("kv")
    tp_index = lax.axis_index("tp")
    block_index = kv_index * tp_count + tp_index
    keyval_local = new_kv.shape[1]
    heads_local = queries.shape[1] // HD
    keyval_pick = block_index * heads_local // (HQ // KVH) - kv_index * keyval_local
    row_count = tokens // blocks
    pool_pages = cache_pool.shape[0]
    page_size = cache_pool.shape[1]
    held = HOLD_MOST * page_size

    hits = hit_pages.shape[0]
    here_page = lax.optimization_barrier(hit_pages - ep_index * pool_pages)
    owned_hits = (here_page >= 0) & (here_page < pool_pages)
    earlier = jnp.arange(hits)[None, :] < jnp.arange(hits)[:, None]
    hit_rank = jnp.sum((earlier & owned_hits[None, :]).astype(jnp.int32), axis=1)
    hit_pick = owned_hits[None, :] & (
        hit_rank[None, :] == jnp.arange(HOLD_MOST, dtype=jnp.int32)[:, None]
    )
    local_page = jnp.sum(jnp.where(hit_pick, here_page[None, :], 0), axis=1)
    chosen = cache_pool.at[local_page].get(mode="promise_in_bounds")
    own_pages = lax.dynamic_index_in_dim(chosen, keyval_pick, 2, keepdims=False).reshape(held, 2 * HD)
    own_suffix = lax.dynamic_index_in_dim(new_kv, keyval_pick, 1, keepdims=False)

    by_expert = jnp.sum(
        jnp.where(
            expert_ids[:, :, None] == jnp.arange(ep_count, dtype=jnp.int32)[None, None, :],
            gate_weights[:, :, None],
            0.0,
        ),
        axis=1,
    )
    weight_part = jnp.concatenate(three_parts(by_expert.T), axis=0)
    weight_rows = weight_part.shape[0]
    weight_part = jnp.pad(
        weight_part, ((0, -weight_rows % WEIGHT_ROWS), (0, 2 * HD - weight_part.shape[1]))
    )
    payload = jnp.concatenate([own_pages, own_suffix, weight_part], axis=0)
    arrived = [payload]
    for step in range(1, ep_count):
        arrived.append(
            lax.ppermute(payload, "ep", [(i, i ^ step) for i in range(ep_count)])
        )
    sources = [ep_index ^ step for step in range(ep_count)]

    all_open = hits == HOLD_MOST * ep_count
    holder = hit_pages // pool_pages
    counts = jnp.sum(
        (holder[None, :] == jnp.stack(sources)[:, None]).astype(jnp.int32) * page_size, axis=1
    )
    if all_open:
        counts = jnp.zeros((1,), jnp.int32)
    place = jnp.stack([ep_index, block_index]).astype(jnp.int32)
    exchange = lambda value, bit: lax.ppermute(
        value, ("kv", "tp"), [(i, i ^ bit) for i in range(blocks)]
    )
    across = lambda value, step: lax.ppermute(
        value, "ep", [(i, i ^ step) for i in range(ep_count)]
    )
    bits = [1 << place for place in range(1, blocks.bit_length() - 1)]

    def scatter(kept, sent, before=None):
        got = received = exchange(sent, 1)
        gives = []
        for bit in reversed(bits):
            half = kept.shape[0] // 2
            give = kept[half:].astype(jnp.float32) + got[half:].astype(jnp.float32)
            give = give.astype(jnp.bfloat16)
            if before is not None and not gives:
                give, before = lax.optimization_barrier((give, before))
            gives.append(give)
            kept = kept[:half].astype(jnp.float32) + got[:half].astype(jnp.float32)
            got = exchange(gives[-1], bit)
        return kept.astype(jnp.float32), got, gives, received

    own_most = 2 * (tokens // page_size)
    own_slots = block_index * row_count + jnp.arange(row_count, dtype=jnp.int32)
    rows_filled = own_slots < span_lengths[ep_index]
    core = jnp.broadcast_to(tp_index.astype(jnp.int32), (1, 1, 2 * HD))
    core, row_mask = lax.optimization_barrier((core, rows_filled.astype(jnp.int32)))
    wide_gain = norm_gain[None, :]
    own_hidden = lax.dynamic_slice_in_dim(hidden_in, block_index * row_count, row_count, 0)
    held_out, held_gate_up, held_down, _ = hold_call(
        [out_weight, gate_up, down_weight], payload, place, row_mask, core, own_hidden, wide_gain
    )
    kept, sent = attend_call(
        span_lengths,
        place,
        counts,
        queries,
        arrived,
        held_out,
        held,
        blocks,
        all_open,
    )
    residual, normed = normalize_call(*scatter(kept, sent)[:2], own_hidden, wide_gain)
    resid_wide = residual.astype(jnp.float32)

    def group_rows(have, bits, before=None):
        for bit in bits:
            have = have + [exchange(part, bit) for part in have]
            if before is not None and len(have) == 2:
                have[1], before = lax.optimization_barrier([have[1], before])
        return have

    row_weights, head_pages = prepare_call(
        span_lengths,
        new_owner,
        place,
        arrived,
        normed,
        blocks,
        tokens,
        held + tokens,
        own_most,
    )
    head_pages = head_pages.reshape(own_most, page_size, 2 * HD)
    ep_bits = [1 << place for place in reversed(range(ep_count.bit_length() - 1))]
    early = [exchange(normed, bit) for bit in bits + [1]]
    direct = [across(normed, bit) for bit in ep_bits]
    row_weights, *tied = lax.optimization_barrier([row_weights] + early + direct)
    early, direct = tied[: len(early)], dict(zip(ep_bits, tied[len(early) :]))
    crossed = {0: normed}
    for bit in ep_bits:
        for step in list(crossed):
            crossed[step ^ bit] = across(crossed[step], bit) if step else direct[bit]
    leading = ep_bits[0]
    forwarded = [step for step in crossed if step & (step - 1)]
    lead_have = group_rows([crossed[leading]], bits[:1])
    lead_have[1:], ahead = lax.optimization_barrier(
        (lead_have[1:], [crossed[step] for step in forwarded])
    )
    crossed.update(zip(forwarded, ahead))
    lead_have = group_rows(lead_have, bits[1:] + [1])
    own_have = [normed]
    for bit, piece in zip(bits + [1], early):
        own_have += [piece] + [exchange(part, bit) for part in own_have[1:]]
    own_kept, own_sent = expert_call(
        (0,), blocks, row_weights, own_have, held_gate_up, held_down, []
    )
    sent = own_sent
    crossed = {0: normed}
    for bit in ep_bits:
        for step in list(crossed):
            crossed[step ^ bit] = across(crossed[step], bit) if step else direct[bit]
    leading = ep_bits[0]
    forwarded = [step for step in crossed if step & (step - 1)]
    lead_have = group_rows([crossed[leading]], bits[:1])
    lead_have[1:], ahead, sent = lax.optimization_barrier(
        (lead_have[1:], [crossed[step] for step in forwarded], sent)
    )
    crossed.update(zip(forwarded, ahead))
    lead_have = group_rows(lead_have, bits[1:] + [1])

    order = [leading] + [step for step in reversed(range(1, ep_count)) if step != leading]
    mixture = resid_wide
    given, finished = [], []
    crossing = []
    for turn, step in enumerate(order):
        after = [sent]
        if turn == 1:
            after += []
        elif turn >= 2:
            after += given[:1]
        if turn == 0:
            have = lead_have
        else:
            piece = crossed[step]
            if turn > 1 and bits:
                piece, reached = lax.optimization_barrier((piece, reached))
            have = group_rows([piece], bits + [1], sent if turn == 1 else received)
            reached = have[1] if bits else piece
        kept, sent = expert_call(
            (step,), blocks, row_weights, have, held_gate_up, held_down, after
        )
        own, got, gives, received = scatter(kept, sent)
        own = (own + got.astype(jnp.float32)).astype(jnp.bfloat16)
        given.append(gives[0] if gives else own)
        finished.append(own)
        crossing.append(across(own, step))
    own_sum, own_got, _, _ = scatter(own_kept, own_sent, got)
    mixture = mixture + own_sum + own_got.astype(jnp.float32)
    for rows in crossing:
        mixture = mixture + rows.astype(jnp.float32)
    layer_out = jnp.where(row_mask[:, None] > 0, mixture, 0.0).astype(jnp.bfloat16)

    if keyval_local == 1:
        decode_pages = head_pages[:, :, None, :]
    else:
        other = lax.ppermute(head_pages, "tp", [(i, i ^ 1) for i in range(tp_count)])
        first = core == 0
        decode_pages = jnp.stack(
            [jnp.where(first, head_pages, other), jnp.where(first, other, head_pages)], axis=2
        )
    return (layer_out, decode_pages)


def solution(mesh):
    placed = (
        P(("groups", "ep"), ("kv", "tp")),
        P(("groups", "ep"), "kv", None),
        P(("groups", "ep"), None, "kv", None),
        P("groups"),
        P("groups"),
        P(("kv", "tp"), None),
        P(("groups", "ep"), None),
        P(),
        P(("groups", "ep"), None),
        P(("groups", "ep"), None),
        P("ep", None, ("kv", "tp"), None),
        P("ep", ("kv", "tp"), None),
        P("groups"),
    )
    return jax.shard_map(
        local,
        mesh=mesh,
        in_specs=placed,
        out_specs=(P(("groups", "ep", "kv", "tp"), None), P(("groups", "ep"), None, "kv", None)),
        check_vma=False,
    )
```

```python
import math

import jax
import jax.numpy as jnp
from jax import lax
from jax.experimental import pallas as pl
from jax.experimental.pallas import tpu as pltpu
from jax.sharding import PartitionSpec as P

HD = 128
HQ = 32
KVH = 4
HOLD_MOST = 16
WEIGHT_ROWS = 16

MASKED = -1e30
EPSILON = 1e-06


def three_parts(wide):
    high = lax.reduce_precision(wide, 8, 7)
    rest = wide - high
    middle = lax.reduce_precision(rest, 8, 7)
    low = rest - middle
    return [part.astype(jnp.bfloat16) for part in (high, middle, low)]


def piece_order(blocks):
    order = [0]
    bit = 2
    while bit < blocks:
        order += [piece ^ bit for piece in order]
        bit *= 2
    return order + [piece ^ 1 for piece in order]


TRANSPOSED = (((1,), (1,)), ((), ()))
WHOLE = pl.BlockSpec(memory_space=pltpu.VMEM)
ANYWHERE = pl.BlockSpec(memory_space=pl.ANY)
SCALARS = pl.BlockSpec(memory_space=pltpu.SMEM)
COLUMNS = 1024
ROWS = 256
VMEM_LIMIT = 16 * 2**20
EXPERT_COST = pl.CostEstimate(flops=1024, bytes_accessed=1024, transcendentals=0)


def hold_kernel(count, *refs):
    sources, held, token, sem = refs[:count], refs[-2 - count : -2], refs[-2], refs[-1]
    token[...] = jnp.zeros_like(token)
    copies = [
        pltpu.make_async_copy(source, target, sem.at[i])
        for i, (source, target) in enumerate(zip(sources, held))
    ]
    for copy in copies:
        copy.start()
    for copy in copies:
        copy.wait()


def hold_call(arrays, *after):
    size = sum(math.prod(array.shape) * 2 for array in arrays)
    return pl.pallas_call(
        lambda *refs: hold_kernel(len(arrays), *refs),
        out_shape=[jax.ShapeDtypeStruct(array.shape, array.dtype) for array in arrays]
        + [jax.ShapeDtypeStruct((8, 128), jnp.float32)],
        in_specs=[ANYWHERE] * (len(arrays) + len(after)),
        out_specs=[WHOLE] * (len(arrays) + 1),
        scratch_shapes=[pltpu.SemaphoreType.DMA((len(arrays),))],
        compiler_params=pltpu.CompilerParams(vmem_limit_bytes=VMEM_LIMIT),
        cost_estimate=pl.CostEstimate(flops=0, bytes_accessed=2 * size, transcendentals=0),
        name="hold",
    )(*arrays, *after)


def normalize_kernel(kept, got, hidden, gain, residual, normed):
    wide = hidden[...].astype(jnp.float32) + (kept[...] + got[...].astype(jnp.float32))
    residual[...] = wide.astype(jnp.bfloat16)
    wide = residual[...].astype(jnp.float32)
    square = jnp.mean(wide * wide, axis=1, keepdims=True)
    normed[...] = (wide * lax.rsqrt(square + EPSILON) * gain[...]).astype(jnp.bfloat16)


def normalize_call(kept, got, hidden, gain):
    rows = jax.ShapeDtypeStruct(hidden.shape, jnp.bfloat16)
    return pl.pallas_call(
        normalize_kernel,
        out_shape=[rows, rows],
        in_specs=[WHOLE] * 4,
        out_specs=[WHOLE] * 2,
        compiler_params=pltpu.CompilerParams(vmem_limit_bytes=VMEM_LIMIT),
        cost_estimate=EXPERT_COST,
        name="normalize",
    )(kept, got, hidden, gain)


def prepare_kernel(ep_count, blocks, weight_at, lens, owners, place, *refs):
    payloads = refs[:ep_count]
    row_weights, pages_ref, ranks = refs[-3:]
    tokens = row_weights.shape[0] // ep_count
    row_count = tokens // blocks
    wide = (tokens, payloads[0].shape[1])
    row = lax.broadcasted_iota(jnp.int32, wide, 0)
    token = row % row_count
    for spot, piece in enumerate(piece_order(blocks)):
        token = token + jnp.where(row // row_count == spot, (place[1] ^ piece) * row_count, 0)
    here = lax.broadcasted_iota(jnp.int32, wide, 1) == token
    for step, payload in enumerate(payloads):
        parts = payload[weight_at:, :].astype(jnp.float32)
        part_row = lax.broadcasted_iota(jnp.int32, parts.shape, 0)
        chosen = (part_row % ep_count == place[0]) & (part_row < 3 * ep_count)
        by_token = jnp.sum(jnp.where(chosen, parts, 0.0), axis=0, keepdims=True)
        column = jnp.sum(jnp.where(here, by_token, 0.0), axis=1, keepdims=True)
        row_weights[step * tokens : (step + 1) * tokens, :] = jnp.broadcast_to(column, (tokens, HD))

    ep_index = place[0]
    page_count = owners.shape[0]
    pages_here = page_count // ep_count
    page_size = tokens // pages_here

    def rank_of(page, earlier):
        ranks[page] = earlier
        return earlier + (owners[page] == ep_index).astype(jnp.int32)

    lax.fori_loop(0, page_count, rank_of, jnp.int32(0))
    pages_ref[...] = jnp.zeros_like(pages_ref)
    for step in range(ep_count):
        source = ep_index ^ step
        for k in range(pages_here):
            page = source * pages_here + k

            @pl.when(owners[page] == ep_index)
            def _(step=step, source=source, k=k, page=page):
                first = weight_at - tokens + k * page_size
                entries = payloads[step][first : first + page_size, :]
                row = lax.broadcasted_iota(jnp.int32, entries.shape, 0) + k * page_size
                entries = jnp.where(row < lens[source], entries.astype(jnp.float32), 0.0)
                at = pl.multiple_of(ranks[page] * page_size, page_size)
                pages_ref[pl.ds(at, page_size), :] = entries.astype(jnp.bfloat16)


def prepare_call(lens, owners, place, arrived, after, blocks, tokens, weight_at, own_most):
    ep_count = len(arrived)
    page_size = tokens * ep_count // owners.shape[0]
    return pl.pallas_call(
        lambda *refs: prepare_kernel(ep_count, blocks, weight_at, *refs),
        out_shape=[
            jax.ShapeDtypeStruct((ep_count * tokens, HD), jnp.float32),
            jax.ShapeDtypeStruct((own_most * page_size, 2 * HD), jnp.bfloat16),
        ],
        in_specs=[SCALARS] * 3 + [WHOLE] * ep_count + [ANYWHERE],
        out_specs=[WHOLE] * 2,
        scratch_shapes=[pltpu.SMEM((owners.shape[0],), jnp.int32)],
        compiler_params=pltpu.CompilerParams(vmem_limit_bytes=VMEM_LIMIT),
        cost_estimate=EXPERT_COST,
        name="prepare",
    )(lens, owners, place, *arrived, after)


def attend_kernel(ep_count, held, tokens, row_blocks, all_open, lens, place, counts, queries, *refs):
    blocks = refs[:ep_count]
    out_weight = refs[ep_count]
    kept_ref, sent_ref = refs[ep_count + 1 : ep_count + 3]
    scores, projected = refs[ep_count + 3 :]
    heads = queries.shape[1] // HD
    ep_index = place[0]
    block_index = place[1]
    suffix = ep_count * tokens

    own_start = jnp.int32(0)
    for j in range(ep_count):
        own_start = own_start + jnp.where(j < ep_index, lens[j], 0)
    column = lax.broadcasted_iota(jnp.int32, (tokens, suffix), 1)
    slot = column % tokens
    query_position = own_start + lax.broadcasted_iota(jnp.int32, (tokens, suffix), 0)
    seen = jnp.zeros((tokens, suffix), jnp.int32)
    for step in range(ep_count):
        source = ep_index ^ step
        start = jnp.int32(0)
        for j in range(ep_count):
            start = start + jnp.where(j < source, lens[j], 0)
        last = jnp.minimum(query_position - start, lens[source] - 1)
        here = (column // tokens == step) & (slot <= last)
        seen = seen + here.astype(jnp.int32)
    bias = jnp.where(seen > 0, 0.0, MASKED)

    suffix_keys = jnp.concatenate([block[held : held + tokens, :HD] for block in blocks], axis=0)
    suffix_values = jnp.concatenate([block[held : held + tokens, HD:] for block in blocks], axis=0)
    scale = math.log2(math.e) / math.sqrt(HD)
    rows = min(ROWS, heads * tokens)
    together = rows // tokens
    attended = []
    for first in range(0, heads, together):
        grouped = jnp.concatenate(
            [queries[:, h * HD : (h + 1) * HD] for h in range(first, first + together)], axis=0
        )
        highest = None
        for step in range(ep_count):
            part = scale * lax.dot_general(
                grouped, blocks[step][:held, :HD], TRANSPOSED, preferred_element_type=jnp.float32
            )
            if not all_open:
                entry = lax.broadcasted_iota(jnp.int32, part.shape, 1)
                part = jnp.where(entry < counts[step], part, MASKED)
            scores[:, step * held : (step + 1) * held] = part
            top = jnp.max(part, axis=1, keepdims=True)
            highest = top if highest is None else jnp.maximum(highest, top)
        part = scale * lax.dot_general(
            grouped, suffix_keys, TRANSPOSED, preferred_element_type=jnp.float32
        )
        part = part + jnp.concatenate([bias] * together, axis=0)
        highest = jnp.maximum(highest, jnp.max(part, axis=1, keepdims=True))
        part = jnp.exp2(part - highest)
        total = jnp.sum(part, axis=1, keepdims=True)
        mixed = jnp.dot(
            part.astype(jnp.bfloat16), suffix_values, preferred_element_type=jnp.float32
        )
        for step in range(ep_count):
            part = jnp.exp2(scores[:, step * held : (step + 1) * held] - highest)
            total += jnp.sum(part, axis=1, keepdims=True)
            mixed += jnp.dot(
                part.astype(jnp.bfloat16),
                blocks[step][:held, HD:],
                preferred_element_type=jnp.float32,
            )
        mixed = (mixed / total).astype(jnp.bfloat16)
        attended += [mixed[h * tokens : (h + 1) * tokens] for h in range(together)]
    attended = jnp.concatenate(attended, axis=1)
    for at in range(0, out_weight.shape[1], COLUMNS):
        projected[:, at : at + COLUMNS] = jnp.dot(
            attended, out_weight[:, at : at + COLUMNS], preferred_element_type=jnp.float32
        )
    count = tokens // row_blocks
    for spot, piece in enumerate(piece_order(row_blocks)):
        rows = projected[pl.ds(pl.multiple_of((block_index ^ piece) * count, count), count), :]
        ref, spot = (kept_ref, spot) if 2 * spot < row_blocks else (sent_ref, spot - row_blocks // 2)
        ref[spot * count : (spot + 1) * count, :] = rows.astype(ref.dtype)


def attend_call(
    lens, place, counts, queries, arrived, out_weight, held, blocks, all_open
):
    tokens = queries.shape[0]
    ep_count = len(arrived)
    model_width = out_weight.shape[1]
    heads = queries.shape[1] // HD
    keys = ep_count * (held + tokens)
    return pl.pallas_call(
        lambda *refs: attend_kernel(ep_count, held, tokens, blocks, all_open, *refs),
        out_shape=[
            jax.ShapeDtypeStruct((tokens // 2, model_width), jnp.float32),
            jax.ShapeDtypeStruct((tokens // 2, model_width), jnp.bfloat16),
        ],
        in_specs=[SCALARS] * 3 + [WHOLE] * (ep_count + 2),
        out_specs=[WHOLE] * 2,
        scratch_shapes=[
            pltpu.VMEM((min(ROWS, heads * tokens), ep_count * held), jnp.float32),
            pltpu.VMEM((tokens, model_width), jnp.float32),
        ],
        compiler_params=pltpu.CompilerParams(vmem_limit_bytes=VMEM_LIMIT),
        cost_estimate=pl.CostEstimate(
            flops=4 * heads * tokens * keys * HD + 2 * tokens * heads * HD * model_width,
            bytes_accessed=2 * heads * HD * model_width,
            transcendentals=heads * tokens * keys,
        ),
        name="attend",
    )(lens, place, counts, queries, *arrived, out_weight)


def expert_kernel(count, steps, blocks, row_weights, *refs):
    row_refs = refs[:count]
    gate_up, down_weight = refs[count : count + 2]
    kept_ref, sent_ref = refs[-2:]
    tokens = 2 * kept_ref.shape[0] // len(steps)
    row_count = tokens // blocks
    row_weight = jnp.concatenate(
        [
            row_weights[step * tokens + spot * row_count : step * tokens + (spot + 1) * row_count, :1]
            for spot in range(blocks)
            for step in steps
        ],
        axis=0,
    )
    gate_part = up_part = 0.0
    for at in range(0, kept_ref.shape[1], COLUMNS):
        rows = jnp.concatenate([ref[:, at : at + COLUMNS] for ref in row_refs], axis=0)
        gate_part += lax.dot_general(
            rows, gate_up[0, 0, :, at : at + COLUMNS], TRANSPOSED, preferred_element_type=jnp.float32
        )
        up_part += lax.dot_general(
            rows, gate_up[0, 1, :, at : at + COLUMNS], TRANSPOSED, preferred_element_type=jnp.float32
        )
    hidden = gate_part / (1.0 + jnp.exp(-gate_part)) * up_part
    hidden = (hidden * row_weight).astype(jnp.bfloat16)
    half = kept_ref.shape[0]
    for at in range(0, kept_ref.shape[1], COLUMNS):
        out = jnp.dot(
            hidden, down_weight[0, :, at : at + COLUMNS], preferred_element_type=jnp.float32
        ).astype(jnp.bfloat16)
        kept_ref[:, at : at + COLUMNS] = out[:half]
        sent_ref[:, at : at + COLUMNS] = out[half:]


def expert_call(steps, blocks, row_weights, have, gate_up, down_weight, after):
    if have[0].shape[0] % 16:
        have = [jnp.concatenate(have, axis=0)]
    tokens = sum(piece.shape[0] for piece in have)
    model_width = have[0].shape[1]
    hidden_units = down_weight.shape[1]
    half = jax.ShapeDtypeStruct((tokens // 2, model_width), jnp.bfloat16)
    return pl.pallas_call(
        lambda *refs: expert_kernel(len(have), steps, blocks, *refs),
        out_shape=(half, half),
        in_specs=[WHOLE] * (len(have) + 3) + [ANYWHERE] * len(after),
        out_specs=(WHOLE, WHOLE),
        compiler_params=pltpu.CompilerParams(vmem_limit_bytes=VMEM_LIMIT),
        cost_estimate=EXPERT_COST,
        name="experts",
    )(row_weights, *have, gate_up, down_weight, *after)


def local(
    queries,
    new_kv,
    cache_pool,
    hit_pages,
    span_lengths,
    out_weight,
    hidden_in,
    norm_gain,
    expert_ids,
    gate_weights,
    gate_up,
    down_weight,
    new_owner,
):
    tokens = queries.shape[0]
    model_width = hidden_in.shape[1]
    ep_count = lax.axis_size("ep")
    tp_count = lax.axis_size("tp")
    blocks = lax.axis_size("kv") * tp_count
    ep_index = lax.axis_index("ep")
    kv_index = lax.axis_index("kv")
    tp_index = lax.axis_index("tp")
    block_index = kv_index * tp_count + tp_index
    keyval_local = new_kv.shape[1]
    heads_local = queries.shape[1] // HD
    keyval_pick = block_index * heads_local // (HQ // KVH) - kv_index * keyval_local
    row_count = tokens // blocks
    pool_pages = cache_pool.shape[0]
    page_size = cache_pool.shape[1]
    held = HOLD_MOST * page_size

    hits = hit_pages.shape[0]
    here_page = lax.optimization_barrier(hit_pages - ep_index * pool_pages)
    owned_hits = (here_page >= 0) & (here_page < pool_pages)
    earlier = jnp.arange(hits)[None, :] < jnp.arange(hits)[:, None]
    hit_rank = jnp.sum((earlier & owned_hits[None, :]).astype(jnp.int32), axis=1)
    hit_pick = owned_hits[None, :] & (
        hit_rank[None, :] == jnp.arange(HOLD_MOST, dtype=jnp.int32)[:, None]
    )
    local_page = jnp.sum(jnp.where(hit_pick, here_page[None, :], 0), axis=1)
    chosen = cache_pool.at[local_page].get(mode="promise_in_bounds")
    own_pages = lax.dynamic_index_in_dim(chosen, keyval_pick, 2, keepdims=False).reshape(held, 2 * HD)
    own_suffix = lax.dynamic_index_in_dim(new_kv, keyval_pick, 1, keepdims=False)

    by_expert = jnp.sum(
        jnp.where(
            expert_ids[:, :, None] == jnp.arange(ep_count, dtype=jnp.int32)[None, None, :],
            gate_weights[:, :, None],
            0.0,
        ),
        axis=1,
    )
    weight_part = jnp.concatenate(three_parts(by_expert.T), axis=0)
    weight_rows = weight_part.shape[0]
    weight_part = jnp.pad(
        weight_part, ((0, -weight_rows % WEIGHT_ROWS), (0, 2 * HD - weight_part.shape[1]))
    )
    payload = jnp.concatenate([own_pages, own_suffix, weight_part], axis=0)
    arrived = [payload]
    for step in range(1, ep_count):
        arrived.append(
            lax.ppermute(payload, "ep", [(i, i ^ step) for i in range(ep_count)])
        )
    sources = [ep_index ^ step for step in range(ep_count)]

    all_open = hits == HOLD_MOST * ep_count
    holder = hit_pages // pool_pages
    counts = jnp.sum(
        (holder[None, :] == jnp.stack(sources)[:, None]).astype(jnp.int32) * page_size, axis=1
    )
    if all_open:
        counts = jnp.zeros((1,), jnp.int32)
    place = jnp.stack([ep_index, block_index]).astype(jnp.int32)
    exchange = lambda value, bit: lax.ppermute(
        value, ("kv", "tp"), [(i, i ^ bit) for i in range(blocks)]
    )
    across = lambda value, step: lax.ppermute(
        value, "ep", [(i, i ^ step) for i in range(ep_count)]
    )
    bits = [1 << place for place in range(1, blocks.bit_length() - 1)]

    def scatter(kept, sent, before=None):
        got = received = exchange(sent, 1)
        gives = []
        for bit in reversed(bits):
            half = kept.shape[0] // 2
            give = kept[half:].astype(jnp.float32) + got[half:].astype(jnp.float32)
            give = give.astype(jnp.bfloat16)
            if before is not None and not gives:
                give, before = lax.optimization_barrier((give, before))
            gives.append(give)
            kept = kept[:half].astype(jnp.float32) + got[:half].astype(jnp.float32)
            got = exchange(gives[-1], bit)
        return kept.astype(jnp.float32), got, gives, received

    own_most = 2 * (tokens // page_size)
    own_slots = block_index * row_count + jnp.arange(row_count, dtype=jnp.int32)
    rows_filled = own_slots < span_lengths[ep_index]
    core = jnp.broadcast_to(tp_index.astype(jnp.int32), (1, 1, 2 * HD))
    core, row_mask = lax.optimization_barrier((core, rows_filled.astype(jnp.int32)))
    wide_gain = norm_gain[None, :]
    own_hidden = lax.dynamic_slice_in_dim(hidden_in, block_index * row_count, row_count, 0)
    held_out, held_gate_up, held_down, _ = hold_call(
        [out_weight, gate_up, down_weight], payload, place, row_mask, core, own_hidden, wide_gain
    )
    kept, sent = attend_call(
        span_lengths,
        place,
        counts,
        queries,
        arrived,
        held_out,
        held,
        blocks,
        all_open,
    )
    residual, normed = normalize_call(*scatter(kept, sent)[:2], own_hidden, wide_gain)
    resid_wide = residual.astype(jnp.float32)

    def group_rows(have, bits, before=None):
        for bit in bits:
            have = have + [exchange(part, bit) for part in have]
            if before is not None and len(have) == 2:
                have[1], before = lax.optimization_barrier([have[1], before])
        return have

    row_weights, head_pages = prepare_call(
        span_lengths,
        new_owner,
        place,
        arrived,
        normed,
        blocks,
        tokens,
        held + tokens,
        own_most,
    )
    head_pages = head_pages.reshape(own_most, page_size, 2 * HD)
    ep_bits = [1 << place for place in reversed(range(ep_count.bit_length() - 1))]
    early = [exchange(normed, bit) for bit in bits + [1]]
    direct = [across(normed, bit) for bit in ep_bits]
    row_weights, *tied = lax.optimization_barrier([row_weights] + early + direct)
    early, direct = tied[: len(early)], dict(zip(ep_bits, tied[len(early) :]))
    crossed = {0: normed}
    for bit in ep_bits:
        for step in list(crossed):
            crossed[step ^ bit] = across(crossed[step], bit) if step else direct[bit]
    leading = ep_bits[0]
    forwarded = [step for step in crossed if step & (step - 1)]
    lead_have = group_rows([crossed[leading]], bits[:1])
    lead_have[1:], ahead = lax.optimization_barrier(
        (lead_have[1:], [crossed[step] for step in forwarded])
    )
    crossed.update(zip(forwarded, ahead))
    lead_have = group_rows(lead_have, bits[1:] + [1])
    own_have = [normed]
    for bit, piece in zip(bits + [1], early):
        own_have += [piece] + [exchange(part, bit) for part in own_have[1:]]
    own_kept, own_sent = expert_call(
        (0,), blocks, row_weights, own_have, held_gate_up, held_down, []
    )
    sent = own_sent
    crossed = {0: normed}
    for bit in ep_bits:
        for step in list(crossed):
            crossed[step ^ bit] = across(crossed[step], bit) if step else direct[bit]
    leading = ep_bits[0]
    forwarded = [step for step in crossed if step & (step - 1)]
    lead_have = group_rows([crossed[leading]], bits[:1])
    lead_have[1:], ahead, sent = lax.optimization_barrier(
        (lead_have[1:], [crossed[step] for step in forwarded], sent)
    )
    crossed.update(zip(forwarded, ahead))
    lead_have = group_rows(lead_have, bits[1:] + [1])

    order = [leading] + [step for step in reversed(range(1, ep_count)) if step != leading]
    mixture = resid_wide
    given, finished = [], []
    crossing = []
    for turn, step in enumerate(order):
        after = [sent]
        if turn == 1:
            after += []
        elif turn >= 2:
            after += given[:1]
        if turn == 0:
            have = lead_have
        else:
            piece = crossed[step]
            if turn > 1 and bits:
                piece, reached = lax.optimization_barrier((piece, reached))
            have = group_rows([piece], bits + [1], sent if turn == 1 else received)
            reached = have[1] if bits else piece
        kept, sent = expert_call(
            (step,), blocks, row_weights, have, held_gate_up, held_down, after
        )
        own, got, gives, received = scatter(kept, sent)
        own = (own + got.astype(jnp.float32)).astype(jnp.bfloat16)
        given.append(gives[0] if gives else own)
        finished.append(own)
        crossing.append(own)
    own_sum, own_got, _, _ = scatter(own_kept, own_sent, got)
    mixture = mixture + own_sum + own_got.astype(jnp.float32)
    sums = dict(zip(order, (rows.astype(jnp.float32) for rows in crossing)))
    sums[0] = mixture
    for bit in reversed(ep_bits):
        for step in [step for step in sums if step & bit]:
            sums[step ^ bit] = sums[step ^ bit] + across(
                sums.pop(step).astype(jnp.bfloat16), bit
            ).astype(jnp.float32)
    mixture = sums[0]
    layer_out = jnp.where(row_mask[:, None] > 0, mixture, 0.0).astype(jnp.bfloat16)

    if keyval_local == 1:
        decode_pages = head_pages[:, :, None, :]
    else:
        other = lax.ppermute(head_pages, "tp", [(i, i ^ 1) for i in range(tp_count)])
        first = core == 0
        decode_pages = jnp.stack(
            [jnp.where(first, head_pages, other), jnp.where(first, other, head_pages)], axis=2
        )
    return (layer_out, decode_pages)


def solution(mesh):
    placed = (
        P(("groups", "ep"), ("kv", "tp")),
        P(("groups", "ep"), "kv", None),
        P(("groups", "ep"), None, "kv", None),
        P("groups"),
        P("groups"),
        P(("kv", "tp"), None),
        P(("groups", "ep"), None),
        P(),
        P(("groups", "ep"), None),
        P(("groups", "ep"), None),
        P("ep", None, ("kv", "tp"), None),
        P("ep", ("kv", "tp"), None),
        P("groups"),
    )
    return jax.shard_map(
        local,
        mesh=mesh,
        in_specs=placed,
        out_specs=(P(("groups", "ep", "kv", "tp"), None), P(("groups", "ep"), None, "kv", None)),
        check_vma=False,
    )
```
